32 devices in a mesh: seq: 8 (over z, x), tp: 4 (over y, core).
Axes of the slice: x: 2, y: 2, z: 4, core: 2. Of those that a mesh axis runs over, the one named last changes fastest.
Arguments:
- tiles: bfloat16 [6144, 1536], P('seq', 'tp'), may hold values from -6 to 6
- tile_target: int32 [6144], P('seq'), may hold values from 0 to 6143, as said below
- slide_id: int32 [6144], P('seq'), may hold values from 0 to 15, never falling along the last dimension, each value on 1 to 1536 neighbouring positions
- proj_weight: bfloat16 [1536, 768], P('tp'), may hold values from -0.15625 to 0.15625
- norm_gain: float32 [768], replicated, may hold values from 0.1 to 1.9
- query_weight: bfloat16 [768, 768], P(None, 'tp'), may hold values from -2 to 2
- key_weight: bfloat16 [768, 768], P(None, 'tp'), may hold values from -2 to 2
- value_weight: bfloat16 [768, 768], P(None, 'tp'), may hold values from -0.21875 to 0.21875
- sub_gain: float32 [768], P('tp'), may hold values from 0.1 to 1.9
- out_weight: bfloat16 [768, 768], P('tp'), may hold values from -0.21875 to 0.21875
Outputs:
- layer_out: bfloat16 [6144, 768], P(('seq', 'tp'))
The draws below stay inside these ranges and needn't reach their ends.
Inputs may be any that keep to these rules, and one draw needn't show every extreme that they name: `tile_target`: A permutation of the positions. The 768 tiles of each seq index send exactly 96 tiles into the block of 768 positions of every seq index.
All inputs are finite; a program needn't handle non-finite values.
Results may differ from the reference program's by a relative error of at most 0.012.
Values may be sent and summed in bfloat16 or wider, within the bound.
No kernel may reach another device: no remote copies, remote signals or barrier semaphores. Data moves between devices by JAX's collectives and lax.ppermute only.
A program may use at most 128 MiB of HBM per device.

```python
import math
import jax
import jax.numpy as jnp
import numpy as np
from jax import lax

D = 768
HEADS = 16
TILE_D = 1536
TOK_DEV = 768
SLIDES = 16
BRANCHES = 5
HEAD_DIM = 48
TOKENS = 6144
PEER_ROWS = 96
SEG_MIN = 768
MOST_SLIDE = 1536
N_SEQ = 8


def draw_tile_target(key, part):
    key = jax.random.fold_in(key, 11)
    first, second = jax.random.split(key)
    sources = jax.vmap(lambda item: jax.random.permutation(item, TOK_DEV))(jax.random.split(first, N_SEQ)).astype(jnp.int32)
    spots = jax.vmap(lambda item: jax.random.permutation(item, TOK_DEV))(jax.random.split(second, N_SEQ)).astype(jnp.int32)
    index = jnp.arange(TOK_DEV, dtype=jnp.int32)
    owner = index // PEER_ROWS
    slot = index % PEER_ROWS
    senders = jnp.arange(N_SEQ, dtype=jnp.int32)
    spot_index = senders[:, None] * PEER_ROWS + slot[None, :]
    owners = jnp.broadcast_to(owner[None, :], (N_SEQ, TOK_DEV))
    value = owners * TOK_DEV + spots[owners, spot_index]
    rows_of = senders[:, None] * TOK_DEV + sources
    return jnp.zeros((TOKENS,), jnp.int32).at[rows_of.reshape(-1)].set(value.reshape(-1))


def shared_normal(key):
    return jax.random.normal(key, (D, D), jnp.float32)


def draw_query_weight(key, part):
    common = shared_normal(key)
    return jnp.clip(common * D ** (-0.5), -2.0, 2.0).astype(jnp.bfloat16)


def draw_key_weight(key, part):
    key = jax.random.fold_in(key, 23)
    own = jax.random.normal(key, (D, D), jnp.float32)
    mixed = own
    return jnp.clip(mixed * D ** (-0.5), -2.0, 2.0).astype(jnp.bfloat16)


def shard_levels(stream_key, shape, cuts, smallest, largest):
    loudness, own = 1.0, jax.random.fold_in(stream_key, 6)
    for dim, blocks in cuts:
        heights = jnp.exp(jax.random.uniform(jax.random.fold_in(own, dim), (blocks,), jnp.float32, smallest / len(cuts), largest / len(cuts)))
        loudness = loudness * jnp.repeat(heights, shape[dim] // blocks).reshape([-1 if axis == dim else 1 for axis in range(len(shape))])
    return loudness


def split_up(count, total, reach, slope):
    portions = [(1 << 20) // math.isqrt(rank ** slope) + 1 for rank in range(2, count + 1)]
    rest, counts = total - reach - (count - 1), [1] * (count - 1)
    while rest > 0:
        candidates = [i for i in range(count - 1) if counts[i] < reach]
        whole, left = sum([portions[i] for i in candidates]), rest
        for i in candidates:
            more = min(reach - counts[i], max(1, left * portions[i] // whole), rest)
            counts[i] = counts[i] + more
            rest = rest - more
    return np.array([reach] + counts)


def uneven_parts(key, number_of, total, bound, slope):
    if number_of == 2:
        one = jax.random.randint(key, (), max(1, total - bound), min(bound, total - 1) + 1)
        return jnp.stack([one, total - one])
    lengths = jnp.asarray(split_up(number_of, total, bound, slope), jnp.int32)
    twos = (number_of - 1) // 2
    source_of, receiver = lengths[1:1 + 2 * twos:2], lengths[2:2 + 2 * twos:2]
    margin = jnp.minimum(source_of - 1, bound - receiver)
    shifted = jax.random.randint(jax.random.fold_in(key, 1), (twos,), 0, 1 << 20) % (margin + 1)
    lengths = lengths.at[1:1 + 2 * twos:2].set(source_of - shifted).at[2:2 + 2 * twos:2].set(receiver + shifted)
    return lengths[jax.random.permutation(jax.random.fold_in(key, 2), number_of)]


def bell_draw(stream_key, extent, spread, limit, pieces=(), kind=jnp.bfloat16):
    entries = spread * jax.random.normal(stream_key, extent, jnp.float32)
    if pieces:
        entries = entries * shard_levels(stream_key, extent, pieces, -0.22, 0.18)
    return jnp.clip(entries, -limit, limit).astype(kind)


def setup_inputs(seed: int = 0) -> dict:
    key_of = jax.random.split(jax.random.key(seed), 11)
    return {
        "tiles": bell_draw(key_of[0], (TOKENS, TILE_D), 1.0, 6.0, ((0, 8), (1, 4))),
        "tile_target": draw_tile_target(jax.random.fold_in(key_of[10], 71), 0),
        "slide_id": jnp.searchsorted(jnp.cumsum(uneven_parts(key_of[2], SLIDES, TOKENS, MOST_SLIDE, 2)), jnp.arange(TOKENS), side="right").astype(jnp.int32),
        "proj_weight": bell_draw(key_of[3], (TILE_D, D), TILE_D ** -0.5, 0.15625, ((0, 4),)),
        "norm_gain": jnp.clip(1.0 + 0.18 * jax.random.normal(key_of[4], (D,), jnp.float32), 0.1, 1.9),
        "query_weight": draw_query_weight(jax.random.fold_in(key_of[10], 71), 0),
        "key_weight": draw_key_weight(jax.random.fold_in(key_of[10], 71), 0),
        "value_weight": bell_draw(key_of[7], (D, D), D ** -0.5, 0.21875, ((1, 4),)),
        "sub_gain": jnp.clip(1.0 + 0.18 * jax.random.normal(key_of[8], (D,), jnp.float32), 0.1, 1.9),
        "out_weight": bell_draw(key_of[9], (D, D), D ** -0.5, 0.21875, ((0, 4),)),
    }


NEG = -1e+30
EPS = 1e-05

def norm_rows(values, gain):
    mean = lax.optimization_barrier(jnp.mean(values, axis=-1, keepdims=True))
    second = lax.optimization_barrier(jnp.mean(values * values, axis=-1, keepdims=True))
    return (values - mean) * lax.rsqrt(second - mean * mean + EPS) * gain

def attend(query, keys, values, query_ids, key_ids):
    scores = jnp.dot(query, keys.T, preferred_element_type=jnp.float32)
    scores = jnp.where(query_ids[:, None] == key_ids[None, :], scores, NEG)
    top = lax.optimization_barrier(jnp.max(scores, axis=1, keepdims=True))
    total = lax.optimization_barrier(jnp.sum(jnp.exp(scores - top), axis=1, keepdims=True))
    lse = top + jnp.log(total)
    weights = jnp.exp(scores - lse).astype(jnp.bfloat16)
    out = jnp.dot(weights, values, preferred_element_type=jnp.float32)
    return (out, lse[:, 0])

def reference(tiles, tile_target, slide_id, proj_weight, norm_gain, query_weight, key_weight, value_weight, sub_gain, out_weight):
    ordered = jnp.zeros_like(tiles).at[tile_target].set(tiles)
    stream = jnp.dot(ordered, proj_weight, preferred_element_type=jnp.float32).astype(jnp.bfloat16)
    normed = norm_rows(stream.astype(jnp.float32), norm_gain).astype(jnp.bfloat16)
    query = (jnp.dot(normed, query_weight, preferred_element_type=jnp.float32) * HEAD_DIM ** (-0.5)).astype(jnp.bfloat16)
    keys = jnp.dot(normed, key_weight, preferred_element_type=jnp.float32).astype(jnp.bfloat16)
    values = jnp.dot(normed, value_weight, preferred_element_type=jnp.float32).astype(jnp.bfloat16)

    def one_head(head):
        start = head * HEAD_DIM
        head_q = lax.dynamic_slice_in_dim(query, start, HEAD_DIM, 1)
        head_k = lax.dynamic_slice_in_dim(keys, start, HEAD_DIM, 1)
        head_v = lax.dynamic_slice_in_dim(values, start, HEAD_DIM, 1)
        outs = []
        lses = []
        for branch in range(BRANCHES):
            rate = 2 ** branch
            width = min(SEG_MIN * rate, TOKENS)
            count = width // rate
            segs = TOKENS // width
            offset = head % rate

            def pick(array):
                shaped = array.reshape((TOKENS // rate, rate) + array.shape[1:])
                return jnp.take(shaped, offset, axis=1)
            q_sel = pick(head_q).reshape(segs, count, HEAD_DIM)
            k_sel = pick(head_k).reshape(segs, count, HEAD_DIM)
            v_sel = pick(head_v).reshape(segs, count, HEAD_DIM)
            id_sel = pick(slide_id).reshape(segs, count)
            got, lse = lax.map(lambda item: attend(item[0], item[1], item[2], item[3], item[3]), (q_sel, k_sel, v_sel, id_sel))
            chosen = jnp.arange(rate, dtype=jnp.int32) == offset
            full_out = jnp.where(chosen[None, :, None], got.reshape(TOKENS // rate, 1, HEAD_DIM), 0.0).reshape(TOKENS, HEAD_DIM)
            full_lse = jnp.where(chosen[None, :], lse.reshape(TOKENS // rate, 1), NEG).reshape(TOKENS)
            outs.append(full_out)
            lses.append(full_lse)
        stacked = jnp.stack(lses)
        top = lax.optimization_barrier(jnp.max(stacked, axis=0))
        factors = jnp.exp(stacked - top[None, :])
        numer = sum((factors[index][:, None] * outs[index] for index in range(BRANCHES)))
        return numer / lax.optimization_barrier(jnp.sum(factors, axis=0))[:, None]
    heads = lax.map(one_head, jnp.arange(HEADS, dtype=jnp.int32))
    attn = heads.transpose(1, 0, 2).reshape(TOKENS, D)
    mixed_in = norm_rows(attn, sub_gain).astype(jnp.bfloat16)
    mixed = jnp.dot(mixed_in, out_weight, preferred_element_type=jnp.float32)
    return (stream.astype(jnp.float32) + mixed).astype(jnp.bfloat16)
```

```python
import functools

import jax
import jax.numpy as jnp
from jax import lax
from jax.experimental import pallas as pl
from jax.experimental.pallas import tpu as pltpu
from jax.sharding import PartitionSpec as P

BRANCHES = 5
HEAD_DIM = 48
SLOT = 64
LANES = 128
IDS = 16
CLASSES = 2 ** (BRANCHES - 1)
NEG = -1e30
EPS = 1e-05
BF16 = jnp.bfloat16
F32 = jnp.float32
VMEM_BYTES = 40 * 1024 * 1024


def up_to(count, step):
    return (count + step - 1) // step * step


def iota(shape, dim):
    return lax.broadcasted_iota(jnp.int32, shape, dim)


def dot(left, right):
    return jnp.dot(left, right, preferred_element_type=F32)


def dot_nt(left, right):
    return lax.dot_general(left, right, (((1,), (1,)), ((), ())), preferred_element_type=F32)


def dot_tn(left, right):
    return lax.dot_general(left, right, (((0,), (0,)), ((), ())), preferred_element_type=F32)


def one_hot(mask):
    return jnp.where(mask, 1.0, 0.0).astype(BF16)


def stored_at(position, rows):
    residue = position & (CLASSES - 1)
    flipped = jnp.zeros_like(residue)
    for bit in range(BRANCHES - 1):
        flipped = flipped + (((residue >> bit) & 1) << (BRANCHES - 2 - bit))
    return flipped * (rows // CLASSES) + (position >> (BRANCHES - 1))


def head_start(level, head, column, rows):
    start = 0
    for bit in range(level):
        value = (head >> bit) & 1 if bit < 2 else (column >> (bit - 2)) & 1
        start = start + value * (rows >> (bit + 1))
    return start


def levels_of(index, head, column, rows):
    total = jnp.zeros(index.shape, jnp.int32)
    for level in range(1, BRANCHES):
        start = head_start(level, head, column, rows)
        inside = (index >= start) & (index < start + (rows >> level))
        total = total + jnp.where(inside, 1, 0)
    return total


def call(kernel, name, outs, args, scratch=(), flops=0, moved=0):
    vmem = pl.BlockSpec(memory_space=pltpu.VMEM)
    return pl.pallas_call(
        kernel,
        name=name,
        out_shape=[jax.ShapeDtypeStruct(shape, dtype) for shape, dtype in outs],
        in_specs=[vmem] * len(args),
        out_specs=[vmem] * len(outs),
        scratch_shapes=list(scratch),
        compiler_params=pltpu.CompilerParams(vmem_limit_bytes=VMEM_BYTES),
        cost_estimate=pl.CostEstimate(flops=flops, bytes_accessed=moved, transcendentals=0),
    )(*args)


def route_kernel(n_seq, n_tp, peer, target_ref, slide_ref, tiles_ref, out_ref):
    rows = tiles_ref.shape[0]
    chunks = tiles_ref.shape[1] // LANES
    sub = peer // n_tp
    sub_pad = up_to(sub, 8)
    blocks = n_seq * n_tp
    place, column = lax.axis_index("seq"), lax.axis_index("tp")
    target = target_ref[...]
    owner = jnp.floor((target.astype(F32) + 0.5) * (1.0 / rows)).astype(jnp.int32)
    flags = jnp.where(iota((n_seq, rows), 0) == owner, 1.0, 0.0)
    before = one_hot(iota((rows, rows), 0) <= iota((rows, rows), 1))
    counts = dot(flags.astype(BF16), before)
    slot = jnp.sum(flags * counts, axis=0, keepdims=True).astype(jnp.int32) - 1
    lane_of = jnp.zeros_like(slot)
    for turn in range(1, n_tp):
        lane_of = lane_of + jnp.where(slot >= turn * sub, 1, 0)
    low = slot - lane_of * sub
    target_row = (owner * n_tp + lane_of) * sub_pad + low
    picked = dot(one_hot(iota((blocks * sub_pad, rows), 0) == target_row), tiles_ref[...])

    spot = stored_at(target - owner * rows, rows)
    high = spot >> 7
    code = ((spot & 127) + 128).astype(F32)
    for bit in range(3):
        code = code * jnp.where((high >> bit) & 1 == 1, 256.0 ** (2**bit), 1.0)
    arrival = place * sub_pad + low
    extra = n_seq * 8
    code_rows = up_to(n_seq * sub_pad, LANES) // LANES
    line = iota((extra, rows), 0)
    mine = (owner == (line >> 3)) & (lane_of == column) & ((arrival >> 7) == (line & 7))
    coded = dot_nt(
        jnp.where(mine, code, 0.0).astype(BF16),
        one_hot(iota((LANES, rows), 0) == (arrival & 127)),
    )
    share = rows // n_tp
    kept = stored_at(iota((1, rows), 1), rows) - column * share
    held = (kept >= 0) & (kept < share) & ((kept >> 7) + code_rows == (line & 7))
    ids = dot_nt(
        jnp.where(held, slide_ref[...].astype(F32), 0.0).astype(BF16),
        one_hot(iota((LANES, rows), 0) == (kept & 127)),
    )
    notes = coded + ids
    pad = out_ref.shape[1] - chunks * sub_pad - 8
    for block in range(blocks):
        base = block * sub_pad
        pieces = [
            picked[base : base + sub_pad, part * LANES : (part + 1) * LANES] for part in range(chunks)
        ]
        start = block // n_tp * 8
        pieces.append(notes[start : start + 8])
        if pad:
            pieces.append(jnp.zeros((pad, LANES), F32))
        out_ref[block] = jnp.concatenate(pieces, axis=0).astype(BF16)


def weights_kernel(query_ref, key_ref, value_ref, gain_ref, out_weight_ref, all_ref, scaled_ref):
    width = query_ref.shape[1]
    heads = width // HEAD_DIM
    wide = heads * SLOT
    spread = one_hot(spread_mask(width, wide, 0))
    for place, ref in enumerate((query_ref, key_ref, value_ref)):
        all_ref[:, place * wide : (place + 1) * wide] = dot(ref[...], spread).astype(BF16)
    total = all_ref.shape[1] - 3 * wide
    at = iota((width, total), 0)
    lane = iota((width, total), 1)
    packed = dot(key_ref[...], one_hot(lane == at)) + dot(value_ref[...], one_hot(lane == at + width))
    all_ref[:, 3 * wide :] = packed.astype(BF16)
    same = iota((width, width), 0) == iota((width, width), 1)
    gain = jnp.sum(jnp.where(same, gain_ref[...], 0.0), axis=1, keepdims=True)
    scaled_ref[...] = (out_weight_ref[...].astype(F32) * gain).astype(BF16)


def spread_mask(width, wide, shift):
    row = iota((width, wide), 0) - shift
    lane = iota((width, wide), 1)
    inner = lane & (SLOT - 1)
    return (inner < HEAD_DIM) & (row == (lane >> 6) * HEAD_DIM + inner)


def project_kernel(n_seq, n_tp, peer, recv_ref, *refs):
    weight_refs = refs[:n_tp]
    stream_ref, codes_ref, ids_ref, work = refs[n_tp:]
    sub_pad = up_to(peer // n_tp, 8)
    chunks = work.shape[1] // LANES
    column = lax.axis_index("tp")
    code_rows = codes_ref.shape[2] // LANES
    share = ids_ref.shape[2]
    total = None
    for turn in range(n_tp):
        other = column ^ turn
        codes = jnp.zeros((8, LANES), F32)
        for source in range(n_seq):
            block = recv_ref[source * n_tp + other].astype(F32)
            for part in range(chunks):
                work[source * sub_pad : (source + 1) * sub_pad, part * LANES : (part + 1) * LANES] = block[
                    part * sub_pad : (part + 1) * sub_pad
                ]
            note = block[chunks * sub_pad : chunks * sub_pad + 8]
            codes = codes + note
            for piece in range(up_to(share, LANES) // LANES):
                length = min(LANES, share - piece * LANES)
                ids_ref[other, source : source + 1, piece * LANES : piece * LANES + length] = note[
                    code_rows + piece : code_rows + piece + 1, :length
                ]
        power = jnp.zeros((8, LANES), F32)
        scale = jnp.ones((8, LANES), F32)
        for step in range(1, 8):
            above = codes >= 128.0 * 256.0**step
            power = power + jnp.where(above, 128.0, 0.0)
            scale = scale * jnp.where(above, 1.0 / 256.0, 1.0)
        spots = jnp.where(codes > 0.0, codes * scale - 128.0 + power, -1.0)
        for piece in range(code_rows):
            codes_ref[turn, :, piece * LANES : (piece + 1) * LANES] = spots[piece : piece + 1].astype(jnp.int32)
        part_sum = dot(work[...].astype(BF16), weight_refs[turn][...])
        total = part_sum if total is None else total + part_sum
    stream_ref[...] = total.astype(BF16)


def heads_kernel(n_tp, levels, codes_ref, gain_ref, weights_ref, *refs):
    shards = refs[:n_tp]
    query_ref, key_ref, value_ref = refs[n_tp : n_tp + 3]
    sets = refs[n_tp + 3 : n_tp + 3 + len(levels)]
    packed = refs[-1]
    rows = query_ref.shape[0]
    wide = query_ref.shape[1]
    heads = wide // SLOT
    column = lax.axis_index("tp")
    ordered = None
    for turn in range(n_tp):
        count = shards[turn].shape[0]
        spots = codes_ref[turn]
        place = one_hot(iota((rows, spots.shape[1]), 0) == spots)[:, :count]
        moved = dot(place, shards[turn][...])
        ordered = moved if ordered is None else ordered + moved
    mean = jnp.mean(ordered, axis=-1, keepdims=True)
    second = jnp.mean(ordered * ordered, axis=-1, keepdims=True)
    normed = (ordered - mean) * lax.rsqrt(second - mean * mean + EPS) * gain_ref[...]
    result = dot(normed.astype(BF16), weights_ref[...])
    query_ref[...] = (result[:, :wide] * HEAD_DIM ** (-0.5)).astype(BF16)
    key_ref[...] = result[:, wide : 2 * wide].astype(BF16)
    value_ref[...] = result[:, 2 * wide : 3 * wide].astype(BF16)
    packed[...] = result[:, 3 * wide :].astype(BF16)
    width = heads * HEAD_DIM
    for ref, level in zip(sets, levels):
        count = rows >> level
        lane = iota((count, 2 * width), 1)
        lane = jnp.where(lane >= width, lane - width, lane)
        chosen = None
        for head in range(heads):
            part = packed[pl.ds(head_start(level, head, column, rows), count), :]
            if chosen is None:
                chosen = part
            else:
                chosen = jnp.where(lane >= head * HEAD_DIM, part, chosen)
        ref[...] = chosen


def id_lanes(ids, wide, apart):
    count = ids.shape[1]
    lane = iota((IDS, wide), 1) & (SLOT - 1)
    group = iota((IDS, wide), 0)
    same = lane - HEAD_DIM == group
    if apart is None:
        table = jnp.where(same, 1.0, 0.0)
    else:
        table = jnp.where((lane >= HEAD_DIM) & ~same, apart, 0.0)
    return dot_tn(one_hot(iota((IDS, count), 0) == ids), table.astype(BF16))


def own_kernel(n_tp, groups, codes_ref, ids_ref, query_ref, key_ref, value_ref, *refs):
    shards = refs[:n_tp]
    acc_ref, masked_ref, base_ref = refs[n_tp : n_tp + 3]
    apart_refs = refs[n_tp + 3 : n_tp + 3 + len(groups)]
    keys_ref, values_ref, apart_all = refs[-3:]
    rows, wide = query_ref.shape
    heads = wide // SLOT
    place, column = lax.axis_index("seq"), lax.axis_index("tp")
    ids = ids_ref[pl.ds(place, 1), :].astype(jnp.int32)
    masked_ref[...] = (query_ref[...].astype(F32) + id_lanes(ids, wide, None)).astype(BF16)
    keys_ref[...] = (key_ref[...].astype(F32) + id_lanes(ids, wide, NEG)).astype(BF16)
    ones = jnp.where((iota((rows, wide), 1) & (SLOT - 1)) >= HEAD_DIM, 1.0, 0.0)
    values_ref[...] = (value_ref[...].astype(F32) + ones).astype(BF16)
    half = rows // 2
    for part in range(2):
        start = part * half
        query = masked_ref[start : start + half, :]
        slot_of = iota((half, wide), 1) >> 6
        spare = (iota((half, wide), 1) & (SLOT - 1)) >= HEAD_DIM + 8
        acc = None
        for head in range(heads):
            one = jnp.where(slot_of == head, query, jnp.zeros((), BF16))
            scores = dot_nt(one, keys_ref[...])
            top = jnp.max(scores, axis=1, keepdims=True)
            weights = jnp.exp(scores - top)
            if part == (head & 1):
                level_q = levels_of(start + iota((half, 1), 0), head, column, rows)
                level_k = levels_of(start + iota((1, half), 1), head, column, rows)
                times = (jnp.minimum(level_q, level_k) + 1).astype(F32)
                scaled = weights[:, start : start + half] * times
                others = weights[:, half - start : rows - start]
                weights = jnp.concatenate([scaled, others] if part == 0 else [others, scaled], axis=1)
            got = dot(weights.astype(BF16), values_ref[...])
            got = jnp.where(spare, top, got)
            acc = got if acc is None else jnp.where(slot_of == head, got, acc)
        acc_ref[start : start + half, :] = acc

    share = base_ref.shape[0]
    wanted = stored_at(column * share + iota((share, 1), 0), rows)
    base = None
    for turn in range(n_tp):
        spots = codes_ref[turn]
        moved = dot(one_hot(wanted == spots)[:, : shards[turn].shape[0]], shards[turn][...])
        base = moved if base is None else base + moved
    base_ref[...] = base.astype(BF16)

    for ref, (level, masks) in zip(apart_refs, groups):
        count = rows >> level
        slots = iota((count, wide), 1) >> 6
        for index, mask in enumerate(masks):
            far = ids_ref[pl.ds(place ^ mask, 1), :].astype(jnp.int32)
            apart_all[...] = id_lanes(far, wide, NEG).astype(BF16)
            chosen = None
            for head in range(heads):
                part = apart_all[pl.ds(head_start(level, head, column, rows), count), :]
                chosen = part if chosen is None else jnp.where(slots >= head, part, chosen)
            ref[index * count : (index + 1) * count, :] = chosen


def far_kernel(n_tp, groups, acc_ref, query_ref, *refs):
    n_groups = len(groups)
    apart_refs = refs[:n_groups]
    refs = refs[n_groups:]
    set_refs = []
    for _, masks in groups:
        set_refs.append(refs[: len(masks)])
        refs = refs[len(masks) :]
    out_refs, acc = refs[:n_tp], refs[n_tp]
    rows, wide = acc_ref.shape
    heads = wide // SLOT
    width = heads * HEAD_DIM
    column = lax.axis_index("tp")
    acc[...] = acc_ref[...]
    spread_key = one_hot(spread_mask(2 * width, wide, 0))
    spread_value = one_hot(spread_mask(2 * width, wide, width))
    for apart_ref, sets, (level, masks) in zip(apart_refs, set_refs, groups):
        count = rows >> level
        total = count * len(masks)
        pairs = jnp.concatenate([ref[...] for ref in sets], axis=0)
        keys = (dot(pairs, spread_key) + apart_ref[...].astype(F32)).astype(BF16)
        ones = jnp.where((iota((total, wide), 1) & (SLOT - 1)) >= HEAD_DIM, 1.0, 0.0)
        values = (dot(pairs, spread_value) + ones).astype(BF16)
        slot_of = iota((count, wide), 1) >> 6
        spare = (iota((count, wide), 1) & (SLOT - 1)) >= HEAD_DIM + 8
        for head in range(heads):
            first = head_start(level, head, column, rows)
            here = pl.ds(first, count)
            one = jnp.where(slot_of == head, query_ref[here, :], jnp.zeros((), BF16))
            scores = dot_nt(one, keys)
            before = acc[here, :]
            at = head * SLOT + HEAD_DIM + 8
            top_before = before[:, at : at + 1]
            top = jnp.maximum(top_before, jnp.max(scores, axis=1, keepdims=True))
            weights = jnp.exp(scores - top)
            level_q = levels_of(first + iota((count, 1), 0), head, column, rows)
            key_row = iota((1, total), 1)
            for index in range(1, len(masks)):
                key_row = key_row - jnp.where(iota((1, total), 1) >= index * count, count, 0)
            level_k = levels_of(first + key_row, head, column, rows)
            times = (jnp.minimum(level_q, level_k) - (level - 1)).astype(F32)
            got = dot((weights * times).astype(BF16), values)
            now = jnp.where(spare, top, before * jnp.exp(top_before - top) + got)
            acc[here, :] = jnp.where(slot_of == head, now, before)

    every = acc[...]
    lane = iota((rows, wide), 1)
    slot_of, inner = lane >> 6, lane & (SLOT - 1)
    share_of = None
    for head in range(heads):
        at = head * SLOT + HEAD_DIM
        part = 1.0 / every[:, at : at + 1]
        share_of = part + jnp.zeros_like(every) if share_of is None else jnp.where(slot_of == head, part, share_of)
    inside = inner < HEAD_DIM
    attn = jnp.where(inside, every * share_of, 0.0)
    mean = jnp.sum(attn, axis=1, keepdims=True) * (1.0 / width)
    high = mean.astype(BF16).astype(F32)
    rest = mean - high
    message = jnp.where(inside, attn - mean, jnp.where(inner == HEAD_DIM, high, rest)).astype(BF16)
    share = out_refs[0].shape[0]
    for turn in range(n_tp):
        wanted = stored_at((column ^ turn) * share + iota((share, 1), 0), rows)
        out_refs[turn][...] = dot(one_hot(wanted == iota((share, rows), 1)), message).astype(BF16)


def mix_kernel(n_tp, base_ref, *refs):
    message_refs = refs[:n_tp]
    weight_refs = refs[n_tp : 2 * n_tp]
    out_ref = refs[-1]
    share, wide = message_refs[0].shape
    heads = wide // SLOT
    features = n_tp * heads * HEAD_DIM
    inside = (iota((share, wide), 1) & (SLOT - 1)) < HEAD_DIM
    parts = []
    means = []
    for ref in message_refs:
        message = ref[...].astype(F32)
        parts.append(message)
        means.append(message[:, HEAD_DIM : HEAD_DIM + 1] + message[:, HEAD_DIM + 1 : HEAD_DIM + 2])
    mean = sum(means) * (1.0 / n_tp)
    parts = [jnp.where(inside, part + (own - mean), 0.0) for part, own in zip(parts, means)]
    spread = sum(jnp.sum(part * part, axis=1, keepdims=True) for part in parts) * (1.0 / features)
    factor = lax.rsqrt(spread + EPS)
    total = base_ref[...].astype(F32)
    gap = jnp.zeros((SLOT - HEAD_DIM, out_ref.shape[1]), BF16)
    for part, ref in zip(parts, weight_refs):
        pieces = []
        for head in range(heads):
            pieces += [ref[head * HEAD_DIM : (head + 1) * HEAD_DIM, :], gap]
        total = total + dot((part * factor).astype(BF16), jnp.concatenate(pieces, axis=0))
    out_ref[...] = total.astype(BF16)


def swap(block, axis, mask):
    count = lax.axis_size(axis)
    return lax.ppermute(block, axis, [(index, index ^ mask) for index in range(count)])


def gather_tp(block):
    across = swap(block, "tp", 2)
    return [block, swap(block, "tp", 1), across, swap(across, "tp", 1)]


def body(
    tiles,
    tile_target,
    slide_id,
    proj_weight,
    norm_gain,
    query_weight,
    key_weight,
    value_weight,
    sub_gain,
    out_weight,
):
    n_seq = lax.axis_size("seq")
    n_tp = lax.axis_size("tp")
    rows, tile_width = tiles.shape
    features = proj_weight.shape[1]
    width = query_weight.shape[1]
    heads = width // HEAD_DIM
    wide = heads * SLOT
    share = rows // n_tp
    peer = rows // n_seq
    sub_pad = up_to(peer // n_tp, 8)
    arriving = n_seq * sub_pad
    chunks = tile_width // LANES
    block_rows = up_to(chunks * sub_pad + 8, 16)

    first_group = max(1, n_seq // 16)
    sizes = [min(first_group * 2**branch, n_seq) for branch in range(BRANCHES)]
    groups = []
    for level in range(BRANCHES):
        masks = tuple(range(1 if level == 0 else sizes[level - 1], sizes[level]))
        if masks:
            groups.append((level, masks))

    (blocks,) = call(
        functools.partial(route_kernel, n_seq, n_tp, peer),
        "route",
        [((n_seq * n_tp, block_rows, LANES), BF16)],
        [tile_target.reshape(1, rows), slide_id.reshape(1, rows), tiles],
    )
    received = lax.all_to_all(blocks, ("seq", "tp"), split_axis=0, concat_axis=0, tiled=True)
    all_weights, scaled_weight = call(
        weights_kernel,
        "weights",
        [((features, 3 * wide + 2 * width), BF16), ((width, features), BF16)],
        [query_weight, key_weight, value_weight, sub_gain.reshape(1, width), out_weight],
    )
    proj_parts = gather_tp(proj_weight)
    out_parts = gather_tp(scaled_weight)

    stream, codes, ids = call(
        functools.partial(project_kernel, n_seq, n_tp, peer),
        "project",
        [
            ((arriving, features), BF16),
            ((n_tp, 1, up_to(arriving, LANES)), jnp.int32),
            ((n_tp, n_seq, share), F32),
        ],
        [received] + proj_parts,
        scratch=[pltpu.VMEM((arriving, tile_width), F32)],
    )
    ids = ids.transpose(1, 0, 2).reshape(n_seq, rows)
    shards = gather_tp(stream)

    results = call(
        functools.partial(heads_kernel, n_tp, [level for level, _ in groups]),
        "heads",
        [((rows, wide), BF16)] * 3 + [((rows >> level, 2 * width), BF16) for level, _ in groups],
        [codes, norm_gain.reshape(1, features), all_weights] + shards,
        scratch=[pltpu.VMEM((rows, 2 * width), BF16)],
    )
    query, key, value = results[:3]
    far_sets = [None] * len(groups)
    for index in reversed(range(len(groups))):
        far_sets[index] = [swap(results[3 + index], "seq", mask) for mask in groups[index][1]]

    own = call(
        functools.partial(own_kernel, n_tp, groups),
        "own",
        [((rows, wide), F32), ((rows, wide), BF16), ((share, features), BF16)]
        + [(((rows >> level) * len(masks), wide), BF16) for level, masks in groups],
        [codes, ids, query, key, value] + shards,
        scratch=[pltpu.VMEM((rows, wide), BF16)] * 3,
    )
    messages = call(
        functools.partial(far_kernel, n_tp, groups),
        "far",
        [((share, wide), BF16)] * n_tp,
        [own[0], own[1]] + list(own[3:]) + [one for sets in far_sets for one in sets],
        scratch=[pltpu.VMEM((rows, wide), F32)],
    )
    arrived = [messages[0]] + [swap(messages[turn], "tp", turn) for turn in range(1, n_tp)]
    (result,) = call(
        functools.partial(mix_kernel, n_tp),
        "mix",
        [((share, features), BF16)],
        [own[2]] + arrived + out_parts,
    )
    return result


def solution(mesh):
    return jax.shard_map(
        body,
        mesh=mesh,
        in_specs=(
            P("seq", "tp"),
            P("seq"),
            P("seq"),
            P("tp", None),
            P(),
            P(None, "tp"),
            P(None, "tp"),
            P(None, "tp"),
            P("tp"),
            P("tp", None),
        ),
        out_specs=P(("seq", "tp"), None),
        check_vma=False,
    )
```

```python
import functools

import jax
import jax.numpy as jnp
from jax import lax
from jax.experimental import pallas as pl
from jax.experimental.pallas import tpu as pltpu
from jax.sharding import PartitionSpec as P

BRANCHES = 5
HEAD_DIM = 48
SLOT = 64
LANES = 128
IDS = 16
CLASSES = 2 ** (BRANCHES - 1)
NEG = -1e30
EPS = 1e-05
BF16 = jnp.bfloat16
F32 = jnp.float32
VMEM_BYTES = 16 * 1024 * 1024
LARGE_VMEM_BYTES = 48 * 1024 * 1024
ALL_VMEM_BYTES = 56 * 1024 * 1024


def up_to(count, step):
    return (count + step - 1) // step * step


def iota(shape, dim):
    return lax.broadcasted_iota(jnp.int32, shape, dim)


def dot(left, right):
    return jnp.dot(left, right, preferred_element_type=F32)


def dot_nt(left, right):
    return lax.dot_general(left, right, (((1,), (1,)), ((), ())), preferred_element_type=F32)


def dot_tn(left, right):
    return lax.dot_general(left, right, (((0,), (0,)), ((), ())), preferred_element_type=F32)


def one_hot(mask):
    return jnp.where(mask, 1.0, 0.0).astype(BF16)


def stored_at(position, rows):
    residue = position & (CLASSES - 1)
    flipped = jnp.zeros_like(residue)
    for bit in range(BRANCHES - 1):
        flipped = flipped + (((residue >> bit) & 1) << (BRANCHES - 2 - bit))
    return flipped * (rows // CLASSES) + (position >> (BRANCHES - 1))


def head_start(level, head, column, rows):
    start = 0
    for bit in range(level):
        value = (head >> bit) & 1 if bit < 2 else (column >> (bit - 2)) & 1
        start = start + value * (rows >> (bit + 1))
    return start


def call(kernel, name, outs, args, scratch=(), cost=1, vmem_bytes=VMEM_BYTES, apart=(), out_apart=()):
    vmem = pl.BlockSpec(memory_space=pltpu.VMEM)
    anywhere = pl.BlockSpec(memory_space=pltpu.HBM)
    return pl.pallas_call(
        kernel,
        name=name,
        out_shape=[jax.ShapeDtypeStruct(shape, dtype) for shape, dtype in outs],
        in_specs=[anywhere if index in apart else vmem for index in range(len(args))],
        out_specs=[anywhere if index in out_apart else vmem for index in range(len(outs))],
        scratch_shapes=list(scratch),
        compiler_params=pltpu.CompilerParams(vmem_limit_bytes=vmem_bytes),
        cost_estimate=pl.CostEstimate(flops=int(cost * 1e9), bytes_accessed=0, transcendentals=0),
    )(*args)


def one_row(ref):
    return jnp.concatenate([ref[index : index + 1, :] for index in range(ref.shape[0])], axis=1)


def route_kernel(
    n_seq,
    n_tp,
    peer,
    target_hbm,
    slide_hbm,
    tiles_hbm,
    proj_hbm,
    out_weight_hbm,
    out_hbm,
    bundle_hbm,
    rest_hbm,
    target_ref,
    slide_ref,
    tiles_ref,
    out_ref,
    bundle_ref,
    rest_ref,
    sems,
    out_sems,
):
    depth = proj_hbm.shape[0]
    along = bundle_hbm.shape[0] - depth
    fetches = [
        pltpu.make_async_copy(target_hbm, target_ref, sems.at[0]),
        pltpu.make_async_copy(slide_hbm, slide_ref, sems.at[1]),
        pltpu.make_async_copy(tiles_hbm, tiles_ref, sems.at[2]),
        pltpu.make_async_copy(proj_hbm, bundle_ref.at[pl.ds(0, depth)], sems.at[3]),
        pltpu.make_async_copy(out_weight_hbm.at[pl.ds(0, along)], bundle_ref.at[pl.ds(depth, along)], sems.at[4]),
        pltpu.make_async_copy(out_weight_hbm.at[pl.ds(along, rest_hbm.shape[0])], rest_ref, sems.at[5]),
    ]
    for fetch in fetches:
        fetch.start()
    fetches[0].wait()
    rows = tiles_ref.shape[0]
    chunks = tiles_ref.shape[1] // LANES
    sub = peer // n_tp
    sub_pad = up_to(sub, 8)
    blocks = n_seq * n_tp
    place, column = lax.axis_index("seq"), lax.axis_index("tp")
    target = one_row(target_ref)
    owner = jnp.floor((target.astype(F32) + 0.5) * (1.0 / rows)).astype(jnp.int32)
    flags = jnp.where(iota((n_seq, rows), 0) == owner, 1.0, 0.0)
    before = one_hot(iota((rows, rows), 0) <= iota((rows, rows), 1))
    counts = dot(flags.astype(BF16), before)
    slot = jnp.sum(flags * counts, axis=0, keepdims=True).astype(jnp.int32) - 1
    lane_of = jnp.zeros_like(slot)
    for turn in range(1, n_tp):
        lane_of = lane_of + jnp.where(slot >= turn * sub, 1, 0)
    low = slot - lane_of * sub
    target_row = (owner * n_tp + lane_of) * sub_pad + low
    chooser = one_hot(iota((blocks * sub_pad, rows), 0) == target_row)

    spot = stored_at(target - owner * rows, rows)
    high = spot >> 7
    code = ((spot & 127) + 128).astype(F32)
    for bit in range(3):
        code = code * jnp.where((high >> bit) & 1 == 1, 256.0 ** (2**bit), 1.0)
    arrival = place * sub_pad + low
    extra = n_seq * 8
    code_rows = up_to(n_seq * sub_pad, LANES) // LANES
    line = iota((extra, rows), 0)
    mine = (owner == (line >> 3)) & (lane_of == column) & ((arrival >> 7) == (line & 7))
    coded = dot_nt(
        jnp.where(mine, code, 0.0).astype(BF16),
        one_hot(iota((LANES, rows), 0) == (arrival & 127)),
    )
    share = rows // n_tp
    fetches[1].wait()
    kept = stored_at(iota((1, rows), 1), rows) - column * share
    held = (kept >= 0) & (kept < share) & ((kept >> 7) + code_rows == (line & 7))
    ids = dot_nt(
        jnp.where(held, one_row(slide_ref).astype(F32), 0.0).astype(BF16),
        one_hot(iota((LANES, rows), 0) == (kept & 127)),
    )
    notes = coded + ids
    for fetch in fetches[3:]:
        fetch.wait()
    stores = [
        pltpu.make_async_copy(bundle_ref, bundle_hbm, sems.at[6]),
        pltpu.make_async_copy(rest_ref, rest_hbm, sems.at[7]),
    ]
    for store in stores:
        store.start()
    fetches[2].wait()
    picked = dot(chooser, tiles_ref[...])
    pad = out_hbm.shape[1] - chunks * sub_pad - 8
    for block in range(blocks):
        base = block * sub_pad
        pieces = [
            picked[base : base + sub_pad, part * LANES : (part + 1) * LANES] for part in range(chunks)
        ]
        start = block // n_tp * 8
        pieces.append(notes[start : start + 8])
        if pad:
            pieces.append(jnp.zeros((pad, LANES), F32))
        out_ref[block] = jnp.concatenate(pieces, axis=0).astype(BF16)
        if block % n_tp == n_tp - 1:
            some = pl.ds(block - n_tp + 1, n_tp)
            stores.append(pltpu.make_async_copy(out_ref.at[some], out_hbm.at[some], out_sems.at[block // n_tp]))
            stores[-1].start()
    for store in stores:
        store.wait()


def spread_mask(width, wide, shift):
    row = iota((width, wide), 0) - shift
    lane = iota((width, wide), 1)
    inner = lane & (SLOT - 1)
    return (inner < HEAD_DIM) & (row == (lane >> 6) * HEAD_DIM + inner)


def project_kernel(n_seq, n_tp, peer, recv_hbm, *refs):
    weight_refs = refs[: n_tp - 1]
    total_ref, last_ref, codes_ref, ids_ref, recv_ref, work, sems = refs[n_tp - 1 :]
    fetches = []
    for source in range(n_seq):
        some = pl.ds(source * n_tp, n_tp)
        fetches.append(pltpu.make_async_copy(recv_hbm.at[some], recv_ref.at[some], sems.at[source]))
        fetches[-1].start()
    sub_pad = up_to(peer // n_tp, 8)
    chunks = work.shape[2] // LANES
    column = lax.axis_index("tp")
    code_rows = codes_ref.shape[2] // LANES
    share = ids_ref.shape[1] // n_tp
    at = chunks * sub_pad
    even = at // 16 * 16
    notes = [jnp.zeros((8, LANES), F32)] * n_tp
    for source in range(n_seq):
        fetches[source].wait()
        for turn in range(n_tp):
            block = recv_ref[source * n_tp + (column ^ turn)].astype(F32)
            for part in range(chunks):
                work[turn, source * sub_pad : (source + 1) * sub_pad, part * LANES : (part + 1) * LANES] = block[
                    part * sub_pad : (part + 1) * sub_pad
                ]
            notes[turn] = notes[turn] + block[at : at + 8]
        pieces = []
        for other in range(n_tp):
            note = recv_ref[source * n_tp + other, even : even + 16, :].astype(F32)[at - even :]
            for piece in range(up_to(share, LANES) // LANES):
                length = min(LANES, share - piece * LANES)
                pieces.append(note[code_rows + piece : code_rows + piece + 1, :length])
        ids_ref[source : source + 1, :] = jnp.concatenate(pieces, axis=1)
    total = None
    for turn in range(n_tp - 1):
        part_sum = dot(work[turn].astype(BF16), weight_refs[turn][: work.shape[2]])
        total = part_sum if total is None else total + part_sum
    total_ref[...] = total
    last_ref[...] = work[n_tp - 1].astype(BF16)
    for turn in range(n_tp):
        codes = notes[turn]
        power = jnp.zeros((8, LANES), F32)
        scale = jnp.ones((8, LANES), F32)
        for step in range(1, 8):
            above = codes >= 128.0 * 256.0**step
            power = power + jnp.where(above, 128.0, 0.0)
            scale = scale * jnp.where(above, 1.0 / 256.0, 1.0)
        spots = jnp.where(codes > 0.0, codes * scale - 128.0 + power, -1.0)
        for piece in range(code_rows):
            codes_ref[turn, :, piece * LANES : (piece + 1) * LANES] = spots[piece : piece + 1].astype(jnp.int32)


def stream_kernel(total_ref, last_ref, weight_ref, stream_ref):
    part_sum = dot(last_ref[...], weight_ref[: last_ref.shape[1]])
    stream_ref[...] = (total_ref[...] + part_sum).astype(BF16)


def key_value_query(stream, gain, weights):
    rows = stream.astype(F32)
    mean = jnp.mean(rows, axis=-1, keepdims=True)
    second = jnp.mean(rows * rows, axis=-1, keepdims=True)
    normed = ((rows - mean) * lax.rsqrt(second - mean * mean + EPS) * gain).astype(BF16)
    result = dot_nt(normed, weights)
    third = weights.shape[0] // 3
    scale = jnp.where(iota((1, 3 * third), 1) >= 2 * third, HEAD_DIM ** (-0.5), 1.0)
    return (result * scale).astype(BF16)


def place_heads(turn, codes_ref, gain_ref, key_ref, value_ref, query_ref, stream_ref, rows):
    weights = jnp.concatenate([key_ref[...], value_ref[...], query_ref[...]], axis=0)
    result = key_value_query(stream_ref[...], one_row(gain_ref), weights)
    spots = codes_ref[turn]
    place = one_hot(iota((rows, spots.shape[1]), 0) == spots)[:, : result.shape[0]]
    return dot(place, result)


def first_heads_kernel(
    groups,
    codes_ref,
    gain_ref,
    key_ref,
    value_ref,
    query_ref,
    stream_ref,
    ids_ref,
    sub_gain_ref,
    out_ref,
    same_ref,
    apart_ref,
    back_ref,
    gains_ref,
    *refs,
):
    rows, wide = same_ref.shape
    heads = wide // SLOT
    width = heads * HEAD_DIM
    place, column = lax.axis_index("seq"), lax.axis_index("tp")
    first = place_heads(0, codes_ref, gain_ref, key_ref, value_ref, query_ref, stream_ref, rows)
    out_ref[...] = first.astype(BF16)

    ids = ids_ref[pl.ds(place, 1), :].astype(jnp.int32)
    same_ref[...] = id_lanes(ids, wide, None).astype(BF16)
    apart_ref[...] = id_lanes(ids, wide, NEG).astype(BF16)
    share = back_ref.shape[1]
    for turn in range(back_ref.shape[0]):
        wanted = stored_at((column ^ turn) * share + iota((share, 1), 0), rows)
        back_ref[turn] = one_hot(wanted == iota((share, rows), 1))
    gain = sub_gain_ref[...]
    high = gain.astype(BF16).astype(F32)
    mid = (gain - high).astype(BF16).astype(F32)
    low = (gain - high) - mid
    line = iota((16, width), 0)
    parts = jnp.where(line == 0, high, jnp.where(line == 1, mid, jnp.where(line == 2, low, 0.0)))
    gains_ref[...] = dot(parts.astype(BF16), one_hot(spread_mask(width, wide, 0))).astype(BF16)
    apart_refs, apart_all = refs[:-1], refs[-1]
    for ref, (level, masks) in zip(apart_refs, groups):
        count = rows >> level
        slots = iota((count, wide), 1) >> 6
        for index, mask in enumerate(masks):
            far = ids_ref[pl.ds(place ^ mask, 1), :].astype(jnp.int32)
            apart_all[...] = id_lanes(far, wide, NEG).astype(BF16)
            chosen = None
            for head in range(heads):
                part = apart_all[pl.ds(head_start(level, head, column, rows), count), :]
                chosen = part if chosen is None else jnp.where(slots >= head, part, chosen)
            ref[index * count : (index + 1) * count, :] = chosen


def more_heads_kernel(
    turn, codes_ref, gain_ref, key_ref, value_ref, query_ref, stream_ref, before_ref, out_ref
):
    more = place_heads(turn, codes_ref, gain_ref, key_ref, value_ref, query_ref, stream_ref, out_ref.shape[0])
    out_ref[...] = (before_ref[...].astype(F32) + more).astype(BF16)


def last_heads_kernel(
    turn, levels, codes_ref, gain_ref, key_ref, value_ref, query_ref, stream_ref, before_ref, packed, *sets
):
    rows = packed.shape[0]
    width = key_ref.shape[0]
    heads = width // HEAD_DIM
    column = lax.axis_index("tp")
    more_heads_kernel(
        turn, codes_ref, gain_ref, key_ref, value_ref, query_ref, stream_ref, before_ref, packed
    )
    for ref, level in zip(sets, levels):
        count = rows >> level
        lane = iota((count, 2 * width), 1)
        lane = jnp.where(lane >= width, lane - width, lane)
        chosen = None
        for head in range(heads):
            part = packed[pl.ds(head_start(level, head, column, rows), count), : 2 * width]
            chosen = part if chosen is None else jnp.where(lane >= head * HEAD_DIM, part, chosen)
        ref[...] = chosen


def id_lanes(ids, wide, apart):
    count = ids.shape[1]
    lane = iota((IDS, wide), 1) & (SLOT - 1)
    group = iota((IDS, wide), 0)
    same = lane - HEAD_DIM == group
    if apart is None:
        table = jnp.where(same, 1.0, 0.0)
    else:
        table = jnp.where((lane >= HEAD_DIM) & ~same, apart, 0.0)
    return dot_tn(one_hot(iota((IDS, count), 0) == ids), table.astype(BF16))


def agreement(level, firsts, column, rows, total, count):
    q_on, k_on = [], []
    for index, (head, first) in enumerate(firsts):
        for size, lines in ((count, q_on), (total, k_on)):
            line, at = iota((8, size), 0), iota((8, size), 1)
            if size > count:
                for step in range(1, size // count):
                    at = at - jnp.where(iota((8, size), 1) >= step * count, count, 0)
            start = jnp.zeros((8, size), jnp.int32)
            length = jnp.zeros((8, size), jnp.int32)
            for branch in range(level, BRANCHES):
                start = jnp.where(line == branch, head_start(branch, head, column, rows) - first, start)
                length = jnp.where(line == branch, rows >> branch, length)
            lines.append(jnp.where((at >= start) & (at < start + length), 1.0, 0.0))
        blank = jnp.zeros((8, count), F32)
        q_on[index] = jnp.concatenate(
            [q_on[index] if place == index else blank for place in range(len(firsts))], axis=1
        )
    return jnp.concatenate(q_on, axis=0).astype(BF16), jnp.concatenate(k_on, axis=0).astype(BF16)


def repeat(block, times):
    return jnp.concatenate([block] * times, axis=1)


def own_kernel(packed_ref, same_ref, apart_ref, acc_ref, tops_ref, masked_ref, keys_ref, values_ref):
    rows, wide = masked_ref.shape
    heads = wide // SLOT
    width = heads * HEAD_DIM
    column = lax.axis_index("tp")
    spread = one_hot(spread_mask(width, wide, 0))
    pairs = packed_ref[:, : 2 * width]
    query = dot(packed_ref[:, 2 * width :], spread)
    masked_ref[...] = (query + same_ref[...].astype(F32)).astype(BF16)
    key = dot(pairs, one_hot(spread_mask(2 * width, wide, 0)))
    keys_ref[...] = (key + apart_ref[...].astype(F32)).astype(BF16)
    ones = jnp.where((iota((rows, wide), 1) & (SLOT - 1)) >= HEAD_DIM, 1.0, 0.0)
    value = dot(pairs, one_hot(spread_mask(2 * width, wide, width)))
    values_ref[...] = (value + ones).astype(BF16)
    half = rows // 2
    slot_of = iota((half, wide), 1) >> 6
    for part in range(2):
        start = part * half
        query = masked_ref[start : start + half, :]
        acc = None
        for head in range(heads):
            one = jnp.where(slot_of == head, query, jnp.zeros((), BF16))
            scores = dot_nt(one, keys_ref[...])
            top = jnp.max(scores, axis=1, keepdims=True)
            tops_ref[head, start : start + half, :] = jnp.broadcast_to(top, (half, LANES))
            weights = jnp.exp(scores - top)
            if part == (head & 1):
                times = dot_tn(*agreement(0, [(head, start)], column, rows, half, half))
                scaled = weights[:, start : start + half] * times
                others = weights[:, half - start : rows - start]
                weights = jnp.concatenate([scaled, others] if part == 0 else [others, scaled], axis=1)
            got = dot(weights.astype(BF16), values_ref[...])
            acc = got if acc is None else jnp.where(slot_of == head, got, acc)
        acc_ref[start : start + half, :] = acc


def merge_sets(level, masks, sets, acc_ref, tops_ref, query_ref, apart_ref, finish):
    rows, wide = query_ref.shape
    heads = wide // SLOT
    width = heads * HEAD_DIM
    column = lax.axis_index("tp")
    count = rows >> level
    some = min(max(1, rows // count), len(masks))
    total = some * count
    spread_key = one_hot(spread_mask(2 * width, wide, 0))
    spread_value = one_hot(spread_mask(2 * width, wide, width))
    slot_of = iota((count, wide), 1) >> 6
    together = heads if heads * count * total <= 2**20 else 1
    for low in range(0, heads, together):
        firsts = [(head, head_start(level, head, column, rows)) for head in range(low, low + together)]
        q_on, k_on = agreement(level, firsts, column, rows, total, count)
        times = dot_tn(q_on, k_on)
        query = jnp.concatenate(
            [
                jnp.where(slot_of == head, query_ref[pl.ds(first, count), :], jnp.zeros((), BF16))
                for head, first in firsts
            ],
            axis=0,
        )
        sums = jnp.concatenate([acc_ref[pl.ds(first, count), :] for _, first in firsts], axis=0)
        tops = jnp.concatenate([tops_ref[head, pl.ds(first, count), :] for head, first in firsts], axis=0)
        for begin in range(0, len(masks), some):
            pairs = jnp.concatenate([ref[...] for ref in sets[begin : begin + some]], axis=0)
            keys = dot(pairs, spread_key) + apart_ref[begin * count : begin * count + total, :].astype(F32)
            ones = jnp.where((iota((total, wide), 1) & (SLOT - 1)) >= HEAD_DIM, 1.0, 0.0)
            values = (dot(pairs, spread_value) + ones).astype(BF16)
            scores = dot_nt(query, keys.astype(BF16))
            top = jnp.maximum(tops, jnp.max(scores, axis=1, keepdims=True))
            weights = jnp.exp(scores - repeat(top, total // LANES)) * times
            got = dot(weights.astype(BF16), values)
            sums = sums * repeat(jnp.exp(tops - top), wide // LANES) + got
            tops = top
        finish(firsts, sums, tops)


def slot_lane(values, inner):
    wide = values.shape[1]
    row, lane = iota((wide, wide), 0), iota((wide, wide), 1)
    pick = one_hot(row == (lane >> 6) * SLOT + inner)
    high = values.astype(BF16)
    low = (values - high.astype(F32)).astype(BF16)
    return dot(high, pick) + dot(low, pick)


def near_kernel(groups, acc_ref, tops_ref, query_ref, *refs):
    apart_refs, refs = refs[: len(groups)], refs[len(groups) :]
    sums_ref, new_tops_ref = refs[-2:]
    wide = query_ref.shape[1]
    sums_ref[...] = acc_ref[...]
    new_tops_ref[...] = tops_ref[...]

    def finish(firsts, sums, tops):
        count = sums.shape[0] // len(firsts)
        slot_of = iota((count, wide), 1) >> 6
        for index, (head, first) in enumerate(firsts):
            here, part = pl.ds(first, count), slice(index * count, (index + 1) * count)
            sums_ref[here, :] = jnp.where(slot_of == head, sums[part], sums_ref[here, :])
            new_tops_ref[head, here, :] = tops[part]

    for apart_ref, (level, masks) in zip(apart_refs, groups):
        merge_sets(level, masks, refs[: len(masks)], sums_ref, new_tops_ref, query_ref, apart_ref, finish)
        refs = refs[len(masks) :]


def mid_kernel(groups, acc_ref, tops_ref, query_ref, *refs):
    sums_ref, _, early_ref, centre_ref = refs[-4:]
    near_kernel(groups, acc_ref, tops_ref, query_ref, *refs[:-2])
    rows, wide = query_ref.shape
    heads = wide // SLOT
    every = sums_ref[...]
    inner = iota((rows, wide), 1) & (SLOT - 1)
    attn = jnp.where(inner < HEAD_DIM, every / slot_lane(every, HEAD_DIM), 0.0)
    average = jnp.full((wide, wide), 1.0, BF16)
    centre = (dot(attn.astype(BF16), average) * (1.0 / (heads * HEAD_DIM))).astype(BF16).astype(F32)
    centre_ref[...] = centre
    early_ref[...] = jnp.where(inner < HEAD_DIM, attn - centre, centre).astype(BF16)


def far_kernel(n_tp, level, masks, acc_ref, tops_ref, query_ref, early_ref, centre_ref, back_ref, gains_ref, *refs):
    apart_ref, refs = refs[0], refs[1:]
    sets, refs = refs[: len(masks)], refs[len(masks) :]
    out_refs, message = refs[:n_tp], refs[-1]
    message[...] = early_ref[...]

    def finish(firsts, sums, tops):
        count = sums.shape[0] // len(firsts)
        lane = iota((count, sums.shape[1]), 1)
        now = sums / slot_lane(sums, HEAD_DIM)
        for index, (head, first) in enumerate(firsts):
            here, part = pl.ds(first, count), slice(index * count, (index + 1) * count)
            mine = (lane >= head * SLOT) & (lane < head * SLOT + HEAD_DIM)
            new = (now[part] - centre_ref[here, :]).astype(BF16)
            message[here, :] = jnp.where(mine, new, message[here, :])

    merge_sets(level, masks, sets, acc_ref, tops_ref, query_ref, apart_ref, finish)
    share = back_ref.shape[1]
    final = message[...]
    for turn in range(n_tp):
        out_refs[turn][:share] = dot(back_ref[turn], final).astype(BF16)
        out_refs[turn][share:] = gains_ref[...]


def base_kernel(n_tp, codes_ref, *refs):
    shards, bundle_refs, rest_refs = refs[:n_tp], refs[n_tp : 2 * n_tp], refs[2 * n_tp : 3 * n_tp]
    base_ref, weights_ref = refs[-2:]
    share = base_ref.shape[0]
    rows = share * n_tp
    wanted = stored_at(lax.axis_index("tp") * share + iota((share, 1), 0), rows)
    base = None
    for turn in range(n_tp):
        spots = codes_ref[turn]
        moved = dot(one_hot(wanted == spots)[:, : shards[turn].shape[0]], shards[turn][...])
        base = moved if base is None else base + moved
    base_ref[...] = base.astype(BF16)
    wide = weights_ref.shape[1]
    heads = wide // SLOT
    gap = jnp.zeros((SLOT - HEAD_DIM, base_ref.shape[1]), BF16)
    for turn, (ref, rest_ref) in enumerate(zip(bundle_refs, rest_refs)):
        along = heads * HEAD_DIM - rest_ref.shape[0]
        depth = ref.shape[0] - along
        for head in range(heads):
            at, to = head * HEAD_DIM, head * SLOT
            early = min(max(along - at, 0), HEAD_DIM)
            if early:
                weights_ref[turn, to : to + early, :] = ref[depth + at : depth + at + early, :]
            if early < HEAD_DIM:
                weights_ref[turn, to + early : to + HEAD_DIM, :] = rest_ref[
                    at + early - along : at + HEAD_DIM - along, :
                ]
            weights_ref[turn, to + HEAD_DIM : to + SLOT, :] = gap


def mix_kernel(n_tp, base_ref, weights_ref, *refs):
    message_refs, out_ref = refs[:n_tp], refs[-1]
    share, wide = base_ref.shape[0], weights_ref.shape[1]
    features = n_tp * (wide // SLOT) * HEAD_DIM
    inside = (iota((share, wide), 1) & (SLOT - 1)) < HEAD_DIM
    parts, centres, gains = [], [], []
    for ref in message_refs:
        message = ref[:share].astype(F32)
        extra = ref[share:].astype(F32)
        parts.append(jnp.where(inside, message, 0.0))
        centres.append(message[:, HEAD_DIM : HEAD_DIM + 1])
        gains.append(extra[0:1] + extra[1:2] + extra[2:3])
    each = features // n_tp
    sums = [jnp.sum(part, axis=1, keepdims=True) + centre * each for part, centre in zip(parts, centres)]
    mean = sum(sums) * (1.0 / features)
    parts = [jnp.where(inside, part + (centre - mean), 0.0) for part, centre in zip(parts, centres)]
    spread = jnp.sum(sum(part * part for part in parts), axis=1, keepdims=True) * (1.0 / features)
    factor = lax.rsqrt(spread + EPS)
    total = base_ref[...].astype(F32)
    for turn, (part, gain) in enumerate(zip(parts, gains)):
        total = total + dot((part * factor * gain).astype(BF16), weights_ref[turn])
    out_ref[...] = total.astype(BF16)


def swap(block, axis, mask):
    count = lax.axis_size(axis)
    return lax.ppermute(block, axis, [(index, index ^ mask) for index in range(count)])


def gather_tp(block):
    across = swap(block, "tp", 2)
    return [block, swap(block, "tp", 1), across, swap(across, "tp", 1)]


def body(
    tiles,
    tile_target,
    slide_id,
    proj_weight,
    norm_gain,
    query_weight,
    key_weight,
    value_weight,
    sub_gain,
    out_weight,
):
    n_seq = lax.axis_size("seq")
    n_tp = lax.axis_size("tp")
    rows, tile_width = tiles.shape
    features = proj_weight.shape[1]
    width = query_weight.shape[1]
    heads = width // HEAD_DIM
    wide = heads * SLOT
    share = rows // n_tp
    peer = rows // n_seq
    sub_pad = up_to(peer // n_tp, 8)
    arriving = n_seq * sub_pad
    chunks = tile_width // LANES
    block_rows = up_to(chunks * sub_pad + 8, 16)

    first_group = max(1, n_seq // 16)
    sizes = [min(first_group * 2**branch, n_seq) for branch in range(BRANCHES)]
    groups = []
    for level in range(BRANCHES):
        masks = tuple(range(1 if level == 0 else sizes[level - 1], sizes[level]))
        if masks:
            groups.append((level, masks))

    vmem_bytes = VMEM_BYTES if n_seq <= 8 else LARGE_VMEM_BYTES
    blocks, bundle, rest = call(
        functools.partial(route_kernel, n_seq, n_tp, peer),
        "route",
        [((n_seq * n_tp, block_rows, LANES), BF16), ((tile_width + width // 3, features), BF16)]
        + [((width - width // 3, features), BF16)],
        [tile_target.reshape(-1, LANES), slide_id.reshape(-1, LANES), tiles, proj_weight, out_weight],
        scratch=[
            pltpu.VMEM((rows // LANES, LANES), jnp.int32),
            pltpu.VMEM((rows // LANES, LANES), jnp.int32),
            pltpu.VMEM(tiles.shape, BF16),
            pltpu.VMEM((n_seq * n_tp, block_rows, LANES), BF16),
            pltpu.VMEM((tile_width + width // 3, features), BF16),
            pltpu.VMEM((width - width // 3, features), BF16),
            pltpu.SemaphoreType.DMA((8,)),
            pltpu.SemaphoreType.DMA((n_seq,)),
        ],
        cost=3,
        vmem_bytes=ALL_VMEM_BYTES,
        apart=(0, 1, 2, 3, 4),
        out_apart=(0, 1, 2),
    )
    received = lax.all_to_all(blocks, ("seq", "tp"), split_axis=0, concat_axis=0, tiled=True)
    bundles, rests = gather_tp(bundle), gather_tp(rest)

    total, last, codes, ids = call(
        functools.partial(project_kernel, n_seq, n_tp, peer),
        "project",
        [((arriving, features), F32), ((arriving, tile_width), BF16)]
        + [((n_tp, 1, up_to(arriving, LANES)), jnp.int32), ((n_seq, rows), F32)],
        [received] + bundles[:-1],
        scratch=[
            pltpu.VMEM(received.shape, BF16),
            pltpu.VMEM((n_tp, arriving, tile_width), F32),
            pltpu.SemaphoreType.DMA((n_seq,)),
        ],
        vmem_bytes=vmem_bytes,
        apart=(0,),
    )
    (stream,) = call(
        stream_kernel,
        "stream",
        [((arriving, features), BF16)],
        [total, last, bundles[-1]],
        vmem_bytes=vmem_bytes,
    )
    shards = gather_tp(stream)

    gain = norm_gain.reshape(-1, LANES)
    weights = [gain, key_weight.T, value_weight.T, query_weight.T]
    partial, same, apart, back, gains, *far_apart = call(
        functools.partial(first_heads_kernel, groups),
        "heads_1",
        [
            ((rows, 3 * width), BF16),
            ((rows, wide), BF16),
            ((rows, wide), BF16),
            ((n_tp, share, rows), BF16),
            ((16, wide), BF16),
        ]
        + [(((rows >> level) * len(masks), wide), BF16) for level, masks in groups],
        [codes] + weights + [shards[0], ids, sub_gain.reshape(1, width)],
        scratch=[pltpu.VMEM((rows, wide), BF16)],
        vmem_bytes=vmem_bytes,
    )
    for turn in range(1, n_tp - 1):
        (partial,) = call(
            functools.partial(more_heads_kernel, turn),
            "heads_2",
            [((rows, 3 * width), BF16)],
            [codes] + weights + [shards[turn], partial],
            cost=10 if turn == n_tp - 2 else 1,
            vmem_bytes=vmem_bytes,
        )
    packed, *sets = call(
        functools.partial(last_heads_kernel, n_tp - 1, [level for level, _ in groups]),
        "heads_3",
        [((rows, 3 * width), BF16)] + [((rows >> level, 2 * width), BF16) for level, _ in groups],
        [codes] + weights + [shards[n_tp - 1], partial],
        vmem_bytes=vmem_bytes,
    )
    sent = [[swap(one, "seq", mask) for mask in masks] for one, (_, masks) in zip(sets[:-1], groups)]
    direct = {mask: swap(sets[-1], "seq", mask) for mask in groups[-1][1] if mask % 2 == 0}
    sent.append([swap(direct[mask - 1], "seq", 1) if mask % 2 else direct[mask] for mask in groups[-1][1]])

    acc, tops, masked = call(
        own_kernel,
        "own",
        [((rows, wide), F32), ((heads, rows, LANES), F32), ((rows, wide), BF16)],
        [packed, same, apart],
        scratch=[pltpu.VMEM((rows, wide), BF16)] * 2,
        cost=0.1,
        vmem_bytes=vmem_bytes,
    )
    for index in range(len(groups) - 1):
        final = index == len(groups) - 2
        acc, tops, *rest_of = call(
            functools.partial(mid_kernel if final else near_kernel, [groups[index]]),
            "mid" if final else "near",
            [((rows, wide), F32), ((heads, rows, LANES), F32)]
            + ([((rows, wide), BF16), ((rows, wide), F32)] if final else []),
            [acc, tops, masked, far_apart[index]] + sent[index],
            cost=6,
            vmem_bytes=vmem_bytes,
        )
    early, centre = rest_of
    messages = call(
        functools.partial(far_kernel, n_tp, *groups[-1]),
        "far",
        [((share + 16, wide), BF16)] * n_tp,
        [acc, tops, masked, early, centre, back, gains, far_apart[-1]] + sent[-1],
        scratch=[pltpu.VMEM((rows, wide), BF16)],
        vmem_bytes=vmem_bytes,
    )
    arrived = [messages[0]] + [swap(messages[turn], "tp", turn) for turn in range(1, n_tp)]
    base, padded = call(
        functools.partial(base_kernel, n_tp),
        "base",
        [((share, features), BF16), ((n_tp, wide, features), BF16)],
        [codes] + shards + bundles + rests,
        vmem_bytes=vmem_bytes,
    )
    (result,) = call(
        functools.partial(mix_kernel, n_tp),
        "mix",
        [((share, features), BF16)],
        [base, padded] + arrived,
    )
    return result


def solution(mesh):
    return jax.shard_map(
        body,
        mesh=mesh,
        in_specs=(
            P("seq", "tp"),
            P("seq"),
            P("seq"),
            P("tp", None),
            P(),
            P(None, "tp"),
            P(None, "tp"),
            P(None, "tp"),
            P("tp"),
            P("tp", None),
        ),
        out_specs=P(("seq", "tp"), None),
        check_vma=False,
    )
```

```python
import functools

import jax
import jax.numpy as jnp
from jax import lax
from jax.experimental import pallas as pl
from jax.experimental.pallas import tpu as pltpu
from jax.sharding import PartitionSpec as P

BRANCHES = 5
HEAD_DIM = 48
SLOT = 64
LANES = 128
IDS = 16
CLASSES = 2 ** (BRANCHES - 1)
NEG = -1e30
EPS = 1e-05
BF16 = jnp.bfloat16
F32 = jnp.float32
VMEM_BYTES = 16 * 1024 * 1024
LARGE_VMEM_BYTES = 48 * 1024 * 1024
ALL_VMEM_BYTES = 56 * 1024 * 1024


def up_to(count, step):
    return (count + step - 1) // step * step


def iota(shape, dim):
    return lax.broadcasted_iota(jnp.int32, shape, dim)


def dot(left, right):
    return jnp.dot(left, right, preferred_element_type=F32)


def dot_nt(left, right):
    return lax.dot_general(left, right, (((1,), (1,)), ((), ())), preferred_element_type=F32)


def dot_tn(left, right):
    return lax.dot_general(left, right, (((0,), (0,)), ((), ())), preferred_element_type=F32)


def one_hot(mask):
    return jnp.where(mask, 1.0, 0.0).astype(BF16)


def stored_at(position, rows):
    residue = position & (CLASSES - 1)
    flipped = jnp.zeros_like(residue)
    for bit in range(BRANCHES - 1):
        flipped = flipped + (((residue >> bit) & 1) << (BRANCHES - 2 - bit))
    return flipped * (rows // CLASSES) + (position >> (BRANCHES - 1))


def head_start(level, head, column, rows):
    start = 0
    for bit in range(level):
        value = (head >> bit) & 1 if bit < 2 else (column >> (bit - 2)) & 1
        start = start + value * (rows >> (bit + 1))
    return start


def call(kernel, name, outs, args, scratch=(), cost=1, vmem_bytes=VMEM_BYTES, apart=(), out_apart=(), aliases=None):
    vmem = pl.BlockSpec(memory_space=pltpu.VMEM)
    anywhere = pl.BlockSpec(memory_space=pltpu.HBM)
    return pl.pallas_call(
        kernel,
        name=name,
        out_shape=[jax.ShapeDtypeStruct(shape, dtype) for shape, dtype in outs],
        in_specs=[anywhere if index in apart else vmem for index in range(len(args))],
        out_specs=[anywhere if index in out_apart else vmem for index in range(len(outs))],
        scratch_shapes=list(scratch),
        input_output_aliases=aliases or {},
        compiler_params=pltpu.CompilerParams(vmem_limit_bytes=vmem_bytes),
        cost_estimate=pl.CostEstimate(flops=int(cost * 1e9), bytes_accessed=0, transcendentals=0),
    )(*args)


def one_row(ref):
    return jnp.concatenate([ref[index : index + 1, :] for index in range(ref.shape[0])], axis=1)


def route_kernel(
    n_seq,
    n_tp,
    peer,
    target_hbm,
    slide_hbm,
    tiles_hbm,
    proj_hbm,
    out_weight_hbm,
    gain_hbm,
    out_hbm,
    bundle_hbm,
    rest_hbm,
    target_ref,
    slide_ref,
    tiles_ref,
    out_ref,
    bundle_ref,
    rest_ref,
    gain_ref,
    sems,
    out_sems,
):
    depth = proj_hbm.shape[0]
    width = out_weight_hbm.shape[0]
    along = width - rest_ref.shape[0]
    fetches = [
        pltpu.make_async_copy(target_hbm, target_ref, sems.at[0]),
        pltpu.make_async_copy(slide_hbm, slide_ref, sems.at[1]),
        pltpu.make_async_copy(tiles_hbm, tiles_ref, sems.at[2]),
        pltpu.make_async_copy(proj_hbm, bundle_ref.at[pl.ds(0, depth)], sems.at[3]),
        pltpu.make_async_copy(out_weight_hbm.at[pl.ds(0, along)], bundle_ref.at[pl.ds(depth, along)], sems.at[4]),
        pltpu.make_async_copy(out_weight_hbm.at[pl.ds(along, rest_ref.shape[0])], rest_ref, sems.at[5]),
        pltpu.make_async_copy(gain_hbm, gain_ref, sems.at[6]),
    ]
    for fetch in fetches:
        fetch.start()
    rows = tiles_ref.shape[0]
    share = rows // n_tp
    code_rows = up_to(n_seq * up_to(peer // n_tp, 8), LANES) // LANES
    kept = stored_at(iota((1, rows), 1), rows) - lax.axis_index("tp") * share
    held = (kept >= 0) & (kept < share) & ((kept >> 7) + code_rows == (iota((n_seq * 8, rows), 0) & 7))
    kept_lane = one_hot(iota((LANES, rows), 0) == (kept & 127))
    before = one_hot(iota((LANES, LANES), 0) <= iota((LANES, LANES), 1))
    fetches[0].wait()
    chunks = tiles_ref.shape[1] // LANES
    sub = peer // n_tp
    sub_pad = up_to(sub, 8)
    blocks = n_seq * n_tp
    place, column = lax.axis_index("seq"), lax.axis_index("tp")
    target = one_row(target_ref)
    owner = jnp.floor((target.astype(F32) + 0.5) * (1.0 / rows)).astype(jnp.int32)
    flags = jnp.where(iota((n_seq, rows), 0) == owner, 1.0, 0.0)
    parts = [flags[:, at : at + LANES] for at in range(0, rows, LANES)]
    counts = dot(jnp.concatenate(parts, axis=0).astype(BF16), before)
    ahead = jnp.zeros((n_seq, 1), F32)
    slots = []
    for index, part in enumerate(parts):
        count = counts[index * n_seq : (index + 1) * n_seq]
        slots.append(jnp.sum(part * (count + ahead), axis=0, keepdims=True))
        ahead = ahead + count[:, LANES - 1 :]
    slot = jnp.concatenate(slots, axis=1).astype(jnp.int32) - 1
    lane_of = jnp.zeros_like(slot)
    for turn in range(1, n_tp):
        lane_of = lane_of + jnp.where(slot >= turn * sub, 1, 0)
    low = slot - lane_of * sub
    target_row = (owner * n_tp + lane_of) * sub_pad + low
    chooser = one_hot(iota((blocks * sub_pad, rows), 0) == target_row)

    spot = stored_at(target - owner * rows, rows)
    high = spot >> 7
    code = ((spot & 127) + 128).astype(F32)
    for bit in range(3):
        code = code * jnp.where((high >> bit) & 1 == 1, 256.0 ** (2**bit), 1.0)
    arrival = place * sub_pad + low
    extra = n_seq * 8
    line = iota((extra, rows), 0)
    mine = (owner == (line >> 3)) & (lane_of == column) & ((arrival >> 7) == (line & 7))
    coded = dot_nt(
        jnp.where(mine, code, 0.0).astype(BF16),
        one_hot(iota((LANES, rows), 0) == (arrival & 127)),
    )
    fetches[1].wait()
    ids = dot_nt(jnp.where(held, one_row(slide_ref).astype(F32), 0.0).astype(BF16), kept_lane)
    notes = coded + ids
    for fetch in fetches[3:]:
        fetch.wait()
    gain = gain_ref[...]
    high = gain.astype(BF16).astype(F32)
    mid = (gain - high).astype(BF16).astype(F32)
    low = (gain - high) - mid
    line = iota((16, width), 0)
    parts = jnp.where(line == 0, high, jnp.where(line == 1, mid, jnp.where(line == 2, low, 0.0)))
    bundle_ref[depth + along :] = jnp.zeros((16, bundle_ref.shape[1]), BF16)
    bundle_ref[depth + along :, :width] = parts.astype(BF16)
    stores = [
        pltpu.make_async_copy(bundle_ref, bundle_hbm, sems.at[7]),
        pltpu.make_async_copy(rest_ref, rest_hbm, sems.at[8]),
    ]
    for store in stores:
        store.start()
    fetches[2].wait()
    picked = dot(chooser, tiles_ref[...])
    pad = out_hbm.shape[1] - chunks * sub_pad - 8
    for block in range(blocks):
        base = block * sub_pad
        pieces = [
            picked[base : base + sub_pad, part * LANES : (part + 1) * LANES] for part in range(chunks)
        ]
        start = block // n_tp * 8
        pieces.append(notes[start : start + 8])
        if pad:
            pieces.append(jnp.zeros((pad, LANES), F32))
        out_ref[block] = jnp.concatenate(pieces, axis=0).astype(BF16)
        if block % n_tp == n_tp - 1:
            some = pl.ds(block - n_tp + 1, n_tp)
            stores.append(pltpu.make_async_copy(out_ref.at[some], out_hbm.at[some], out_sems.at[block // n_tp]))
            stores[-1].start()
    for store in stores:
        store.wait()


def spread_mask(width, wide, shift):
    row = iota((width, wide), 0) - shift
    lane = iota((width, wide), 1)
    inner = lane & (SLOT - 1)
    return (inner < HEAD_DIM) & (row == (lane >> 6) * HEAD_DIM + inner)


def project_kernel(n_seq, n_tp, peer, recv_hbm, *refs):
    total_ref, later_ref, codes_ref, ids_ref, recv_ref, work, sems = refs[n_tp - 2 :]
    weight_refs = refs[: n_tp - 2]
    fetches = []
    for source in range(n_seq):
        some = pl.ds(source * n_tp, n_tp)
        fetches.append(pltpu.make_async_copy(recv_hbm.at[some], recv_ref.at[some], sems.at[source]))
        fetches[-1].start()
    sub_pad = up_to(peer // n_tp, 8)
    chunks = work.shape[2] // LANES
    column = lax.axis_index("tp")
    code_rows = codes_ref.shape[2] // LANES
    share = ids_ref.shape[1] // n_tp
    at = chunks * sub_pad
    even = at // 16 * 16
    notes = [jnp.zeros((8, LANES), F32)] * n_tp
    for source in range(n_seq):
        fetches[source].wait()
        for turn in range(n_tp):
            block = recv_ref[source * n_tp + (column ^ turn)].astype(F32)
            for part in range(chunks):
                work[turn, source * sub_pad : (source + 1) * sub_pad, part * LANES : (part + 1) * LANES] = block[
                    part * sub_pad : (part + 1) * sub_pad
                ]
            notes[turn] = notes[turn] + block[at : at + 8]
        pieces = []
        for other in range(n_tp):
            note = recv_ref[source * n_tp + other, even : even + 16, :].astype(F32)[at - even :]
            for piece in range(up_to(share, LANES) // LANES):
                length = min(LANES, share - piece * LANES)
                pieces.append(note[code_rows + piece : code_rows + piece + 1, :length])
        ids_ref[source : source + 1, :] = jnp.concatenate(pieces, axis=1)
    total = None
    for turn in range(1, n_tp - 1):
        part_sum = dot(work[turn].astype(BF16), weight_refs[turn - 1][: work.shape[2]])
        total = part_sum if total is None else total + part_sum
    total_ref[...] = total
    later_ref[0] = work[0].astype(BF16)
    later_ref[1] = work[n_tp - 1].astype(BF16)
    for turn in range(n_tp):
        codes = notes[turn]
        power = jnp.zeros((8, LANES), F32)
        scale = jnp.ones((8, LANES), F32)
        for step in range(1, 8):
            above = codes >= 128.0 * 256.0**step
            power = power + jnp.where(above, 128.0, 0.0)
            scale = scale * jnp.where(above, 1.0 / 256.0, 1.0)
        spots = jnp.where(codes > 0.0, codes * scale - 128.0 + power, -1.0)
        for piece in range(code_rows):
            codes_ref[turn, :, piece * LANES : (piece + 1) * LANES] = spots[piece : piece + 1].astype(jnp.int32)


def stream_kernel(total_ref, later_ref, first_ref, last_ref, stream_ref):
    total = total_ref[...] + dot(later_ref[0], first_ref[...])
    stream_ref[...] = (total + dot(later_ref[1], last_ref[: later_ref.shape[2]])).astype(BF16)


def key_value_query(stream, gain, weights):
    rows = stream.astype(F32)
    mean = jnp.mean(rows, axis=-1, keepdims=True)
    second = jnp.mean(rows * rows, axis=-1, keepdims=True)
    normed = ((rows - mean) * lax.rsqrt(second - mean * mean + EPS) * gain).astype(BF16)
    result = dot_nt(normed, weights)
    third = weights.shape[0] // 3
    scale = jnp.where(iota((1, 3 * third), 1) >= 2 * third, HEAD_DIM ** (-0.5), 1.0)
    return (result * scale).astype(BF16)


def place_heads(turn, codes_ref, gain_ref, key_ref, value_ref, query_ref, stream_ref, rows):
    weights = jnp.concatenate([key_ref[...], value_ref[...], query_ref[...]], axis=0)
    result = key_value_query(stream_ref[...], one_row(gain_ref), weights)
    spots = codes_ref[turn]
    place = one_hot(iota((rows, spots.shape[1]), 0) == spots)[:, : result.shape[0]]
    return dot(place, result)


def first_heads_kernel(
    groups,
    codes_ref,
    gain_ref,
    key_ref,
    value_ref,
    query_ref,
    stream_ref,
    ids_ref,
    *refs,
):
    n_tp = codes_ref.shape[0]
    bundle_refs, rest_refs, refs = refs[:n_tp], refs[n_tp : 2 * n_tp], refs[2 * n_tp :]
    out_ref, same_ref, apart_ref, back_ref, weights_ref, gains_ref, spreads_ref = refs[:7]
    refs = refs[7:]
    rows, wide = same_ref.shape
    heads = wide // SLOT
    width = heads * HEAD_DIM
    place, column = lax.axis_index("seq"), lax.axis_index("tp")
    first = place_heads(0, codes_ref, gain_ref, key_ref, value_ref, query_ref, stream_ref, rows)
    out_ref[...] = first.astype(BF16)
    for shift in range(2):
        spreads_ref[shift] = one_hot(spread_mask(2 * width, wide, shift * width))

    ids = ids_ref[pl.ds(place, 1), :].astype(jnp.int32)
    same_ref[...] = id_lanes(ids, wide, None).astype(BF16)
    apart_ref[...] = id_lanes(ids, wide, NEG).astype(BF16)
    share = back_ref.shape[1]
    for turn in range(back_ref.shape[0]):
        wanted = stored_at((column ^ turn) * share + iota((share, 1), 0), rows)
        back_ref[turn] = one_hot(wanted == iota((share, rows), 1))
    spread = one_hot(spread_mask(width, wide, 0))
    gap = jnp.zeros((SLOT - HEAD_DIM, weights_ref.shape[2]), BF16)
    for turn, (ref, rest_ref) in enumerate(zip(bundle_refs, rest_refs)):
        along = width - rest_ref.shape[0]
        depth = ref.shape[0] - 16 - along
        gains_ref[turn] = dot(ref[depth + along :, :width], spread).astype(BF16)
        for head in range(heads):
            at, to = head * HEAD_DIM, head * SLOT
            early = min(max(along - at, 0), HEAD_DIM)
            if early:
                weights_ref[turn, to : to + early, :] = ref[depth + at : depth + at + early, :]
            if early < HEAD_DIM:
                weights_ref[turn, to + early : to + HEAD_DIM, :] = rest_ref[
                    at + early - along : at + HEAD_DIM - along, :
                ]
            weights_ref[turn, to + HEAD_DIM : to + SLOT, :] = gap
    apart_refs, apart_all = refs[:-1], refs[-1]
    for ref, (level, masks) in zip(apart_refs, groups):
        count = rows >> level
        slots = iota((count, wide), 1) >> 6
        for index, mask in enumerate(masks):
            far = ids_ref[pl.ds(place ^ mask, 1), :].astype(jnp.int32)
            apart_all[...] = id_lanes(far, wide, NEG).astype(BF16)
            chosen = None
            for head in range(heads):
                part = apart_all[pl.ds(head_start(level, head, column, rows), count), :]
                chosen = part if chosen is None else jnp.where(slots >= head, part, chosen)
            ref[index * count : (index + 1) * count, :] = chosen


def more_heads_kernel(
    turn, codes_ref, gain_ref, key_ref, value_ref, query_ref, stream_ref, before_ref, out_ref
):
    more = place_heads(turn, codes_ref, gain_ref, key_ref, value_ref, query_ref, stream_ref, out_ref.shape[0])
    out_ref[...] = (before_ref[...].astype(F32) + more).astype(BF16)


def last_heads_kernel(
    turn, levels, codes_ref, gain_ref, key_ref, value_ref, query_ref, stream_ref, before_ref, packed, *sets
):
    rows = packed.shape[0]
    width = key_ref.shape[0]
    heads = width // HEAD_DIM
    column = lax.axis_index("tp")
    more_heads_kernel(
        turn, codes_ref, gain_ref, key_ref, value_ref, query_ref, stream_ref, before_ref, packed
    )
    for ref, level in zip(sets, levels):
        count = rows >> level
        lane = iota((count, 2 * width), 1)
        lane = jnp.where(lane >= width, lane - width, lane)
        chosen = None
        for head in range(heads):
            part = packed[pl.ds(head_start(level, head, column, rows), count), : 2 * width]
            chosen = part if chosen is None else jnp.where(lane >= head * HEAD_DIM, part, chosen)
        ref[...] = chosen


def id_lanes(ids, wide, apart):
    count = ids.shape[1]
    lane = iota((IDS, wide), 1) & (SLOT - 1)
    group = iota((IDS, wide), 0)
    same = lane - HEAD_DIM == group
    if apart is None:
        table = jnp.where(same, 1.0, 0.0)
    else:
        table = jnp.where((lane >= HEAD_DIM) & ~same, apart, 0.0)
    return dot_tn(one_hot(iota((IDS, count), 0) == ids), table.astype(BF16))


def agreement(level, group, column, rows, total, count):
    q_on, k_on = [], []
    for index, (head, first) in enumerate(group):
        for size, on in ((count, q_on), (total, k_on)):
            line, at = iota((8, size), 0), iota((8, size), 1)
            for step in range(1, size // count):
                at = at - jnp.where(iota((8, size), 1) >= step * count, count, 0)
            start = jnp.zeros((8, size), jnp.int32)
            length = jnp.zeros((8, size), jnp.int32)
            for branch in range(level, BRANCHES):
                start = jnp.where(line == branch, head_start(branch, head, column, rows) - first, start)
                length = jnp.where(line == branch, rows >> branch, length)
            on.append(jnp.where((at >= start) & (at < start + length), 1.0, 0.0))
        blank = jnp.zeros((8, count), F32)
        q_on[index] = jnp.concatenate([q_on[index] if place == index else blank for place in range(len(group))], axis=1)
    return jnp.concatenate(q_on, axis=0).astype(BF16), jnp.concatenate(k_on, axis=0).astype(BF16)


def repeat(block, times):
    return jnp.concatenate([block] * times, axis=1)


def own_kernel(packed_ref, same_ref, apart_ref, spreads_ref, acc_ref, tops_ref, masked_ref, keys_ref, values_ref):
    rows, wide = masked_ref.shape
    heads = wide // SLOT
    width = heads * HEAD_DIM
    column = lax.axis_index("tp")
    pairs = packed_ref[:, : 2 * width]
    query = dot(packed_ref[:, 2 * width :], spreads_ref[0, :width])
    masked_ref[...] = (query + same_ref[...].astype(F32)).astype(BF16)
    key = dot(pairs, spreads_ref[0])
    keys_ref[...] = (key + apart_ref[...].astype(F32)).astype(BF16)
    ones = jnp.where((iota((rows, wide), 1) & (SLOT - 1)) >= HEAD_DIM, 1.0, 0.0)
    value = dot(pairs, spreads_ref[1])
    values_ref[...] = (value + ones).astype(BF16)
    half = rows // 2
    slot_of = iota((half, wide), 1) >> 6
    for part in range(2):
        start = part * half
        query = masked_ref[start : start + half, :]
        acc = None
        for head in range(heads):
            one = jnp.where(slot_of == head, query, jnp.zeros((), BF16))
            scores = dot_nt(one, keys_ref[...])
            top = jnp.max(scores, axis=1, keepdims=True)
            tops_ref[head, start : start + half, :] = jnp.broadcast_to(top, (half, LANES))
            weights = jnp.exp(scores - top)
            if part == (head & 1):
                times = dot_tn(*agreement(0, [(head, start)], column, rows, half, half))
                scaled = weights[:, start : start + half] * times
                others = weights[:, half - start : rows - start]
                weights = jnp.concatenate([scaled, others] if part == 0 else [others, scaled], axis=1)
            got = dot(weights.astype(BF16), values_ref[...])
            acc = got if acc is None else jnp.where(slot_of == head, got, acc)
        acc_ref[start : start + half, :] = acc


def weigh_inner(weights, group, column, rows):
    count = rows >> 1
    length = rows >> 2
    head = group[0][0]
    start = head_start(2, head, column, rows) - head_start(1, head, column, rows)
    low, high = start // LANES * LANES, up_to(start + length, LANES)
    q_on, k_on = agreement(1, group, column, rows, count, count)
    part = weights[start : start + length]
    part = [part[:, :low], part[:, low:high] * dot_tn(q_on[:, start : start + length], k_on[:, low:high]), part[:, high:]]
    part = jnp.concatenate([one for one in part if one.shape[1]], axis=1)
    return jnp.concatenate([part, weights[length:]] if start == 0 else [weights[:start], part], axis=0)


def merge_sets(level, masks, sets, acc_ref, tops_ref, query_ref, spreads_ref, apart_ref):
    rows, wide = query_ref.shape
    column = lax.axis_index("tp")
    count = rows >> level
    some = min(max(1, rows // count), len(masks))
    total = some * count
    slot_of = iota((count, wide), 1) >> 6
    ones = jnp.where((iota((total, wide), 1) & (SLOT - 1)) >= HEAD_DIM, 1.0, 0.0)
    chunks = []
    for begin in range(0, len(masks), some):
        pairs = jnp.concatenate([ref[...] for ref in sets[begin : begin + some]], axis=0)
        keys = dot(pairs, spreads_ref[0]) + apart_ref[begin * count : begin * count + total, :].astype(F32)
        values = dot(pairs, spreads_ref[1]) + ones
        chunks.append((keys.astype(BF16), values.astype(BF16)))
    heads = wide // SLOT
    together = heads if heads * count * total <= 2**19 else 1
    states = []
    for low in range(0, heads, together):
        group = [(head, head_start(level, head, column, rows)) for head in range(low, low + together)]
        heres = [(head, pl.ds(first, count)) for head, first in group]
        query = [jnp.where(slot_of == head, query_ref[here, :], jnp.zeros((), BF16)) for head, here in heres]
        sums = [acc_ref[here, :] for _, here in heres]
        tops = [tops_ref[head, here, :] for head, here in heres]
        states.append((group, heres) + tuple(jnp.concatenate(parts, axis=0) for parts in (query, sums, tops)))
    merged = []
    for group, heres, query, sums, tops in states:
        inner = level == 1 and total == count and together == 1
        if not inner:
            times = dot_tn(*agreement(level, group, column, rows, total, count))
        for keys, values in chunks:
            scores = dot_nt(query, keys)
            top = jnp.maximum(tops, jnp.max(scores, axis=1, keepdims=True))
            weights = jnp.exp(scores - repeat(top, total // LANES))
            weights = weigh_inner(weights, group, column, rows) if inner else weights * times
            got = dot(weights.astype(BF16), values)
            sums = sums * repeat(jnp.exp(tops - top), wide // LANES) + got
            tops = top
        for index, (head, here) in enumerate(heres):
            part = slice(index * count, (index + 1) * count)
            merged.append((head, here, sums[part], tops[part]))
    return merged


def slot_lane(values, inner):
    wide = values.shape[1]
    row, lane = iota((wide, wide), 0), iota((wide, wide), 1)
    pick = one_hot(row == (lane >> 6) * SLOT + inner)
    high = values.astype(BF16)
    low = (values - high.astype(F32)).astype(BF16)
    return dot(high, pick) + dot(low, pick)


def near_kernel(groups, acc_ref, tops_ref, query_ref, spreads_ref, *refs):
    apart_refs, refs = refs[: len(groups)], refs[len(groups) :]
    sums_ref, new_tops_ref = refs[-2:]
    wide = query_ref.shape[1]
    del acc_ref, tops_ref

    for apart_ref, (level, masks) in zip(apart_refs, groups):
        merged = merge_sets(
            level, masks, refs[: len(masks)], sums_ref, new_tops_ref, query_ref, spreads_ref, apart_ref
        )
        refs = refs[len(masks) :]
        for head, here, sums, tops in merged:
            slot_of = iota(sums.shape, 1) >> 6
            sums_ref[here, :] = jnp.where(slot_of == head, sums, sums_ref[here, :])
            new_tops_ref[head, here, :] = tops


def mid_kernel(groups, acc_ref, tops_ref, query_ref, spreads_ref, *refs):
    sums_ref, _, early_ref, centre_ref = refs[-4:]
    near_kernel(groups, acc_ref, tops_ref, query_ref, spreads_ref, *refs[:-2])
    rows, wide = query_ref.shape
    heads = wide // SLOT
    every = sums_ref[...]
    inner = iota((rows, wide), 1) & (SLOT - 1)
    attn = jnp.where(inner < HEAD_DIM, every / slot_lane(every, HEAD_DIM), 0.0)
    average = jnp.full((wide, wide), 1.0, BF16)
    centre = (dot(attn.astype(BF16), average) * (1.0 / (heads * HEAD_DIM))).astype(BF16).astype(F32)
    centre_ref[...] = centre
    early_ref[...] = jnp.where(inner < HEAD_DIM, attn - centre, centre).astype(BF16)


def far_kernel(n_tp, level, masks, acc_ref, tops_ref, query_ref, spreads_ref, early_ref, centre_ref, back_ref, *refs):
    apart_ref, refs = refs[0], refs[1:]
    sets, refs = refs[: len(masks)], refs[len(masks) :]
    out_refs, message = refs[:n_tp], refs[-1]
    message[...] = early_ref[...]

    merged = merge_sets(level, masks, sets, acc_ref, tops_ref, query_ref, spreads_ref, apart_ref)
    for head, here, sums, _ in merged:
        lane = iota(sums.shape, 1)
        mine = (lane >= head * SLOT) & (lane < head * SLOT + HEAD_DIM)
        new = (sums / slot_lane(sums, HEAD_DIM) - centre_ref[here, :]).astype(BF16)
        message[here, :] = jnp.where(mine, new, message[here, :])
    final = message[...]
    for turn in range(n_tp):
        out_refs[turn][...] = dot(back_ref[turn], final).astype(BF16)


def base_kernel(n_tp, codes_ref, *refs):
    shards, base_ref = refs[:n_tp], refs[n_tp]
    share = base_ref.shape[0]
    wanted = stored_at(lax.axis_index("tp") * share + iota((share, 1), 0), share * n_tp)
    base = None
    for turn in range(n_tp):
        spots = codes_ref[turn]
        moved = dot(one_hot(wanted == spots)[:, : shards[turn].shape[0]], shards[turn][...])
        base = moved if base is None else base + moved
    base_ref[...] = base.astype(BF16)


def mix_kernel(n_tp, base_ref, weights_ref, gains_ref, *refs):
    message_refs, out_ref = refs[:n_tp], refs[-1]
    share, wide = base_ref.shape[0], weights_ref.shape[1]
    features = n_tp * (wide // SLOT) * HEAD_DIM
    inside = (iota((share, wide), 1) & (SLOT - 1)) < HEAD_DIM
    parts, centres, gains = [], [], []
    for turn, ref in enumerate(message_refs):
        message = ref[...].astype(F32)
        extra = gains_ref[turn].astype(F32)
        parts.append(jnp.where(inside, message, 0.0))
        centres.append(message[:, HEAD_DIM : HEAD_DIM + 1])
        gains.append(extra[0:1] + extra[1:2] + extra[2:3])
    each = features // n_tp
    sums = [jnp.sum(part, axis=1, keepdims=True) + centre * each for part, centre in zip(parts, centres)]
    mean = sum(sums) * (1.0 / features)
    parts = [jnp.where(inside, part + (centre - mean), 0.0) for part, centre in zip(parts, centres)]
    spread = jnp.sum(sum(part * part for part in parts), axis=1, keepdims=True) * (1.0 / features)
    factor = lax.rsqrt(spread + EPS)
    total = base_ref[...].astype(F32)
    for turn, (part, gain) in enumerate(zip(parts, gains)):
        total = total + dot((part * factor * gain).astype(BF16), weights_ref[turn])
    out_ref[...] = total.astype(BF16)


def swap(block, axis, mask):
    count = lax.axis_size(axis)
    return lax.ppermute(block, axis, [(index, index ^ mask) for index in range(count)])


def gather_tp(block):
    across = swap(block, "tp", 2)
    return [block, swap(block, "tp", 1), across, swap(across, "tp", 1)]


def body(
    tiles,
    tile_target,
    slide_id,
    proj_weight,
    norm_gain,
    query_weight,
    key_weight,
    value_weight,
    sub_gain,
    out_weight,
):
    n_seq = lax.axis_size("seq")
    n_tp = lax.axis_size("tp")
    rows, tile_width = tiles.shape
    features = proj_weight.shape[1]
    width = query_weight.shape[1]
    heads = width // HEAD_DIM
    wide = heads * SLOT
    share = rows // n_tp
    peer = rows // n_seq
    sub_pad = up_to(peer // n_tp, 8)
    arriving = n_seq * sub_pad
    chunks = tile_width // LANES
    block_rows = up_to(chunks * sub_pad + 8, 16)

    first_group = max(1, n_seq // 16)
    sizes = [min(first_group * 2**branch, n_seq) for branch in range(BRANCHES)]
    groups = []
    for level in range(BRANCHES):
        masks = tuple(range(1 if level == 0 else sizes[level - 1], sizes[level]))
        if masks:
            groups.append((level, masks))

    vmem_bytes = VMEM_BYTES if n_seq <= 8 else LARGE_VMEM_BYTES
    blocks, bundle, rest = call(
        functools.partial(route_kernel, n_seq, n_tp, peer),
        "route",
        [((n_seq * n_tp, block_rows, LANES), BF16), ((tile_width + width // 3 + 16, features), BF16)]
        + [((width - width // 3, features), BF16)],
        [tile_target.reshape(-1, LANES), slide_id.reshape(-1, LANES), tiles]
        + [proj_weight, out_weight, sub_gain.reshape(1, width)],
        scratch=[
            pltpu.VMEM((rows // LANES, LANES), jnp.int32),
            pltpu.VMEM((rows // LANES, LANES), jnp.int32),
            pltpu.VMEM(tiles.shape, BF16),
            pltpu.VMEM((n_seq * n_tp, block_rows, LANES), BF16),
            pltpu.VMEM((tile_width + width // 3 + 16, features), BF16),
            pltpu.VMEM((width - width // 3, features), BF16),
            pltpu.VMEM((1, width), F32),
            pltpu.SemaphoreType.DMA((9,)),
            pltpu.SemaphoreType.DMA((n_seq,)),
        ],
        cost=3,
        vmem_bytes=ALL_VMEM_BYTES,
        apart=(0, 1, 2, 3, 4, 5),
        out_apart=(0, 1, 2),
    )
    received = lax.all_to_all(blocks, ("seq", "tp"), split_axis=0, concat_axis=0, tiled=True)
    bundles, rests = gather_tp(bundle), gather_tp(rest)

    total, later, codes, ids = call(
        functools.partial(project_kernel, n_seq, n_tp, peer),
        "project",
        [((arriving, features), F32), ((2, arriving, tile_width), BF16)]
        + [((n_tp, 1, up_to(arriving, LANES)), jnp.int32), ((n_seq, rows), F32)],
        [received] + bundles[1:-1],
        scratch=[
            pltpu.VMEM(received.shape, BF16),
            pltpu.VMEM((n_tp, arriving, tile_width), F32),
            pltpu.SemaphoreType.DMA((n_seq,)),
        ],
        vmem_bytes=vmem_bytes,
        apart=(0,),
    )
    (stream,) = call(
        stream_kernel,
        "stream",
        [((arriving, features), BF16)],
        [total, later, proj_weight, bundles[-1]],
        vmem_bytes=vmem_bytes,
    )
    shards = gather_tp(stream)

    gain = norm_gain.reshape(-1, LANES)
    weights = [gain, key_weight.T, value_weight.T, query_weight.T]
    partial, same, apart, back, padded, gains, spreads, *far_apart = call(
        functools.partial(first_heads_kernel, groups),
        "heads_1",
        [
            ((rows, 3 * width), BF16),
            ((rows, wide), BF16),
            ((rows, wide), BF16),
            ((n_tp, share, rows), BF16),
            ((n_tp, wide, features), BF16),
            ((n_tp, 16, wide), BF16),
            ((2, 2 * width, wide), BF16),
        ]
        + [(((rows >> level) * len(masks), wide), BF16) for level, masks in groups],
        [codes] + weights + [shards[0], ids] + bundles + rests,
        scratch=[pltpu.VMEM((rows, wide), BF16)],
        vmem_bytes=vmem_bytes,
    )
    for turn in range(1, n_tp - 1):
        (partial,) = call(
            functools.partial(more_heads_kernel, turn),
            "heads_2",
            [((rows, 3 * width), BF16)],
            [codes] + weights + [shards[turn], partial],
            cost=10 if turn == n_tp - 2 else 1,
            vmem_bytes=vmem_bytes,
        )
    packed, *sets = call(
        functools.partial(last_heads_kernel, n_tp - 1, [level for level, _ in groups]),
        "heads_3",
        [((rows, 3 * width), BF16)] + [((rows >> level, 2 * width), BF16) for level, _ in groups],
        [codes] + weights + [shards[n_tp - 1], partial],
        vmem_bytes=vmem_bytes,
    )
    sent = [[swap(one, "seq", mask) for mask in masks] for one, (_, masks) in zip(sets[:-1], groups)]
    direct = {mask: swap(sets[-1], "seq", mask) for mask in groups[-1][1] if mask % 2 == 0}
    sent.append([swap(direct[mask - 1], "seq", 1) if mask % 2 else direct[mask] for mask in groups[-1][1]])

    acc, tops, masked = call(
        own_kernel,
        "own",
        [((rows, wide), F32), ((heads, rows, LANES), F32), ((rows, wide), BF16)],
        [packed, same, apart, spreads],
        scratch=[pltpu.VMEM((rows, wide), BF16)] * 2,
        cost=0.1,
        vmem_bytes=vmem_bytes,
    )
    for index in range(len(groups) - 1):
        final = index == len(groups) - 2
        acc, tops, *rest_of = call(
            functools.partial(mid_kernel if final else near_kernel, [groups[index]]),
            "mid" if final else "near",
            [((rows, wide), F32), ((heads, rows, LANES), F32)]
            + ([((rows, wide), BF16), ((rows, wide), F32)] if final else []),
            [acc, tops, masked, spreads, far_apart[index]] + sent[index],
            aliases={0: 0, 1: 1},
            cost=6,
            vmem_bytes=vmem_bytes,
        )
    early, centre = rest_of
    messages = call(
        functools.partial(far_kernel, n_tp, *groups[-1]),
        "far",
        [((share, wide), BF16)] * n_tp,
        [acc, tops, masked, spreads, early, centre, back, far_apart[-1]] + sent[-1],
        scratch=[pltpu.VMEM((rows, wide), BF16)],
        vmem_bytes=vmem_bytes,
    )
    arrived = [messages[0]] + [swap(messages[turn], "tp", turn) for turn in range(1, n_tp)]
    (base,) = call(
        functools.partial(base_kernel, n_tp),
        "base",
        [((share, features), BF16)],
        [codes] + shards,
        vmem_bytes=vmem_bytes,
    )
    (result,) = call(
        functools.partial(mix_kernel, n_tp),
        "mix",
        [((share, features), BF16)],
        [base, padded, gains] + arrived,
    )
    return result


def solution(mesh):
    return jax.shard_map(
        body,
        mesh=mesh,
        in_specs=(
            P("seq", "tp"),
            P("seq"),
            P("seq"),
            P("tp", None),
            P(),
            P(None, "tp"),
            P(None, "tp"),
            P(None, "tp"),
            P("tp"),
            P("tp", None),
        ),
        out_specs=P(("seq", "tp"), None),
        check_vma=False,
    )
```

```python
import functools

import jax
import jax.numpy as jnp
from jax import lax
from jax.experimental import pallas as pl
from jax.experimental.pallas import tpu as pltpu
from jax.sharding import PartitionSpec as P

BRANCHES = 5
HEAD_DIM = 48
SLOT = 64
LANES = 128
IDS = 16
CLASSES = 2 ** (BRANCHES - 1)
NEG = -1e30
EPS = 1e-05
BF16 = jnp.bfloat16
F32 = jnp.float32
HINT_COST = 1
VMEM_BYTES = 16 * 1024 * 1024
LARGE_VMEM_BYTES = 48 * 1024 * 1024
ALL_VMEM_BYTES = 56 * 1024 * 1024


def up_to(count, step):
    return (count + step - 1) // step * step


def iota(shape, dim):
    return lax.broadcasted_iota(jnp.int32, shape, dim)


def dot(left, right):
    return jnp.dot(left, right, preferred_element_type=F32)


def dot_nt(left, right):
    return lax.dot_general(left, right, (((1,), (1,)), ((), ())), preferred_element_type=F32)


def dot_tn(left, right):
    return lax.dot_general(left, right, (((0,), (0,)), ((), ())), preferred_element_type=F32)


def one_hot(mask):
    return jnp.where(mask, 1.0, 0.0).astype(BF16)


def stored_at(position, rows):
    residue = position & (CLASSES - 1)
    flipped = jnp.zeros_like(residue)
    for bit in range(BRANCHES - 1):
        flipped = flipped + (((residue >> bit) & 1) << (BRANCHES - 2 - bit))
    return flipped * (rows // CLASSES) + (position >> (BRANCHES - 1))


def head_start(level, head, column, rows):
    start = 0
    for bit in range(level):
        value = (head >> bit) & 1 if bit < 2 else (column >> (bit - 2)) & 1
        start = start + value * (rows >> (bit + 1))
    return start


def call(kernel, name, outs, args, scratch=(), cost=1, vmem_bytes=VMEM_BYTES, apart=(), out_apart=(), aliases=None):
    vmem = pl.BlockSpec(memory_space=pltpu.VMEM)
    anywhere = pl.BlockSpec(memory_space=pltpu.HBM)
    return pl.pallas_call(
        kernel,
        name=name,
        out_shape=[jax.ShapeDtypeStruct(shape, dtype) for shape, dtype in outs],
        in_specs=[anywhere if index in apart else vmem for index in range(len(args))],
        out_specs=[anywhere if index in out_apart else vmem for index in range(len(outs))],
        scratch_shapes=list(scratch),
        input_output_aliases=aliases or {},
        compiler_params=pltpu.CompilerParams(vmem_limit_bytes=vmem_bytes),
        cost_estimate=pl.CostEstimate(flops=int(cost * 1e9), bytes_accessed=0, transcendentals=0),
    )(*args)


def one_row(ref):
    return jnp.concatenate([ref[index : index + 1, :] for index in range(ref.shape[0])], axis=1)


def route_kernel(
    n_seq,
    n_tp,
    peer,
    target_hbm,
    slide_hbm,
    tiles_hbm,
    out_hbm,
    target_ref,
    slide_ref,
    tiles_ref,
    out_ref,
    sems,
    out_sems,
):
    fetches = [
        pltpu.make_async_copy(target_hbm, target_ref, sems.at[0]),
        pltpu.make_async_copy(slide_hbm, slide_ref, sems.at[1]),
        pltpu.make_async_copy(tiles_hbm, tiles_ref, sems.at[2]),
    ]
    for fetch in fetches:
        fetch.start()
    rows = tiles_ref.shape[0]
    share = rows // n_tp
    code_rows = up_to(n_seq * up_to(peer // n_tp, 8), LANES) // LANES
    kept = stored_at(iota((1, rows), 1), rows) - lax.axis_index("tp") * share
    held = (kept >= 0) & (kept < share) & ((kept >> 7) + code_rows == (iota((n_seq * 8, rows), 0) & 7))
    kept_lane = one_hot(iota((LANES, rows), 0) == (kept & 127))
    before = one_hot(iota((LANES, LANES), 0) <= iota((LANES, LANES), 1))
    fetches[0].wait()
    chunks = tiles_ref.shape[1] // LANES
    sub = peer // n_tp
    sub_pad = up_to(sub, 8)
    blocks = n_seq * n_tp
    place, column = lax.axis_index("seq"), lax.axis_index("tp")
    target = one_row(target_ref)
    owner = jnp.floor((target.astype(F32) + 0.5) * (1.0 / rows)).astype(jnp.int32)
    flags = jnp.where(iota((n_seq, rows), 0) == owner, 1.0, 0.0)
    parts = [flags[:, at : at + LANES] for at in range(0, rows, LANES)]
    counts = dot(jnp.concatenate(parts, axis=0).astype(BF16), before)
    ahead = jnp.zeros((n_seq, 1), F32)
    slots = []
    for index, part in enumerate(parts):
        count = counts[index * n_seq : (index + 1) * n_seq]
        slots.append(jnp.sum(part * (count + ahead), axis=0, keepdims=True))
        ahead = ahead + count[:, LANES - 1 :]
    slot = jnp.concatenate(slots, axis=1).astype(jnp.int32) - 1
    lane_of = jnp.zeros_like(slot)
    for turn in range(1, n_tp):
        lane_of = lane_of + jnp.where(slot >= turn * sub, 1, 0)
    low = slot - lane_of * sub
    target_row = (owner * n_tp + lane_of) * sub_pad + low
    chooser = one_hot(iota((blocks * sub_pad, rows), 0) == target_row)

    spot = stored_at(target - owner * rows, rows)
    high = spot >> 7
    code = ((spot & 127) + 128).astype(F32)
    for bit in range(3):
        code = code * jnp.where((high >> bit) & 1 == 1, 256.0 ** (2**bit), 1.0)
    arrival = place * sub_pad + low
    extra = n_seq * 8
    line = iota((extra, rows), 0)
    mine = (owner == (line >> 3)) & (lane_of == column) & ((arrival >> 7) == (line & 7))
    coded = dot_nt(
        jnp.where(mine, code, 0.0).astype(BF16),
        one_hot(iota((LANES, rows), 0) == (arrival & 127)),
    )
    fetches[1].wait()
    ids = dot_nt(jnp.where(held, one_row(slide_ref).astype(F32), 0.0).astype(BF16), kept_lane)
    notes = coded + ids
    stores = []
    fetches[2].wait()
    picked = dot(chooser, tiles_ref[...])
    pad = out_hbm.shape[1] - chunks * sub_pad - 8
    for block in range(blocks):
        base = block * sub_pad
        pieces = [
            picked[base : base + sub_pad, part * LANES : (part + 1) * LANES] for part in range(chunks)
        ]
        start = block // n_tp * 8
        pieces.append(notes[start : start + 8])
        if pad:
            pieces.append(jnp.zeros((pad, LANES), F32))
        out_ref[block] = jnp.concatenate(pieces, axis=0).astype(BF16)
        if block % n_tp == n_tp - 1:
            some = pl.ds(block - n_tp + 1, n_tp)
            stores.append(pltpu.make_async_copy(out_ref.at[some], out_hbm.at[some], out_sems.at[block // n_tp]))
            stores[-1].start()
    for store in stores:
        store.wait()


def spread_mask(width, wide, shift):
    row = iota((width, wide), 0) - shift
    lane = iota((width, wide), 1)
    inner = lane & (SLOT - 1)
    return (inner < HEAD_DIM) & (row == (lane >> 6) * HEAD_DIM + inner)


def hint_kernel(weight_ref, out_ref):
    out_ref[...] = weight_ref[: out_ref.shape[0], : out_ref.shape[1]]


def scale_kernel(gain_ref, weight_ref, scaled_ref):
    width = weight_ref.shape[0]
    same = iota((width, width), 0) == iota((width, width), 1)
    gain = jnp.sum(jnp.where(same, gain_ref[...], 0.0), axis=1, keepdims=True)
    scaled_ref[...] = (weight_ref[...].astype(F32) * gain).astype(BF16)


def project_kernel(n_seq, n_tp, peer, recv_hbm, early_ref, beside_ref, *refs):
    del early_ref, beside_ref
    weight_refs = refs[: n_tp - 1]
    total_ref, later_ref, codes_ref, ids_ref, recv_ref, work, sems = refs[n_tp - 1 :]
    fetches = []
    for source in range(n_seq):
        some = pl.ds(source * n_tp, n_tp)
        fetches.append(pltpu.make_async_copy(recv_hbm.at[some], recv_ref.at[some], sems.at[source]))
        fetches[-1].start()
    sub_pad = up_to(peer // n_tp, 8)
    chunks = work.shape[2] // LANES
    column = lax.axis_index("tp")
    code_rows = codes_ref.shape[2] // LANES
    share = ids_ref.shape[1] // n_tp
    at = chunks * sub_pad
    even = at // 16 * 16
    notes = [jnp.zeros((8, LANES), F32)] * n_tp
    for source in range(n_seq):
        fetches[source].wait()
        for turn in range(n_tp):
            block = recv_ref[source * n_tp + (column ^ turn)].astype(F32)
            for part in range(chunks):
                work[turn, source * sub_pad : (source + 1) * sub_pad, part * LANES : (part + 1) * LANES] = block[
                    part * sub_pad : (part + 1) * sub_pad
                ]
            notes[turn] = notes[turn] + block[at : at + 8]
        pieces = []
        for other in range(n_tp):
            note = recv_ref[source * n_tp + other, even : even + 16, :].astype(F32)[at - even :]
            for piece in range(up_to(share, LANES) // LANES):
                length = min(LANES, share - piece * LANES)
                pieces.append(note[code_rows + piece : code_rows + piece + 1, :length])
        ids_ref[source : source + 1, :] = jnp.concatenate(pieces, axis=1)
    total = None
    for turn in range(1, n_tp):
        part_sum = dot(work[turn].astype(BF16), weight_refs[turn - 1][...])
        total = part_sum if total is None else total + part_sum
    total_ref[...] = total
    later_ref[...] = work[0].astype(BF16)
    for turn in range(n_tp):
        codes = notes[turn]
        power = jnp.zeros((8, LANES), F32)
        scale = jnp.ones((8, LANES), F32)
        for step in range(1, 8):
            above = codes >= 128.0 * 256.0**step
            power = power + jnp.where(above, 128.0, 0.0)
            scale = scale * jnp.where(above, 1.0 / 256.0, 1.0)
        spots = jnp.where(codes > 0.0, codes * scale - 128.0 + power, -1.0)
        for piece in range(code_rows):
            codes_ref[turn, :, piece * LANES : (piece + 1) * LANES] = spots[piece : piece + 1].astype(jnp.int32)


def stream_kernel(total_ref, later_ref, weight_ref, stream_ref):
    stream_ref[...] = (total_ref[...] + dot(later_ref[...], weight_ref[...])).astype(BF16)


def key_value_query(stream, gain, weights):
    rows = stream.astype(F32)
    mean = jnp.mean(rows, axis=-1, keepdims=True)
    second = jnp.mean(rows * rows, axis=-1, keepdims=True)
    normed = ((rows - mean) * lax.rsqrt(second - mean * mean + EPS) * gain).astype(BF16)
    result = dot_nt(normed, weights)
    third = weights.shape[0] // 3
    scale = jnp.where(iota((1, 3 * third), 1) >= 2 * third, HEAD_DIM ** (-0.5), 1.0)
    return (result * scale).astype(BF16)


def place_heads(turn, codes_ref, gain_ref, key_ref, value_ref, query_ref, stream_ref, rows):
    weights = jnp.concatenate([key_ref[...], value_ref[...], query_ref[...]], axis=0)
    result = key_value_query(stream_ref[...], one_row(gain_ref), weights)
    spots = codes_ref[turn]
    place = one_hot(iota((rows, spots.shape[1]), 0) == spots)[:, : result.shape[0]]
    return dot(place, result)


def first_heads_kernel(
    groups,
    codes_ref,
    gain_ref,
    key_ref,
    value_ref,
    query_ref,
    stream_ref,
    ids_ref,
    *refs,
):
    out_ref, same_ref, apart_ref, back_ref, spreads_ref = refs[:5]
    refs = refs[5:]
    rows, wide = same_ref.shape
    heads = wide // SLOT
    width = heads * HEAD_DIM
    place, column = lax.axis_index("seq"), lax.axis_index("tp")
    first = place_heads(0, codes_ref, gain_ref, key_ref, value_ref, query_ref, stream_ref, rows)
    out_ref[...] = first.astype(BF16)
    for shift in range(2):
        spreads_ref[shift] = one_hot(spread_mask(2 * width, wide, shift * width))

    ids = ids_ref[pl.ds(place, 1), :].astype(jnp.int32)
    same_ref[...] = id_lanes(ids, wide, None).astype(BF16)
    apart_ref[...] = id_lanes(ids, wide, NEG).astype(BF16)
    share = back_ref.shape[1]
    for turn in range(back_ref.shape[0]):
        wanted = stored_at((column ^ turn) * share + iota((share, 1), 0), rows)
        back_ref[turn] = one_hot(wanted == iota((share, rows), 1))
    apart_refs, apart_all = refs[:-1], refs[-1]
    for ref, (level, masks) in zip(apart_refs, groups):
        count = rows >> level
        slots = iota((count, wide), 1) >> 6
        for index, mask in enumerate(masks):
            far = ids_ref[pl.ds(place ^ mask, 1), :].astype(jnp.int32)
            apart_all[...] = id_lanes(far, wide, NEG).astype(BF16)
            chosen = None
            for head in range(heads):
                part = apart_all[pl.ds(head_start(level, head, column, rows), count), :]
                chosen = part if chosen is None else jnp.where(slots >= head, part, chosen)
            ref[index * count : (index + 1) * count, :] = chosen


def more_heads_kernel(turn, codes_ref, gain_ref, key_ref, value_ref, query_ref, stream_ref, before_ref, *refs):
    given_ref, out_ref, on_ref = refs if len(refs) == 3 else (None, refs[-1], None)
    more = place_heads(turn, codes_ref, gain_ref, key_ref, value_ref, query_ref, stream_ref, out_ref.shape[0])
    out_ref[...] = (before_ref[...].astype(F32) + more).astype(BF16)
    if on_ref is not None:
        on_ref[...] = given_ref[...]


def last_heads_kernel(
    turn, levels, codes_ref, gain_ref, key_ref, value_ref, query_ref, stream_ref, before_ref, packed, *sets
):
    rows = packed.shape[0]
    width = key_ref.shape[0]
    heads = width // HEAD_DIM
    column = lax.axis_index("tp")
    more_heads_kernel(
        turn, codes_ref, gain_ref, key_ref, value_ref, query_ref, stream_ref, before_ref, packed
    )
    for ref, level in zip(sets, levels):
        count = rows >> level
        lane = iota((count, 2 * width), 1)
        lane = jnp.where(lane >= width, lane - width, lane)
        chosen = None
        for head in range(heads):
            part = packed[pl.ds(head_start(level, head, column, rows), count), : 2 * width]
            chosen = part if chosen is None else jnp.where(lane >= head * HEAD_DIM, part, chosen)
        ref[...] = chosen


def id_lanes(ids, wide, apart):
    count = ids.shape[1]
    lane = iota((IDS, wide), 1) & (SLOT - 1)
    group = iota((IDS, wide), 0)
    same = lane - HEAD_DIM == group
    if apart is None:
        table = jnp.where(same, 1.0, 0.0)
    else:
        table = jnp.where((lane >= HEAD_DIM) & ~same, apart, 0.0)
    return dot_tn(one_hot(iota((IDS, count), 0) == ids), table.astype(BF16))


def agreement(level, group, column, rows, total, count):
    q_on, k_on = [], []
    for index, (head, first) in enumerate(group):
        for size, on in ((count, q_on), (total, k_on)):
            line, at = iota((8, size), 0), iota((8, size), 1)
            for step in range(1, size // count):
                at = at - jnp.where(iota((8, size), 1) >= step * count, count, 0)
            start = jnp.zeros((8, size), jnp.int32)
            length = jnp.zeros((8, size), jnp.int32)
            for branch in range(level, BRANCHES):
                start = jnp.where(line == branch, head_start(branch, head, column, rows) - first, start)
                length = jnp.where(line == branch, rows >> branch, length)
            on.append(jnp.where((at >= start) & (at < start + length), 1.0, 0.0))
        blank = jnp.zeros((8, count), F32)
        q_on[index] = jnp.concatenate([q_on[index] if place == index else blank for place in range(len(group))], axis=1)
    return jnp.concatenate(q_on, axis=0).astype(BF16), jnp.concatenate(k_on, axis=0).astype(BF16)


def repeat(block, times):
    return jnp.concatenate([block] * times, axis=1)


def own_kernel(packed_ref, same_ref, apart_ref, spreads_ref, acc_ref, tops_ref, masked_ref, keys_ref, values_ref):
    rows, wide = masked_ref.shape
    heads = wide // SLOT
    width = heads * HEAD_DIM
    column = lax.axis_index("tp")
    pairs = packed_ref[:, : 2 * width]
    query = dot(packed_ref[:, 2 * width :], spreads_ref[0, :width])
    masked_ref[...] = (query + same_ref[...].astype(F32)).astype(BF16)
    key = dot(pairs, spreads_ref[0])
    keys_ref[...] = (key + apart_ref[...].astype(F32)).astype(BF16)
    ones = jnp.where((iota((rows, wide), 1) & (SLOT - 1)) >= HEAD_DIM, 1.0, 0.0)
    value = dot(pairs, spreads_ref[1])
    values_ref[...] = (value + ones).astype(BF16)
    half = rows // 2
    slot_of = iota((half, wide), 1) >> 6
    for part in range(2):
        start = part * half
        query = masked_ref[start : start + half, :]
        acc = None
        for head in range(heads):
            one = jnp.where(slot_of == head, query, jnp.zeros((), BF16))
            scores = dot_nt(one, keys_ref[...])
            top = jnp.max(scores, axis=1, keepdims=True)
            tops_ref[head, start : start + half, :] = jnp.broadcast_to(top, (half, LANES))
            weights = jnp.exp(scores - top)
            if part == (head & 1):
                times = dot_tn(*agreement(0, [(head, start)], column, rows, half, half))
                scaled = weights[:, start : start + half] * times
                others = weights[:, half - start : rows - start]
                weights = jnp.concatenate([scaled, others] if part == 0 else [others, scaled], axis=1)
            got = dot(weights.astype(BF16), values_ref[...])
            acc = got if acc is None else jnp.where(slot_of == head, got, acc)
        acc_ref[start : start + half, :] = acc


def weigh_inner(weights, group, column, rows):
    count = rows >> 1
    length = rows >> 2
    head = group[0][0]
    start = head_start(2, head, column, rows) - head_start(1, head, column, rows)
    low, high = start // LANES * LANES, up_to(start + length, LANES)
    q_on, k_on = agreement(1, group, column, rows, count, count)
    part = weights[start : start + length]
    part = [part[:, :low], part[:, low:high] * dot_tn(q_on[:, start : start + length], k_on[:, low:high]), part[:, high:]]
    part = jnp.concatenate([one for one in part if one.shape[1]], axis=1)
    return jnp.concatenate([part, weights[length:]] if start == 0 else [weights[:start], part], axis=0)


def merge_sets(level, masks, sets, acc_ref, tops_ref, query_ref, spreads_ref, apart_ref):
    rows, wide = query_ref.shape
    column = lax.axis_index("tp")
    count = rows >> level
    some = min(max(1, rows // count), len(masks))
    total = some * count
    slot_of = iota((count, wide), 1) >> 6
    ones = jnp.where((iota((total, wide), 1) & (SLOT - 1)) >= HEAD_DIM, 1.0, 0.0)
    chunks = []
    for begin in range(0, len(masks), some):
        pairs = jnp.concatenate([ref[...] for ref in sets[begin : begin + some]], axis=0)
        keys = dot(pairs, spreads_ref[0]) + apart_ref[begin * count : begin * count + total, :].astype(F32)
        values = dot(pairs, spreads_ref[1]) + ones
        chunks.append((keys.astype(BF16), values.astype(BF16)))
    heads = wide // SLOT
    together = heads if heads * count * total <= 2**19 else 1
    states = []
    for low in range(0, heads, together):
        group = [(head, head_start(level, head, column, rows)) for head in range(low, low + together)]
        heres = [(head, pl.ds(first, count)) for head, first in group]
        query = [jnp.where(slot_of == head, query_ref[here, :], jnp.zeros((), BF16)) for head, here in heres]
        sums = [acc_ref[here, :] for _, here in heres]
        tops = [tops_ref[head, here, :] for head, here in heres]
        states.append((group, heres) + tuple(jnp.concatenate(parts, axis=0) for parts in (query, sums, tops)))
    merged = []
    for group, heres, query, sums, tops in states:
        inner = level == 1 and total == count and together == 1
        if not inner:
            times = dot_tn(*agreement(level, group, column, rows, total, count))
        for keys, values in chunks:
            scores = dot_nt(query, keys)
            top = jnp.maximum(tops, jnp.max(scores, axis=1, keepdims=True))
            weights = jnp.exp(scores - repeat(top, total // LANES))
            weights = weigh_inner(weights, group, column, rows) if inner else weights * times
            got = dot(weights.astype(BF16), values)
            sums = sums * repeat(jnp.exp(tops - top), wide // LANES) + got
            tops = top
        for index, (head, here) in enumerate(heres):
            part = slice(index * count, (index + 1) * count)
            merged.append((head, here, sums[part], tops[part]))
    return merged


def slot_lane(values, inner):
    wide = values.shape[1]
    row, lane = iota((wide, wide), 0), iota((wide, wide), 1)
    pick = one_hot(row == (lane >> 6) * SLOT + inner)
    high = values.astype(BF16)
    low = (values - high.astype(F32)).astype(BF16)
    return dot(high, pick) + dot(low, pick)


def near_kernel(groups, acc_ref, tops_ref, query_ref, spreads_ref, *refs):
    apart_refs, refs = refs[: len(groups)], refs[len(groups) :]
    sums_ref, new_tops_ref = refs[-2:]
    wide = query_ref.shape[1]
    del acc_ref, tops_ref

    for apart_ref, (level, masks) in zip(apart_refs, groups):
        merged = merge_sets(
            level, masks, refs[: len(masks)], sums_ref, new_tops_ref, query_ref, spreads_ref, apart_ref
        )
        refs = refs[len(masks) :]
        for head, here, sums, tops in merged:
            slot_of = iota(sums.shape, 1) >> 6
            sums_ref[here, :] = jnp.where(slot_of == head, sums, sums_ref[here, :])
            new_tops_ref[head, here, :] = tops


def mid_kernel(groups, acc_ref, tops_ref, query_ref, spreads_ref, *refs):
    sums_ref, _, early_ref, centre_ref = refs[-4:]
    near_kernel(groups, acc_ref, tops_ref, query_ref, spreads_ref, *refs[:-2])
    rows, wide = query_ref.shape
    heads = wide // SLOT
    every = sums_ref[...]
    inner = iota((rows, wide), 1) & (SLOT - 1)
    attn = jnp.where(inner < HEAD_DIM, every / slot_lane(every, HEAD_DIM), 0.0)
    average = jnp.full((wide, wide), 1.0, BF16)
    centre = (dot(attn.astype(BF16), average) * (1.0 / (heads * HEAD_DIM))).astype(BF16).astype(F32)
    centre_ref[...] = centre
    early_ref[...] = jnp.where(inner < HEAD_DIM, attn - centre, centre).astype(BF16)


def far_kernel(n_tp, level, masks, acc_ref, tops_ref, query_ref, spreads_ref, early_ref, centre_ref, back_ref, *refs):
    apart_ref, refs = refs[0], refs[1:]
    sets, refs = refs[: len(masks)], refs[len(masks) :]
    out_refs, message = refs[:n_tp], refs[-1]
    message[...] = early_ref[...]

    merged = merge_sets(level, masks, sets, acc_ref, tops_ref, query_ref, spreads_ref, apart_ref)
    for head, here, sums, _ in merged:
        lane = iota(sums.shape, 1)
        mine = (lane >= head * SLOT) & (lane < head * SLOT + HEAD_DIM)
        new = (sums / slot_lane(sums, HEAD_DIM) - centre_ref[here, :]).astype(BF16)
        message[here, :] = jnp.where(mine, new, message[here, :])
    final = message[...]
    for turn in range(n_tp):
        out_refs[turn][...] = dot(back_ref[turn], final).astype(BF16)


def base_kernel(n_tp, codes_ref, *refs):
    shards, part_refs = refs[:n_tp], refs[n_tp : 2 * n_tp]
    base_ref, weights_ref = refs[-2:]
    share = base_ref.shape[0]
    wanted = stored_at(lax.axis_index("tp") * share + iota((share, 1), 0), share * n_tp)
    base = None
    for turn in range(n_tp):
        spots = codes_ref[turn]
        moved = dot(one_hot(wanted == spots)[:, : shards[turn].shape[0]], shards[turn][...])
        base = moved if base is None else base + moved
    base_ref[...] = base.astype(BF16)
    heads = weights_ref.shape[1] // SLOT
    gap = jnp.zeros((SLOT - HEAD_DIM, weights_ref.shape[2]), BF16)
    for turn, ref in enumerate(part_refs):
        for head in range(heads):
            at, to = head * HEAD_DIM, head * SLOT
            weights_ref[turn, to : to + HEAD_DIM, :] = ref[at : at + HEAD_DIM, :]
            weights_ref[turn, to + HEAD_DIM : to + SLOT, :] = gap


def mix_kernel(n_tp, base_ref, weights_ref, *refs):
    message_refs, out_ref = refs[:n_tp], refs[-1]
    share, wide = base_ref.shape[0], weights_ref.shape[1]
    features = n_tp * (wide // SLOT) * HEAD_DIM
    inside = (iota((share, wide), 1) & (SLOT - 1)) < HEAD_DIM
    parts, centres = [], []
    for ref in message_refs:
        message = ref[...].astype(F32)
        parts.append(jnp.where(inside, message, 0.0))
        centres.append(message[:, HEAD_DIM : HEAD_DIM + 1])
    each = features // n_tp
    sums = [jnp.sum(part, axis=1, keepdims=True) + centre * each for part, centre in zip(parts, centres)]
    mean = sum(sums) * (1.0 / features)
    parts = [jnp.where(inside, part + (centre - mean), 0.0) for part, centre in zip(parts, centres)]
    spread = jnp.sum(sum(part * part for part in parts), axis=1, keepdims=True) * (1.0 / features)
    factor = lax.rsqrt(spread + EPS)
    total = base_ref[...].astype(F32)
    for turn, part in enumerate(parts):
        total = total + dot((part * factor).astype(BF16), weights_ref[turn])
    out_ref[...] = total.astype(BF16)


def swap(block, axis, mask):
    count = lax.axis_size(axis)
    return lax.ppermute(block, axis, [(index, index ^ mask) for index in range(count)])


def gather_tp(block):
    across = swap(block, "tp", 2)
    return [block, swap(block, "tp", 1), across, swap(across, "tp", 1)]


def body(
    tiles,
    tile_target,
    slide_id,
    proj_weight,
    norm_gain,
    query_weight,
    key_weight,
    value_weight,
    sub_gain,
    out_weight,
):
    n_seq = lax.axis_size("seq")
    n_tp = lax.axis_size("tp")
    rows, tile_width = tiles.shape
    features = proj_weight.shape[1]
    width = query_weight.shape[1]
    heads = width // HEAD_DIM
    wide = heads * SLOT
    share = rows // n_tp
    peer = rows // n_seq
    sub_pad = up_to(peer // n_tp, 8)
    arriving = n_seq * sub_pad
    chunks = tile_width // LANES
    block_rows = up_to(chunks * sub_pad + 8, 16)

    first_group = max(1, n_seq // 16)
    sizes = [min(first_group * 2**branch, n_seq) for branch in range(BRANCHES)]
    groups = []
    for level in range(BRANCHES):
        masks = tuple(range(1 if level == 0 else sizes[level - 1], sizes[level]))
        if masks:
            groups.append((level, masks))

    vmem_bytes = VMEM_BYTES if n_seq <= 8 else LARGE_VMEM_BYTES
    (blocks,) = call(
        functools.partial(route_kernel, n_seq, n_tp, peer),
        "route",
        [((n_seq * n_tp, block_rows, LANES), BF16)],
        [tile_target.reshape(-1, LANES), slide_id.reshape(-1, LANES), tiles],
        scratch=[
            pltpu.VMEM((rows // LANES, LANES), jnp.int32),
            pltpu.VMEM((rows // LANES, LANES), jnp.int32),
            pltpu.VMEM(tiles.shape, BF16),
            pltpu.VMEM((n_seq * n_tp, block_rows, LANES), BF16),
            pltpu.SemaphoreType.DMA((3,)),
            pltpu.SemaphoreType.DMA((n_seq,)),
        ],
        cost=3,
        vmem_bytes=ALL_VMEM_BYTES,
        apart=(0, 1, 2),
        out_apart=(0,),
    )
    received = lax.all_to_all(blocks, ("seq", "tp"), split_axis=0, concat_axis=0, tiled=True)
    proj_parts = gather_tp(proj_weight)
    (early,) = call(hint_kernel, "hint", [((16, LANES), BF16)], [proj_parts[-1]], cost=HINT_COST)
    (scaled,) = call(
        scale_kernel, "scale", [((width, features), BF16)], [sub_gain.reshape(1, width), out_weight], cost=1
    )

    beside = swap(scaled, "tp", 1)
    total, later, codes, ids = call(
        functools.partial(project_kernel, n_seq, n_tp, peer),
        "project",
        [((arriving, features), F32), ((arriving, tile_width), BF16)]
        + [((n_tp, 1, up_to(arriving, LANES)), jnp.int32), ((n_seq, rows), F32)],
        [received, early, beside] + proj_parts[1:],
        scratch=[
            pltpu.VMEM(received.shape, BF16),
            pltpu.VMEM((n_tp, arriving, tile_width), F32),
            pltpu.SemaphoreType.DMA((n_seq,)),
        ],
        vmem_bytes=vmem_bytes,
        apart=(0,),
    )
    (stream,) = call(
        stream_kernel,
        "stream",
        [((arriving, features), BF16)],
        [total, later, proj_weight],
        vmem_bytes=vmem_bytes,
    )
    shards = gather_tp(stream)

    gain = norm_gain.reshape(-1, LANES)
    weights = [gain, key_weight.T, value_weight.T, query_weight.T]
    partial, same, apart, back, spreads, *far_apart = call(
        functools.partial(first_heads_kernel, groups),
        "heads_1",
        [
            ((rows, 3 * width), BF16),
            ((rows, wide), BF16),
            ((rows, wide), BF16),
            ((n_tp, share, rows), BF16),
            ((2, 2 * width, wide), BF16),
        ]
        + [(((rows >> level) * len(masks), wide), BF16) for level, masks in groups],
        [codes] + weights + [shards[0], ids],
        scratch=[pltpu.VMEM((rows, wide), BF16)],
        vmem_bytes=vmem_bytes,
    )
    across = swap(scaled, "tp", 2)
    out_parts = [scaled, beside]
    for turn in range(1, n_tp - 1):
        given = [across] if turn == 1 else out_parts[3:]
        partial, *on = call(
            functools.partial(more_heads_kernel, turn),
            "heads_2",
            [((rows, 3 * width), BF16)] + [((width, features), BF16)] * (turn == 1),
            [codes] + weights + [shards[turn], partial] + given,
            cost=10 if turn == n_tp - 2 else 1,
            vmem_bytes=vmem_bytes,
        )
        if on:
            out_parts += on + [swap(on[0], "tp", 1)]
    packed, *sets = call(
        functools.partial(last_heads_kernel, n_tp - 1, [level for level, _ in groups]),
        "heads_3",
        [((rows, 3 * width), BF16)] + [((rows >> level, 2 * width), BF16) for level, _ in groups],
        [codes] + weights + [shards[n_tp - 1], partial],
        vmem_bytes=vmem_bytes,
    )
    sent = [[swap(one, "seq", mask) for mask in masks] for one, (_, masks) in zip(sets[:-1], groups)]
    direct = {mask: swap(sets[-1], "seq", mask) for mask in groups[-1][1] if mask % 2 == 0}
    sent.append([swap(direct[mask - 1], "seq", 1) if mask % 2 else direct[mask] for mask in groups[-1][1]])

    acc, tops, masked = call(
        own_kernel,
        "own",
        [((rows, wide), F32), ((heads, rows, LANES), F32), ((rows, wide), BF16)],
        [packed, same, apart, spreads],
        scratch=[pltpu.VMEM((rows, wide), BF16)] * 2,
        cost=0.1,
        vmem_bytes=vmem_bytes,
    )
    for index in range(len(groups) - 1):
        final = index == len(groups) - 2
        acc, tops, *rest_of = call(
            functools.partial(mid_kernel if final else near_kernel, [groups[index]]),
            "mid" if final else "near",
            [((rows, wide), F32), ((heads, rows, LANES), F32)]
            + ([((rows, wide), BF16), ((rows, wide), F32)] if final else []),
            [acc, tops, masked, spreads, far_apart[index]] + sent[index],
            aliases={0: 0, 1: 1},
            cost=6,
            vmem_bytes=vmem_bytes,
        )
    early, centre = rest_of
    messages = call(
        functools.partial(far_kernel, n_tp, *groups[-1]),
        "far",
        [((share, wide), BF16)] * n_tp,
        [acc, tops, masked, spreads, early, centre, back, far_apart[-1]] + sent[-1],
        scratch=[pltpu.VMEM((rows, wide), BF16)],
        vmem_bytes=vmem_bytes,
    )
    arrived = [messages[0]] + [swap(messages[turn], "tp", turn) for turn in range(1, n_tp)]
    base, padded = call(
        functools.partial(base_kernel, n_tp),
        "base",
        [((share, features), BF16), ((n_tp, wide, features), BF16)],
        [codes] + shards + out_parts,
        vmem_bytes=vmem_bytes,
    )
    (result,) = call(
        functools.partial(mix_kernel, n_tp),
        "mix",
        [((share, features), BF16)],
        [base, padded] + arrived,
    )
    return result


def solution(mesh):
    return jax.shard_map(
        body,
        mesh=mesh,
        in_specs=(
            P("seq", "tp"),
            P("seq"),
            P("seq"),
            P("tp", None),
            P(),
            P(None, "tp"),
            P(None, "tp"),
            P(None, "tp"),
            P("tp"),
            P("tp", None),
        ),
        out_specs=P(("seq", "tp"), None),
        check_vma=False,
    )
```

```python
import functools

import jax
import jax.numpy as jnp
from jax import lax
from jax.experimental import pallas as pl
from jax.experimental.pallas import tpu as pltpu
from jax.sharding import PartitionSpec as P

BRANCHES = 5
HEAD_DIM = 48
SLOT = 64
LANES = 128
IDS = 16
CLASSES = 2 ** (BRANCHES - 1)
NEG = -1e30
EPS = 1e-05
BF16 = jnp.bfloat16
F32 = jnp.float32
HINT_COST = 1
VMEM_BYTES = 16 * 1024 * 1024
LARGE_VMEM_BYTES = 48 * 1024 * 1024
ALL_VMEM_BYTES = 56 * 1024 * 1024


def up_to(count, step):
    return (count + step - 1) // step * step


def iota(shape, dim):
    return lax.broadcasted_iota(jnp.int32, shape, dim)


def dot(left, right):
    return jnp.dot(left, right, preferred_element_type=F32)


def dot_nt(left, right):
    return lax.dot_general(left, right, (((1,), (1,)), ((), ())), preferred_element_type=F32)


def dot_tn(left, right):
    return lax.dot_general(left, right, (((0,), (0,)), ((), ())), preferred_element_type=F32)


def one_hot(mask):
    return jnp.where(mask, 1.0, 0.0).astype(BF16)


def stored_at(position, rows):
    residue = position & (CLASSES - 1)
    flipped = jnp.zeros_like(residue)
    for bit in range(BRANCHES - 1):
        flipped = flipped + (((residue >> bit) & 1) << (BRANCHES - 2 - bit))
    return flipped * (rows // CLASSES) + (position >> (BRANCHES - 1))


def head_start(level, head, column, rows):
    start = 0
    for bit in range(level):
        value = (head >> bit) & 1 if bit < 2 else (column >> (bit - 2)) & 1
        start = start + value * (rows >> (bit + 1))
    return start


def call(kernel, name, outs, args, scratch=(), cost=1, vmem_bytes=VMEM_BYTES, apart=(), out_apart=(), aliases=None):
    vmem = pl.BlockSpec(memory_space=pltpu.VMEM)
    anywhere = pl.BlockSpec(memory_space=pltpu.HBM)
    return pl.pallas_call(
        kernel,
        name=name,
        out_shape=[jax.ShapeDtypeStruct(shape, dtype) for shape, dtype in outs],
        in_specs=[anywhere if index in apart else vmem for index in range(len(args))],
        out_specs=[anywhere if index in out_apart else vmem for index in range(len(outs))],
        scratch_shapes=list(scratch),
        input_output_aliases=aliases or {},
        compiler_params=pltpu.CompilerParams(vmem_limit_bytes=vmem_bytes),
        cost_estimate=pl.CostEstimate(flops=int(cost * 1e9), bytes_accessed=0, transcendentals=0),
    )(*args)


def one_row(ref):
    return jnp.concatenate([ref[index : index + 1, :] for index in range(ref.shape[0])], axis=1)


def route_kernel(
    n_seq,
    n_tp,
    peer,
    target_hbm,
    slide_hbm,
    tiles_hbm,
    out_hbm,
    target_ref,
    slide_ref,
    tiles_ref,
    out_ref,
    sems,
    out_sems,
):
    fetches = [
        pltpu.make_async_copy(target_hbm, target_ref, sems.at[0]),
        pltpu.make_async_copy(slide_hbm, slide_ref, sems.at[1]),
        pltpu.make_async_copy(tiles_hbm, tiles_ref, sems.at[2]),
    ]
    for fetch in fetches:
        fetch.start()
    rows = tiles_ref.shape[0]
    share = rows // n_tp
    code_rows = up_to(n_seq * up_to(peer // n_tp, 8), LANES) // LANES
    kept = stored_at(iota((1, rows), 1), rows) - lax.axis_index("tp") * share
    held = (kept >= 0) & (kept < share) & ((kept >> 7) + code_rows == (iota((n_seq * 8, rows), 0) & 7))
    kept_lane = one_hot(iota((LANES, rows), 0) == (kept & 127))
    before = one_hot(iota((LANES, LANES), 0) <= iota((LANES, LANES), 1))
    fetches[0].wait()
    chunks = tiles_ref.shape[1] // LANES
    sub = peer // n_tp
    sub_pad = up_to(sub, 8)
    blocks = n_seq * n_tp
    place, column = lax.axis_index("seq"), lax.axis_index("tp")
    target = one_row(target_ref)
    owner = jnp.floor((target.astype(F32) + 0.5) * (1.0 / rows)).astype(jnp.int32)
    flags = jnp.where(iota((n_seq, rows), 0) == owner, 1.0, 0.0)
    parts = [flags[:, at : at + LANES] for at in range(0, rows, LANES)]
    counts = dot(jnp.concatenate(parts, axis=0).astype(BF16), before)
    ahead = jnp.zeros((n_seq, 1), F32)
    slots = []
    for index, part in enumerate(parts):
        count = counts[index * n_seq : (index + 1) * n_seq]
        slots.append(jnp.sum(part * (count + ahead), axis=0, keepdims=True))
        ahead = ahead + count[:, LANES - 1 :]
    slot = jnp.concatenate(slots, axis=1).astype(jnp.int32) - 1
    lane_of = jnp.zeros_like(slot)
    for turn in range(1, n_tp):
        lane_of = lane_of + jnp.where(slot >= turn * sub, 1, 0)
    low = slot - lane_of * sub
    target_row = (owner * n_tp + lane_of) * sub_pad + low
    chooser = one_hot(iota((blocks * sub_pad, rows), 0) == target_row)

    stores = []
    fetches[1].wait()
    fetches[2].wait()
    picked = dot(chooser, tiles_ref[...])
    spot = stored_at(target - owner * rows, rows)
    high = spot >> 7
    code = ((spot & 127) + 128).astype(F32)
    for bit in range(3):
        code = code * jnp.where((high >> bit) & 1 == 1, 256.0 ** (2**bit), 1.0)
    arrival = place * sub_pad + low
    extra = n_seq * 8
    line = iota((extra, rows), 0)
    mine = (owner == (line >> 3)) & (lane_of == column) & ((arrival >> 7) == (line & 7))
    coded = dot_nt(
        jnp.where(mine, code, 0.0).astype(BF16),
        one_hot(iota((LANES, rows), 0) == (arrival & 127)),
    )
    ids = dot_nt(jnp.where(held, one_row(slide_ref).astype(F32), 0.0).astype(BF16), kept_lane)
    notes = coded + ids
    pad = out_hbm.shape[1] - chunks * sub_pad - 8
    for block in range(blocks):
        base = block * sub_pad
        pieces = [
            picked[base : base + sub_pad, part * LANES : (part + 1) * LANES] for part in range(chunks)
        ]
        start = block // n_tp * 8
        pieces.append(notes[start : start + 8])
        if pad:
            pieces.append(jnp.zeros((pad, LANES), F32))
        out_ref[block] = jnp.concatenate(pieces, axis=0).astype(BF16)
        if block % n_tp == n_tp - 1:
            some = pl.ds(block - n_tp + 1, n_tp)
            stores.append(pltpu.make_async_copy(out_ref.at[some], out_hbm.at[some], out_sems.at[block // n_tp]))
            stores[-1].start()
    for store in stores:
        store.wait()


def spread_mask(width, wide, shift):
    row = iota((width, wide), 0) - shift
    lane = iota((width, wide), 1)
    inner = lane & (SLOT - 1)
    return (inner < HEAD_DIM) & (row == (lane >> 6) * HEAD_DIM + inner)


def hint_kernel(weight_ref, out_ref):
    out_ref[...] = weight_ref[: out_ref.shape[0], : out_ref.shape[1]]


def scale_kernel(gain_ref, weight_ref, scaled_hbm, scaled_ref, sem):
    width = weight_ref.shape[0]
    same = iota((width, width), 0) == iota((width, width), 1)
    gain = jnp.sum(jnp.where(same, gain_ref[...], 0.0), axis=1, keepdims=True)
    scaled_ref[...] = (weight_ref[...].astype(F32) * gain).astype(BF16)
    store = pltpu.make_async_copy(scaled_ref, scaled_hbm, sem)
    store.start()
    store.wait()


def project_kernel(n_seq, n_tp, peer, recv_hbm, early_ref, beside_ref, *refs):
    del early_ref, beside_ref
    weight_refs = refs[: n_tp - 1]
    total_ref, later_ref, codes_ref, ids_ref, recv_ref, sems = refs[n_tp - 1 :]
    fetches = []
    for source in range(n_seq):
        some = pl.ds(source * n_tp, n_tp)
        fetches.append(pltpu.make_async_copy(recv_hbm.at[some], recv_ref.at[some], sems.at[source]))
        fetches[-1].start()
    sub_pad = up_to(peer // n_tp, 8)
    chunks = later_ref.shape[1] // LANES
    column = lax.axis_index("tp")
    code_rows = codes_ref.shape[2] // LANES
    share = ids_ref.shape[1] // n_tp
    at = chunks * sub_pad
    even = at // 16 * 16
    for fetch in fetches:
        fetch.wait()
    notes, laid = [], []
    for turn in range(n_tp):
        blocks = [recv_ref[source * n_tp + (column ^ turn)].astype(F32) for source in range(n_seq)]
        notes.append(sum(block[at : at + 8] for block in blocks))
        columns = [
            jnp.concatenate([block[part * sub_pad : (part + 1) * sub_pad] for block in blocks], axis=0).astype(BF16)
            for part in range(chunks)
        ]
        laid.append(jnp.concatenate(columns, axis=1))
    total = None
    for turn in range(1, n_tp):
        part_sum = dot(laid[turn], weight_refs[turn - 1][...])
        total = part_sum if total is None else total + part_sum
    total_ref[...] = total
    for source in range(n_seq):
        pieces = []
        for other in range(n_tp):
            note = recv_ref[source * n_tp + other, even : even + 16, :].astype(F32)[at - even :]
            for piece in range(up_to(share, LANES) // LANES):
                length = min(LANES, share - piece * LANES)
                pieces.append(note[code_rows + piece : code_rows + piece + 1, :length])
        ids_ref[source : source + 1, :] = jnp.concatenate(pieces, axis=1)
    later_ref[...] = laid[0]
    for turn in range(n_tp):
        codes = notes[turn]
        power = jnp.zeros((8, LANES), F32)
        scale = jnp.ones((8, LANES), F32)
        for step in range(1, 8):
            above = codes >= 128.0 * 256.0**step
            power = power + jnp.where(above, 128.0, 0.0)
            scale = scale * jnp.where(above, 1.0 / 256.0, 1.0)
        spots = jnp.where(codes > 0.0, codes * scale - 128.0 + power, -1.0)
        for piece in range(code_rows):
            codes_ref[turn, :, piece * LANES : (piece + 1) * LANES] = spots[piece : piece + 1].astype(jnp.int32)


def stream_kernel(total_ref, later_ref, weight_ref, stream_ref):
    stream_ref[...] = (total_ref[...] + dot(later_ref[...], weight_ref[...])).astype(BF16)


def key_value_query(stream, gain, weights):
    rows = stream.astype(F32)
    mean = jnp.mean(rows, axis=-1, keepdims=True)
    second = jnp.mean(rows * rows, axis=-1, keepdims=True)
    normed = ((rows - mean) * lax.rsqrt(second - mean * mean + EPS) * gain).astype(BF16)
    result = dot_nt(normed, weights)
    third = weights.shape[0] // 3
    scale = jnp.where(iota((1, 3 * third), 1) >= 2 * third, HEAD_DIM ** (-0.5), 1.0)
    return (result * scale).astype(BF16)


def place_heads(turn, codes_ref, gain_ref, key_ref, value_ref, query_ref, stream_ref, rows):
    weights = jnp.concatenate([key_ref[...], value_ref[...], query_ref[...]], axis=0)
    result = key_value_query(stream_ref[...], one_row(gain_ref), weights)
    spots = codes_ref[turn]
    place = one_hot(iota((rows, spots.shape[1]), 0) == spots)[:, : result.shape[0]]
    return dot(place, result)


def first_heads_kernel(
    groups,
    codes_ref,
    gain_ref,
    key_ref,
    value_ref,
    query_ref,
    stream_ref,
    ids_ref,
    *refs,
):
    out_ref, same_ref, apart_ref, back_ref, spreads_ref = refs[:5]
    refs = refs[5:]
    rows, wide = same_ref.shape
    heads = wide // SLOT
    width = heads * HEAD_DIM
    place, column = lax.axis_index("seq"), lax.axis_index("tp")
    first = place_heads(0, codes_ref, gain_ref, key_ref, value_ref, query_ref, stream_ref, rows)
    out_ref[...] = first.astype(BF16)
    for shift in range(2):
        spreads_ref[shift] = one_hot(spread_mask(2 * width, wide, shift * width))

    ids = ids_ref[pl.ds(place, 1), :].astype(jnp.int32)
    same_ref[...] = id_lanes(ids, wide, None).astype(BF16)
    apart_ref[...] = id_lanes(ids, wide, NEG).astype(BF16)
    share = back_ref.shape[1]
    for turn in range(back_ref.shape[0]):
        wanted = stored_at((column ^ turn) * share + iota((share, 1), 0), rows)
        back_ref[turn] = one_hot(wanted == iota((share, rows), 1))
    apart_refs, apart_all = refs[:-1], refs[-1]
    for ref, (level, masks) in zip(apart_refs, groups):
        count = rows >> level
        slots = iota((count, wide), 1) >> 6
        for index, mask in enumerate(masks):
            far = ids_ref[pl.ds(place ^ mask, 1), :].astype(jnp.int32)
            apart_all[...] = id_lanes(far, wide, NEG).astype(BF16)
            chosen = None
            for head in range(heads):
                part = apart_all[pl.ds(head_start(level, head, column, rows), count), :]
                chosen = part if chosen is None else jnp.where(slots >= head, part, chosen)
            ref[index * count : (index + 1) * count, :] = chosen


def more_heads_kernel(turn, codes_ref, gain_ref, key_ref, value_ref, query_ref, stream_ref, before_ref, *refs):
    given_ref, out_ref, on_ref = refs if len(refs) == 3 else (None, refs[-1], None)
    more = place_heads(turn, codes_ref, gain_ref, key_ref, value_ref, query_ref, stream_ref, out_ref.shape[0])
    out_ref[...] = (before_ref[...].astype(F32) + more).astype(BF16)
    if on_ref is not None:
        on_ref[...] = given_ref[...]


def last_heads_kernel(
    turn, levels, codes_ref, gain_ref, key_ref, value_ref, query_ref, stream_ref, before_ref, packed, *sets
):
    rows = packed.shape[0]
    width = key_ref.shape[0]
    heads = width // HEAD_DIM
    column = lax.axis_index("tp")
    more_heads_kernel(
        turn, codes_ref, gain_ref, key_ref, value_ref, query_ref, stream_ref, before_ref, packed
    )
    for ref, level in zip(sets, levels):
        count = rows >> level
        lane = iota((count, 2 * width), 1)
        lane = jnp.where(lane >= width, lane - width, lane)
        chosen = None
        for head in range(heads):
            part = packed[pl.ds(head_start(level, head, column, rows), count), : 2 * width]
            chosen = part if chosen is None else jnp.where(lane >= head * HEAD_DIM, part, chosen)
        ref[...] = chosen


def id_lanes(ids, wide, apart):
    count = ids.shape[1]
    lane = iota((IDS, wide), 1) & (SLOT - 1)
    group = iota((IDS, wide), 0)
    same = lane - HEAD_DIM == group
    if apart is None:
        table = jnp.where(same, 1.0, 0.0)
    else:
        table = jnp.where((lane >= HEAD_DIM) & ~same, apart, 0.0)
    return dot_tn(one_hot(iota((IDS, count), 0) == ids), table.astype(BF16))


def agreement(level, group, column, rows, total, count):
    q_on, k_on = [], []
    for index, (head, first) in enumerate(group):
        for size, on in ((count, q_on), (total, k_on)):
            line, at = iota((8, size), 0), iota((8, size), 1)
            for step in range(1, size // count):
                at = at - jnp.where(iota((8, size), 1) >= step * count, count, 0)
            start = jnp.zeros((8, size), jnp.int32)
            length = jnp.zeros((8, size), jnp.int32)
            for branch in range(level, BRANCHES):
                start = jnp.where(line == branch, head_start(branch, head, column, rows) - first, start)
                length = jnp.where(line == branch, rows >> branch, length)
            on.append(jnp.where((at >= start) & (at < start + length), 1.0, 0.0))
        blank = jnp.zeros((8, count), F32)
        q_on[index] = jnp.concatenate([q_on[index] if place == index else blank for place in range(len(group))], axis=1)
    return jnp.concatenate(q_on, axis=0).astype(BF16), jnp.concatenate(k_on, axis=0).astype(BF16)


def repeat(block, times):
    return jnp.concatenate([block] * times, axis=1)


def own_kernel(packed_ref, same_ref, apart_ref, spreads_ref, acc_ref, tops_ref, masked_ref, keys_ref, values_ref):
    rows, wide = masked_ref.shape
    heads = wide // SLOT
    width = heads * HEAD_DIM
    column = lax.axis_index("tp")
    pairs = packed_ref[:, : 2 * width]
    query = dot(packed_ref[:, 2 * width :], spreads_ref[0, :width])
    masked_ref[...] = (query + same_ref[...].astype(F32)).astype(BF16)
    key = dot(pairs, spreads_ref[0])
    keys_ref[...] = (key + apart_ref[...].astype(F32)).astype(BF16)
    ones = jnp.where((iota((rows, wide), 1) & (SLOT - 1)) >= HEAD_DIM, 1.0, 0.0)
    value = dot(pairs, spreads_ref[1])
    values_ref[...] = (value + ones).astype(BF16)
    half = rows // 2
    slot_of = iota((half, wide), 1) >> 6
    for part in range(2):
        start = part * half
        query = masked_ref[start : start + half, :]
        acc = None
        for head in range(heads):
            one = jnp.where(slot_of == head, query, jnp.zeros((), BF16))
            scores = dot_nt(one, keys_ref[...])
            top = jnp.max(scores, axis=1, keepdims=True)
            tops_ref[head, start : start + half, :] = jnp.broadcast_to(top, (half, LANES))
            weights = jnp.exp(scores - top)
            if part == (head & 1):
                times = dot_tn(*agreement(0, [(head, start)], column, rows, half, half))
                scaled = weights[:, start : start + half] * times
                others = weights[:, half - start : rows - start]
                weights = jnp.concatenate([scaled, others] if part == 0 else [others, scaled], axis=1)
            got = dot(weights.astype(BF16), values_ref[...])
            acc = got if acc is None else jnp.where(slot_of == head, got, acc)
        acc_ref[start : start + half, :] = acc


def weigh_inner(weights, group, column, rows):
    count = rows >> 1
    length = rows >> 2
    head = group[0][0]
    start = head_start(2, head, column, rows) - head_start(1, head, column, rows)
    low, high = start // LANES * LANES, up_to(start + length, LANES)
    q_on, k_on = agreement(1, group, column, rows, count, count)
    part = weights[start : start + length]
    part = [part[:, :low], part[:, low:high] * dot_tn(q_on[:, start : start + length], k_on[:, low:high]), part[:, high:]]
    part = jnp.concatenate([one for one in part if one.shape[1]], axis=1)
    return jnp.concatenate([part, weights[length:]] if start == 0 else [weights[:start], part], axis=0)


def merge_sets(level, masks, sets, acc_ref, tops_ref, query_ref, spreads_ref, apart_ref):
    rows, wide = query_ref.shape
    column = lax.axis_index("tp")
    count = rows >> level
    some = min(max(1, rows // count), len(masks))
    total = some * count
    slot_of = iota((count, wide), 1) >> 6
    ones = jnp.where((iota((total, wide), 1) & (SLOT - 1)) >= HEAD_DIM, 1.0, 0.0)
    chunks = []
    for begin in range(0, len(masks), some):
        pairs = jnp.concatenate([ref[...] for ref in sets[begin : begin + some]], axis=0)
        keys = dot(pairs, spreads_ref[0]) + apart_ref[begin * count : begin * count + total, :].astype(F32)
        values = dot(pairs, spreads_ref[1]) + ones
        chunks.append((keys.astype(BF16), values.astype(BF16)))
    heads = wide // SLOT
    together = heads if heads * count * total <= 2**19 else 1
    states = []
    for low in range(0, heads, together):
        group = [(head, head_start(level, head, column, rows)) for head in range(low, low + together)]
        heres = [(head, pl.ds(first, count)) for head, first in group]
        query = [jnp.where(slot_of == head, query_ref[here, :], jnp.zeros((), BF16)) for head, here in heres]
        sums = [acc_ref[here, :] for _, here in heres]
        tops = [tops_ref[head, here, :] for head, here in heres]
        states.append((group, heres) + tuple(jnp.concatenate(parts, axis=0) for parts in (query, sums, tops)))
    merged = []
    for group, heres, query, sums, tops in states:
        inner = level == 1 and total == count and together == 1
        if not inner:
            times = dot_tn(*agreement(level, group, column, rows, total, count))
        for keys, values in chunks:
            scores = dot_nt(query, keys)
            top = jnp.maximum(tops, jnp.max(scores, axis=1, keepdims=True))
            weights = jnp.exp(scores - repeat(top, total // LANES))
            weights = weigh_inner(weights, group, column, rows) if inner else weights * times
            got = dot(weights.astype(BF16), values)
            sums = sums * repeat(jnp.exp(tops - top), wide // LANES) + got
            tops = top
        for index, (head, here) in enumerate(heres):
            part = slice(index * count, (index + 1) * count)
            merged.append((head, here, sums[part], tops[part]))
    return merged


def slot_lane(values, inner):
    wide = values.shape[1]
    row, lane = iota((wide, wide), 0), iota((wide, wide), 1)
    pick = one_hot(row == (lane >> 6) * SLOT + inner)
    high = values.astype(BF16)
    low = (values - high.astype(F32)).astype(BF16)
    return dot(high, pick) + dot(low, pick)


def near_kernel(groups, acc_ref, tops_ref, query_ref, spreads_ref, *refs):
    apart_refs, refs = refs[: len(groups)], refs[len(groups) :]
    sums_ref, new_tops_ref = refs[-2:]
    wide = query_ref.shape[1]
    del acc_ref, tops_ref

    for apart_ref, (level, masks) in zip(apart_refs, groups):
        merged = merge_sets(
            level, masks, refs[: len(masks)], sums_ref, new_tops_ref, query_ref, spreads_ref, apart_ref
        )
        refs = refs[len(masks) :]
        for head, here, sums, tops in merged:
            slot_of = iota(sums.shape, 1) >> 6
            sums_ref[here, :] = jnp.where(slot_of == head, sums, sums_ref[here, :])
            new_tops_ref[head, here, :] = tops


def mid_kernel(groups, acc_ref, tops_ref, query_ref, spreads_ref, back_ref, *refs, n_sent):
    sent_refs = refs[-n_sent:]
    refs = refs[:-n_sent]
    sums_ref, _, early_ref, centre_ref = refs[-4:]
    near_kernel(groups, acc_ref, tops_ref, query_ref, spreads_ref, *refs[:-2])
    rows, wide = query_ref.shape
    heads = wide // SLOT
    every = sums_ref[...]
    inner = iota((rows, wide), 1) & (SLOT - 1)
    attn = jnp.where(inner < HEAD_DIM, every / slot_lane(every, HEAD_DIM), 0.0)
    average = jnp.full((wide, wide), 1.0, BF16)
    centre = (dot(attn.astype(BF16), average) * (1.0 / (heads * HEAD_DIM))).astype(BF16).astype(F32)
    centre_ref[...] = centre
    early = jnp.where(inner < HEAD_DIM, attn - centre, centre).astype(BF16)
    early_ref[...] = early
    for index, ref in enumerate(sent_refs):
        ref[...] = dot(back_ref[back_ref.shape[0] - n_sent + index], early).astype(BF16)


def far_kernel(n_tp, level, masks, acc_ref, tops_ref, query_ref, spreads_ref, early_ref, centre_ref, back_ref, *refs):
    apart_ref, refs = refs[0], refs[1:]
    sets, refs = refs[: len(masks)], refs[len(masks) :]
    out_refs, message = refs[:n_tp], refs[-1]
    message[...] = early_ref[...]

    merged = merge_sets(level, masks, sets, acc_ref, tops_ref, query_ref, spreads_ref, apart_ref)
    changed = None
    for head, here, sums, _ in merged:
        lane = iota(sums.shape, 1)
        mine = (lane >= head * SLOT) & (lane < head * SLOT + HEAD_DIM)
        new = (sums / slot_lane(sums, HEAD_DIM) - centre_ref[here, :]).astype(BF16)
        message[here, :] = jnp.where(mine, new, message[here, :])
        changed = new if changed is None else jnp.where(lane >= head * SLOT, new, changed)
    final = message[...]
    rows = message.shape[0]
    count = rows >> level
    for turn in range(n_tp):
        ref = out_refs[turn]
        if ref.shape[0] == back_ref.shape[1]:
            ref[...] = dot(back_ref[turn], final).astype(BF16)
        else:
            each = rows // CLASSES
            classes = count // each
            line = iota((ref.shape[0], count), 0)
            spot = (lax.axis_index("tp") ^ turn) * (each // n_tp) + line // classes
            wanted = (line % classes) * each + spot
            pick = (iota((ref.shape[0], count), 1) == wanted) & (line < count // n_tp)
            ref[...] = dot(one_hot(pick), changed).astype(BF16)


def base_kernel(n_tp, codes_ref, *refs):
    shards, part_refs = refs[:n_tp], refs[n_tp : 2 * n_tp]
    base_ref, weights_ref = refs[-2:]
    share = base_ref.shape[0]
    wanted = stored_at(lax.axis_index("tp") * share + iota((share, 1), 0), share * n_tp)
    base = None
    for turn in range(n_tp):
        spots = codes_ref[turn]
        moved = dot(one_hot(wanted == spots)[:, : shards[turn].shape[0]], shards[turn][...])
        base = moved if base is None else base + moved
    base_ref[...] = base.astype(BF16)
    heads = weights_ref.shape[1] // SLOT
    gap = jnp.zeros((SLOT - HEAD_DIM, weights_ref.shape[2]), BF16)
    for turn, ref in enumerate(part_refs):
        for head in range(heads):
            at, to = head * HEAD_DIM, head * SLOT
            weights_ref[turn, to : to + HEAD_DIM, :] = ref[at : at + HEAD_DIM, :]
            weights_ref[turn, to + HEAD_DIM : to + SLOT, :] = gap


def mix_kernel(n_tp, level, base_ref, weights_ref, *refs):
    message_refs, change_refs, out_ref = refs[:n_tp], refs[n_tp:-1], refs[-1]
    share, wide = base_ref.shape[0], weights_ref.shape[1]
    features = n_tp * (wide // SLOT) * HEAD_DIM
    lane = iota((share, wide), 1)
    inside = (lane & (SLOT - 1)) < HEAD_DIM
    parts, centres = [], []
    for turn, ref in enumerate(message_refs):
        message = ref[...].astype(F32)
        centres.append(message[:, HEAD_DIM : HEAD_DIM + 1])
        if turn >= n_tp - len(change_refs):
            change = change_refs[turn - n_tp + len(change_refs)][...]
            count = change.shape[0]
            moved = dot(one_hot(iota((share, count), 1) == iota((share, count), 0) >> level), change)
            head = (lax.axis_index("tp") ^ turn) * (wide // SLOT) + (lane >> 6)
            late = ((iota((share, wide), 0) ^ head) & (2**level - 1)) == 0
            message = jnp.where(late, moved, message)
        parts.append(jnp.where(inside, message, 0.0))
    each = features // n_tp
    sums = [jnp.sum(part, axis=1, keepdims=True) + centre * each for part, centre in zip(parts, centres)]
    mean = sum(sums) * (1.0 / features)
    parts = [jnp.where(inside, part + (centre - mean), 0.0) for part, centre in zip(parts, centres)]
    spread = jnp.sum(sum(part * part for part in parts), axis=1, keepdims=True) * (1.0 / features)
    factor = lax.rsqrt(spread + EPS)
    total = base_ref[...].astype(F32)
    for turn, part in enumerate(parts):
        total = total + dot((part * factor).astype(BF16), weights_ref[turn])
    out_ref[...] = total.astype(BF16)


def swap(block, axis, mask):
    count = lax.axis_size(axis)
    return lax.ppermute(block, axis, [(index, index ^ mask) for index in range(count)])


def gather_tp(block):
    across = swap(block, "tp", 2)
    return [block, swap(block, "tp", 1), across, swap(across, "tp", 1)]


def body(
    tiles,
    tile_target,
    slide_id,
    proj_weight,
    norm_gain,
    query_weight,
    key_weight,
    value_weight,
    sub_gain,
    out_weight,
):
    n_seq = lax.axis_size("seq")
    n_tp = lax.axis_size("tp")
    rows, tile_width = tiles.shape
    features = proj_weight.shape[1]
    width = query_weight.shape[1]
    heads = width // HEAD_DIM
    wide = heads * SLOT
    share = rows // n_tp
    peer = rows // n_seq
    sub_pad = up_to(peer // n_tp, 8)
    arriving = n_seq * sub_pad
    chunks = tile_width // LANES
    block_rows = up_to(chunks * sub_pad + 8, 16)

    first_group = max(1, n_seq // 16)
    sizes = [min(first_group * 2**branch, n_seq) for branch in range(BRANCHES)]
    groups = []
    for level in range(BRANCHES):
        masks = tuple(range(1 if level == 0 else sizes[level - 1], sizes[level]))
        if masks:
            groups.append((level, masks))

    vmem_bytes = VMEM_BYTES if n_seq <= 8 else LARGE_VMEM_BYTES
    (blocks,) = call(
        functools.partial(route_kernel, n_seq, n_tp, peer),
        "route",
        [((n_seq * n_tp, block_rows, LANES), BF16)],
        [tile_target.reshape(-1, LANES), slide_id.reshape(-1, LANES), tiles],
        scratch=[
            pltpu.VMEM((rows // LANES, LANES), jnp.int32),
            pltpu.VMEM((rows // LANES, LANES), jnp.int32),
            pltpu.VMEM(tiles.shape, BF16),
            pltpu.VMEM((n_seq * n_tp, block_rows, LANES), BF16),
            pltpu.SemaphoreType.DMA((3,)),
            pltpu.SemaphoreType.DMA((n_seq,)),
        ],
        cost=3,
        vmem_bytes=ALL_VMEM_BYTES,
        apart=(0, 1, 2),
        out_apart=(0,),
    )
    received = lax.all_to_all(blocks, ("seq", "tp"), split_axis=0, concat_axis=0, tiled=True)
    proj_parts = gather_tp(proj_weight)
    (early,) = call(hint_kernel, "hint", [((16, LANES), BF16)], [proj_parts[-1]], cost=HINT_COST)
    (scaled,) = call(
        scale_kernel,
        "scale",
        [((width, features), BF16)],
        [sub_gain.reshape(1, width), out_weight],
        scratch=[pltpu.VMEM((width, features), BF16), pltpu.SemaphoreType.DMA],
        cost=1,
        out_apart=(0,),
    )

    beside = swap(scaled, "tp", 1)
    total, later, codes, ids = call(
        functools.partial(project_kernel, n_seq, n_tp, peer),
        "project",
        [((arriving, features), F32), ((arriving, tile_width), BF16)]
        + [((n_tp, 1, up_to(arriving, LANES)), jnp.int32), ((n_seq, rows), F32)],
        [received, early, beside] + proj_parts[1:],
        cost=0.5,
        scratch=[
            pltpu.VMEM(received.shape, BF16),
            pltpu.SemaphoreType.DMA((n_seq,)),
        ],
        vmem_bytes=vmem_bytes,
        apart=(0,),
    )
    (stream,) = call(
        stream_kernel,
        "stream",
        [((arriving, features), BF16)],
        [total, later, proj_weight],
        cost=0.1,
        vmem_bytes=vmem_bytes,
    )
    shards = gather_tp(stream)

    gain = norm_gain.reshape(-1, LANES)
    weights = [gain, key_weight.T, value_weight.T, query_weight.T]
    partial, same, apart, back, spreads, *far_apart = call(
        functools.partial(first_heads_kernel, groups),
        "heads_1",
        [
            ((rows, 3 * width), BF16),
            ((rows, wide), BF16),
            ((rows, wide), BF16),
            ((n_tp, share, rows), BF16),
            ((2, 2 * width, wide), BF16),
        ]
        + [(((rows >> level) * len(masks), wide), BF16) for level, masks in groups],
        [codes] + weights + [shards[0], ids],
        scratch=[pltpu.VMEM((rows, wide), BF16)],
        vmem_bytes=vmem_bytes,
    )
    across = swap(scaled, "tp", 2)
    out_parts = [scaled, beside]
    for turn in range(1, n_tp - 1):
        given = [across] if turn == 1 else out_parts[3:]
        partial, *on = call(
            functools.partial(more_heads_kernel, turn),
            "heads_2",
            [((rows, 3 * width), BF16)] + [((width, features), BF16)] * (turn == 1),
            [codes] + weights + [shards[turn], partial] + given,
            cost=10 if turn == n_tp - 2 else 1,
            vmem_bytes=vmem_bytes,
        )
        if on:
            out_parts += on + [swap(on[0], "tp", 1)]
    packed, *sets = call(
        functools.partial(last_heads_kernel, n_tp - 1, [level for level, _ in groups]),
        "heads_3",
        [((rows, 3 * width), BF16)] + [((rows >> level, 2 * width), BF16) for level, _ in groups],
        [codes] + weights + [shards[n_tp - 1], partial],
        vmem_bytes=vmem_bytes,
    )
    sent = [[swap(one, "seq", mask) for mask in masks] for one, (_, masks) in zip(sets[:-1], groups)]
    direct = {mask: swap(sets[-1], "seq", mask) for mask in groups[-1][1] if mask % 2 == 0}
    sent.append([swap(direct[mask - 1], "seq", 1) if mask % 2 else direct[mask] for mask in groups[-1][1]])

    acc, tops, masked = call(
        own_kernel,
        "own",
        [((rows, wide), F32), ((heads, rows, LANES), F32), ((rows, wide), BF16)],
        [packed, same, apart, spreads],
        scratch=[pltpu.VMEM((rows, wide), BF16)] * 2,
        cost=0.1,
        vmem_bytes=vmem_bytes,
    )
    n_sent = n_tp - 1
    for index in range(len(groups) - 1):
        kernel, outs, given = near_kernel, [], []
        if index == len(groups) - 2:
            kernel, given = functools.partial(mid_kernel, n_sent=n_sent), [back]
            outs = [((rows, wide), BF16), ((rows, wide), F32)] + [((share, wide), BF16)] * n_sent
        acc, tops, *more = call(
            functools.partial(kernel, [groups[index]]),
            "mid" if outs else "near",
            [((rows, wide), F32), ((heads, rows, LANES), F32)] + outs,
            [acc, tops, masked, spreads] + given + [far_apart[index]] + sent[index],
            aliases={0: 0, 1: 1},
            cost=6,
            vmem_bytes=vmem_bytes,
        )
    early, centre, *ahead = more
    messages = call(
        functools.partial(far_kernel, n_tp, *groups[-1]),
        "far",
        [((share, wide), BF16)] * (n_tp - n_sent)
        + [((up_to((rows >> groups[-1][0]) // n_tp, 16), wide), BF16)] * n_sent,
        [acc, tops, masked, spreads, early, centre, back, far_apart[-1]] + sent[-1],
        scratch=[pltpu.VMEM((rows, wide), BF16)],
        vmem_bytes=vmem_bytes,
    )
    ahead = [swap(one, "tp", n_tp - n_sent + index) for index, one in enumerate(ahead)]
    arrived = [messages[0]] + [swap(messages[turn], "tp", turn) for turn in range(1, n_tp)]
    arrived = arrived[: n_tp - n_sent] + ahead + arrived[n_tp - n_sent :]
    base, padded = call(
        functools.partial(base_kernel, n_tp),
        "base",
        [((share, features), BF16), ((n_tp, wide, features), BF16)],
        [codes] + shards + out_parts,
        cost=0.3,
        vmem_bytes=vmem_bytes,
    )
    (result,) = call(
        functools.partial(mix_kernel, n_tp, groups[-1][0]),
        "mix",
        [((share, features), BF16)],
        [base, padded] + arrived,
    )
    return result


def solution(mesh):
    return jax.shard_map(
        body,
        mesh=mesh,
        in_specs=(
            P("seq", "tp"),
            P("seq"),
            P("seq"),
            P("tp", None),
            P(),
            P(None, "tp"),
            P(None, "tp"),
            P(None, "tp"),
            P("tp"),
            P("tp", None),
        ),
        out_specs=P(("seq", "tp"), None),
        check_vma=False,
    )
```

```python
import functools

import jax
import jax.numpy as jnp
from jax import lax
from jax.experimental import pallas as pl
from jax.experimental.pallas import tpu as pltpu
from jax.sharding import PartitionSpec as P

BRANCHES = 5
HEAD_DIM = 48
SLOT = 64
LANES = 128
IDS = 16
CLASSES = 2 ** (BRANCHES - 1)
NEG = -1e30
EPS = 1e-05
BF16 = jnp.bfloat16
F32 = jnp.float32
HINT_COST = 1
VMEM_BYTES = 16 * 1024 * 1024
LARGE_VMEM_BYTES = 48 * 1024 * 1024
ALL_VMEM_BYTES = 56 * 1024 * 1024


def up_to(count, step):
    return (count + step - 1) // step * step


def iota(shape, dim):
    return lax.broadcasted_iota(jnp.int32, shape, dim)


def dot(left, right):
    return jnp.dot(left, right, preferred_element_type=F32)


def dot_nt(left, right):
    return lax.dot_general(left, right, (((1,), (1,)), ((), ())), preferred_element_type=F32)


def dot_tn(left, right):
    return lax.dot_general(left, right, (((0,), (0,)), ((), ())), preferred_element_type=F32)


def one_hot(mask):
    return jnp.where(mask, 1.0, 0.0).astype(BF16)


def stored_at(position, rows):
    residue = position & (CLASSES - 1)
    flipped = jnp.zeros_like(residue)
    for bit in range(BRANCHES - 1):
        flipped = flipped + (((residue >> bit) & 1) << (BRANCHES - 2 - bit))
    return flipped * (rows // CLASSES) + (position >> (BRANCHES - 1))


def head_start(level, head, column, rows):
    start = 0
    for bit in range(level):
        value = (head >> bit) & 1 if bit < 2 else (column >> (bit - 2)) & 1
        start = start + value * (rows >> (bit + 1))
    return start


def call(kernel, name, outs, args, scratch=(), cost=1, vmem_bytes=VMEM_BYTES, apart=(), out_apart=(), aliases=None):
    vmem = pl.BlockSpec(memory_space=pltpu.VMEM)
    anywhere = pl.BlockSpec(memory_space=pltpu.HBM)
    return pl.pallas_call(
        kernel,
        name=name,
        out_shape=[jax.ShapeDtypeStruct(shape, dtype) for shape, dtype in outs],
        in_specs=[anywhere if index in apart else vmem for index in range(len(args))],
        out_specs=[anywhere if index in out_apart else vmem for index in range(len(outs))],
        scratch_shapes=list(scratch),
        input_output_aliases=aliases or {},
        compiler_params=pltpu.CompilerParams(vmem_limit_bytes=vmem_bytes),
        cost_estimate=pl.CostEstimate(flops=int(cost * 1e9), bytes_accessed=0, transcendentals=0),
    )(*args)


def one_row(ref):
    return jnp.concatenate([ref[index : index + 1, :] for index in range(ref.shape[0])], axis=1)


def route_kernel(
    n_seq,
    n_tp,
    peer,
    target_hbm,
    slide_hbm,
    tiles_hbm,
    out_hbm,
    target_ref,
    slide_ref,
    tiles_ref,
    out_ref,
    sems,
    out_sems,
):
    fetches = [
        pltpu.make_async_copy(target_hbm, target_ref, sems.at[0]),
        pltpu.make_async_copy(slide_hbm, slide_ref, sems.at[1]),
        pltpu.make_async_copy(tiles_hbm, tiles_ref, sems.at[2]),
    ]
    for fetch in fetches:
        fetch.start()
    rows = tiles_ref.shape[0]
    share = rows // n_tp
    code_rows = up_to(n_seq * up_to(peer // n_tp, 8), LANES) // LANES
    kept = stored_at(iota((1, rows), 1), rows) - lax.axis_index("tp") * share
    held = (kept >= 0) & (kept < share) & ((kept >> 7) + code_rows == (iota((n_seq * 8, rows), 0) & 7))
    kept_lane = one_hot(iota((LANES, rows), 0) == (kept & 127))
    before = one_hot(iota((LANES, LANES), 0) <= iota((LANES, LANES), 1))
    fetches[0].wait()
    chunks = tiles_ref.shape[1] // LANES
    sub = peer // n_tp
    sub_pad = up_to(sub, 8)
    blocks = n_seq * n_tp
    place, column = lax.axis_index("seq"), lax.axis_index("tp")
    target = one_row(target_ref)
    owner = jnp.floor((target.astype(F32) + 0.5) * (1.0 / rows)).astype(jnp.int32)
    flags = jnp.where(iota((n_seq, rows), 0) == owner, 1.0, 0.0)
    parts = [flags[:, at : at + LANES] for at in range(0, rows, LANES)]
    counts = dot(jnp.concatenate(parts, axis=0).astype(BF16), before)
    ahead = jnp.zeros((n_seq, 1), F32)
    slots = []
    for index, part in enumerate(parts):
        count = counts[index * n_seq : (index + 1) * n_seq]
        slots.append(jnp.sum(part * (count + ahead), axis=0, keepdims=True))
        ahead = ahead + count[:, LANES - 1 :]
    slot = jnp.concatenate(slots, axis=1).astype(jnp.int32) - 1
    lane_of = jnp.zeros_like(slot)
    for turn in range(1, n_tp):
        lane_of = lane_of + jnp.where(slot >= turn * sub, 1, 0)
    low = slot - lane_of * sub
    target_row = (owner * n_tp + lane_of) * sub_pad + low
    chooser = one_hot(iota((blocks * sub_pad, rows), 0) == target_row)

    stores = []
    fetches[1].wait()
    fetches[2].wait()
    picked = dot(chooser, tiles_ref[...])
    spot = stored_at(target - owner * rows, rows)
    high = spot >> 7
    code = ((spot & 127) + 128).astype(F32)
    for bit in range(3):
        code = code * jnp.where((high >> bit) & 1 == 1, 256.0 ** (2**bit), 1.0)
    arrival = place * sub_pad + low
    extra = n_seq * 8
    line = iota((extra, rows), 0)
    mine = (owner == (line >> 3)) & (lane_of == column) & ((arrival >> 7) == (line & 7))
    coded = dot_nt(
        jnp.where(mine, code, 0.0).astype(BF16),
        one_hot(iota((LANES, rows), 0) == (arrival & 127)),
    )
    ids = dot_nt(jnp.where(held, one_row(slide_ref).astype(F32), 0.0).astype(BF16), kept_lane)
    notes = coded + ids
    pad = out_hbm.shape[1] - chunks * sub_pad - 8
    for block in range(blocks):
        base = block * sub_pad
        pieces = [
            picked[base : base + sub_pad, part * LANES : (part + 1) * LANES] for part in range(chunks)
        ]
        start = block // n_tp * 8
        pieces.append(notes[start : start + 8])
        if pad:
            pieces.append(jnp.zeros((pad, LANES), F32))
        out_ref[block] = jnp.concatenate(pieces, axis=0).astype(BF16)
        if block % n_tp == n_tp - 1:
            some = pl.ds(block - n_tp + 1, n_tp)
            stores.append(pltpu.make_async_copy(out_ref.at[some], out_hbm.at[some], out_sems.at[block // n_tp]))
            stores[-1].start()
    for store in stores:
        store.wait()


def spread_mask(width, wide, shift):
    row = iota((width, wide), 0) - shift
    lane = iota((width, wide), 1)
    inner = lane & (SLOT - 1)
    return (inner < HEAD_DIM) & (row == (lane >> 6) * HEAD_DIM + inner)


def hint_kernel(weight_ref, out_ref):
    out_ref[...] = weight_ref[: out_ref.shape[0], : out_ref.shape[1]]


def scale_kernel(gain_ref, weight_ref, scaled_hbm, scaled_ref, sem):
    width = weight_ref.shape[0]
    same = iota((width, width), 0) == iota((width, width), 1)
    gain = jnp.sum(jnp.where(same, gain_ref[...], 0.0), axis=1, keepdims=True)
    scaled_ref[...] = (weight_ref[...].astype(F32) * gain).astype(BF16)
    store = pltpu.make_async_copy(scaled_ref, scaled_hbm, sem)
    store.start()
    store.wait()


def project_kernel(n_seq, n_tp, peer, recv_hbm, early_ref, beside_ref, *refs):
    del early_ref, beside_ref
    weight_refs = refs[:n_tp]
    stream_ref, codes_ref, ids_ref, recv_ref, sems = refs[n_tp:]
    fetches = []
    for source in range(n_seq):
        some = pl.ds(source * n_tp, n_tp)
        fetches.append(pltpu.make_async_copy(recv_hbm.at[some], recv_ref.at[some], sems.at[source]))
        fetches[-1].start()
    sub_pad = up_to(peer // n_tp, 8)
    chunks = weight_refs[0].shape[0] // LANES
    column = lax.axis_index("tp")
    code_rows = codes_ref.shape[2] // LANES
    share = ids_ref.shape[1] // n_tp
    at = chunks * sub_pad
    even = at // 16 * 16
    for fetch in fetches:
        fetch.wait()
    notes, laid = [], []
    for turn in range(n_tp):
        blocks = [recv_ref[source * n_tp + (column ^ turn)].astype(F32) for source in range(n_seq)]
        notes.append(sum(block[at : at + 8] for block in blocks))
        columns = [
            jnp.concatenate([block[part * sub_pad : (part + 1) * sub_pad] for block in blocks], axis=0).astype(BF16)
            for part in range(chunks)
        ]
        laid.append(jnp.concatenate(columns, axis=1))
    total = None
    for turn in reversed(range(n_tp)):
        part_sum = dot(laid[turn], weight_refs[turn][...])
        total = part_sum if total is None else total + part_sum
    stream_ref[...] = total.astype(BF16)
    for source in range(n_seq):
        pieces = []
        for other in range(n_tp):
            note = recv_ref[source * n_tp + other, even : even + 16, :].astype(F32)[at - even :]
            for piece in range(up_to(share, LANES) // LANES):
                length = min(LANES, share - piece * LANES)
                pieces.append(note[code_rows + piece : code_rows + piece + 1, :length])
        ids_ref[source : source + 1, :] = jnp.concatenate(pieces, axis=1)
    for turn in range(n_tp):
        codes = notes[turn]
        power = jnp.zeros((8, LANES), F32)
        scale = jnp.ones((8, LANES), F32)
        for step in range(1, 8):
            above = codes >= 128.0 * 256.0**step
            power = power + jnp.where(above, 128.0, 0.0)
            scale = scale * jnp.where(above, 1.0 / 256.0, 1.0)
        spots = jnp.where(codes > 0.0, codes * scale - 128.0 + power, -1.0)
        for piece in range(code_rows):
            codes_ref[turn, :, piece * LANES : (piece + 1) * LANES] = spots[piece : piece + 1].astype(jnp.int32)


def key_value_query(stream, gain, weights):
    rows = stream.astype(F32)
    mean = jnp.mean(rows, axis=-1, keepdims=True)
    second = jnp.mean(rows * rows, axis=-1, keepdims=True)
    normed = ((rows - mean) * lax.rsqrt(second - mean * mean + EPS) * gain).astype(BF16)
    result = dot_nt(normed, weights)
    third = weights.shape[0] // 3
    scale = jnp.where(iota((1, 3 * third), 1) >= 2 * third, HEAD_DIM ** (-0.5), 1.0)
    return (result * scale).astype(BF16)


def place_heads(turn, codes_ref, gain_ref, key_ref, value_ref, query_ref, stream_ref, rows):
    weights = jnp.concatenate([key_ref[...], value_ref[...], query_ref[...]], axis=0)
    result = key_value_query(stream_ref[...], one_row(gain_ref), weights)
    spots = codes_ref[turn]
    place = one_hot(iota((rows, spots.shape[1]), 0) == spots)[:, : result.shape[0]]
    return dot(place, result)


def first_heads_kernel(
    groups,
    codes_ref,
    gain_ref,
    key_ref,
    value_ref,
    query_ref,
    stream_ref,
    ids_ref,
    *refs,
):
    out_ref, same_ref, apart_ref, back_ref, spreads_ref = refs[:5]
    refs = refs[5:]
    rows, wide = same_ref.shape
    heads = wide // SLOT
    width = heads * HEAD_DIM
    place, column = lax.axis_index("seq"), lax.axis_index("tp")
    first = place_heads(0, codes_ref, gain_ref, key_ref, value_ref, query_ref, stream_ref, rows)
    out_ref[...] = first.astype(BF16)
    for shift in range(2):
        spreads_ref[shift] = one_hot(spread_mask(2 * width, wide, shift * width))

    ids = ids_ref[pl.ds(place, 1), :].astype(jnp.int32)
    same_ref[...] = id_lanes(ids, wide, None).astype(BF16)
    apart_ref[...] = id_lanes(ids, wide, NEG).astype(BF16)
    share = back_ref.shape[1]
    for turn in range(back_ref.shape[0]):
        wanted = stored_at((column ^ turn) * share + iota((share, 1), 0), rows)
        back_ref[turn] = one_hot(wanted == iota((share, rows), 1))
    apart_refs, apart_all = refs[:-1], refs[-1]
    for ref, (level, masks) in zip(apart_refs, groups):
        count = rows >> level
        slots = iota((count, wide), 1) >> 6
        for index, mask in enumerate(masks):
            far = ids_ref[pl.ds(place ^ mask, 1), :].astype(jnp.int32)
            apart_all[...] = id_lanes(far, wide, NEG).astype(BF16)
            chosen = None
            for head in range(heads):
                part = apart_all[pl.ds(head_start(level, head, column, rows), count), :]
                chosen = part if chosen is None else jnp.where(slots >= head, part, chosen)
            ref[index * count : (index + 1) * count, :] = chosen


def more_heads_kernel(turn, codes_ref, gain_ref, key_ref, value_ref, query_ref, stream_ref, before_ref, *refs):
    given_ref, out_ref, on_ref = refs if len(refs) == 3 else (None, refs[-1], None)
    more = place_heads(turn, codes_ref, gain_ref, key_ref, value_ref, query_ref, stream_ref, out_ref.shape[0])
    out_ref[...] = (before_ref[...].astype(F32) + more).astype(BF16)
    if on_ref is not None:
        on_ref[...] = given_ref[...]


def last_heads_kernel(
    turn, levels, codes_ref, gain_ref, key_ref, value_ref, query_ref, stream_ref, before_ref, packed, *sets
):
    rows = packed.shape[0]
    width = key_ref.shape[0]
    heads = width // HEAD_DIM
    column = lax.axis_index("tp")
    more_heads_kernel(
        turn, codes_ref, gain_ref, key_ref, value_ref, query_ref, stream_ref, before_ref, packed
    )
    for ref, level in zip(sets, levels):
        count = rows >> level
        lane = iota((count, 2 * width), 1)
        lane = jnp.where(lane >= width, lane - width, lane)
        chosen = None
        for head in range(heads):
            part = packed[pl.ds(head_start(level, head, column, rows), count), : 2 * width]
            chosen = part if chosen is None else jnp.where(lane >= head * HEAD_DIM, part, chosen)
        ref[...] = chosen


def id_lanes(ids, wide, apart):
    count = ids.shape[1]
    lane = iota((IDS, wide), 1) & (SLOT - 1)
    group = iota((IDS, wide), 0)
    same = lane - HEAD_DIM == group
    if apart is None:
        table = jnp.where(same, 1.0, 0.0)
    else:
        table = jnp.where((lane >= HEAD_DIM) & ~same, apart, 0.0)
    return dot_tn(one_hot(iota((IDS, count), 0) == ids), table.astype(BF16))


def agreement(level, group, column, rows, total, count):
    q_on, k_on = [], []
    for index, (head, first) in enumerate(group):
        for size, on in ((count, q_on), (total, k_on)):
            line, at = iota((8, size), 0), iota((8, size), 1)
            for step in range(1, size // count):
                at = at - jnp.where(iota((8, size), 1) >= step * count, count, 0)
            start = jnp.zeros((8, size), jnp.int32)
            length = jnp.zeros((8, size), jnp.int32)
            for branch in range(level, BRANCHES):
                start = jnp.where(line == branch, head_start(branch, head, column, rows) - first, start)
                length = jnp.where(line == branch, rows >> branch, length)
            on.append(jnp.where((at >= start) & (at < start + length), 1.0, 0.0))
        blank = jnp.zeros((8, count), F32)
        q_on[index] = jnp.concatenate([q_on[index] if place == index else blank for place in range(len(group))], axis=1)
    return jnp.concatenate(q_on, axis=0).astype(BF16), jnp.concatenate(k_on, axis=0).astype(BF16)


def repeat(block, times):
    return jnp.concatenate([block] * times, axis=1)


def own_kernel(packed_ref, same_ref, apart_ref, spreads_ref, acc_ref, tops_ref, masked_ref, keys_ref, values_ref):
    rows, wide = masked_ref.shape
    heads = wide // SLOT
    width = heads * HEAD_DIM
    column = lax.axis_index("tp")
    pairs = packed_ref[:, : 2 * width]
    query = dot(packed_ref[:, 2 * width :], spreads_ref[0, :width])
    masked_ref[...] = (query + same_ref[...].astype(F32)).astype(BF16)
    key = dot(pairs, spreads_ref[0])
    keys_ref[...] = (key + apart_ref[...].astype(F32)).astype(BF16)
    ones = jnp.where((iota((rows, wide), 1) & (SLOT - 1)) >= HEAD_DIM, 1.0, 0.0)
    value = dot(pairs, spreads_ref[1])
    values_ref[...] = (value + ones).astype(BF16)
    half = rows // 2
    slot_of = iota((rows, wide), 1) >> 6
    query = masked_ref[...]
    acc = None
    for head in range(heads):
        one = jnp.where(slot_of == head, query, jnp.zeros((), BF16))
        scores = dot_nt(one, keys_ref[...])
        top = jnp.max(scores, axis=1, keepdims=True)
        tops_ref[head] = jnp.broadcast_to(top, (rows, LANES))
        weights = jnp.exp(scores - top)
        start = (head & 1) * half
        times = dot_tn(*agreement(0, [(head, start)], column, rows, half, half))
        scaled = weights[start : start + half, start : start + half] * times
        others = weights[start : start + half, half - start : rows - start]
        part = jnp.concatenate([others, scaled] if start else [scaled, others], axis=1)
        rest = weights[half - start : rows - start]
        weights = jnp.concatenate([rest, part] if start else [part, rest], axis=0)
        got = dot(weights.astype(BF16), values_ref[...])
        acc = got if acc is None else jnp.where(slot_of == head, got, acc)
    acc_ref[...] = acc


def weigh_inner(weights, group, column, rows):
    count = rows >> 1
    length = rows >> 2
    head = group[0][0]
    start = head_start(2, head, column, rows) - head_start(1, head, column, rows)
    low, high = start // LANES * LANES, up_to(start + length, LANES)
    q_on, k_on = agreement(1, group, column, rows, count, count)
    part = weights[start : start + length]
    part = [part[:, :low], part[:, low:high] * dot_tn(q_on[:, start : start + length], k_on[:, low:high]), part[:, high:]]
    part = jnp.concatenate([one for one in part if one.shape[1]], axis=1)
    return jnp.concatenate([part, weights[length:]] if start == 0 else [weights[:start], part], axis=0)


def merge_sets(level, masks, sets, acc_ref, tops_ref, query_ref, spreads_ref, apart_ref):
    rows, wide = query_ref.shape
    column = lax.axis_index("tp")
    count = rows >> level
    some = min(max(1, rows // count), len(masks))
    total = some * count
    slot_of = iota((count, wide), 1) >> 6
    ones = jnp.where((iota((total, wide), 1) & (SLOT - 1)) >= HEAD_DIM, 1.0, 0.0)
    chunks = []
    for begin in range(0, len(masks), some):
        pairs = jnp.concatenate([ref[...] for ref in sets[begin : begin + some]], axis=0)
        keys = dot(pairs, spreads_ref[0]) + apart_ref[begin * count : begin * count + total, :].astype(F32)
        values = dot(pairs, spreads_ref[1]) + ones
        chunks.append((keys.astype(BF16), values.astype(BF16)))
    heads = wide // SLOT
    together = heads if heads * count * total <= 2**19 else 1
    states = []
    for low in range(0, heads, together):
        group = [(head, head_start(level, head, column, rows)) for head in range(low, low + together)]
        heres = [(head, pl.ds(first, count)) for head, first in group]
        query = [jnp.where(slot_of == head, query_ref[here, :], jnp.zeros((), BF16)) for head, here in heres]
        sums = [acc_ref[here, :] for _, here in heres]
        tops = [tops_ref[head, here, :] for head, here in heres]
        states.append((group, heres) + tuple(jnp.concatenate(parts, axis=0) for parts in (query, sums, tops)))
    merged = []
    for group, heres, query, sums, tops in states:
        inner = level == 1 and total == count and together == 1
        if not inner:
            times = dot_tn(*agreement(level, group, column, rows, total, count))
        for keys, values in chunks:
            scores = dot_nt(query, keys)
            top = jnp.maximum(tops, jnp.max(scores, axis=1, keepdims=True))
            weights = jnp.exp(scores - repeat(top, total // LANES))
            weights = weigh_inner(weights, group, column, rows) if inner else weights * times
            got = dot(weights.astype(BF16), values)
            sums = sums * repeat(jnp.exp(tops - top), wide // LANES) + got
            tops = top
        for index, (head, here) in enumerate(heres):
            part = slice(index * count, (index + 1) * count)
            merged.append((head, here, sums[part], tops[part]))
    return merged


def slot_lane(values, inner):
    wide = values.shape[1]
    row, lane = iota((wide, wide), 0), iota((wide, wide), 1)
    pick = one_hot(row == (lane >> 6) * SLOT + inner)
    high = values.astype(BF16)
    low = (values - high.astype(F32)).astype(BF16)
    return dot(high, pick) + dot(low, pick)


def near_kernel(groups, acc_ref, tops_ref, query_ref, spreads_ref, *refs):
    apart_refs, refs = refs[: len(groups)], refs[len(groups) :]
    sums_ref, new_tops_ref = refs[-2:]
    wide = query_ref.shape[1]
    del acc_ref, tops_ref

    for apart_ref, (level, masks) in zip(apart_refs, groups):
        merged = merge_sets(
            level, masks, refs[: len(masks)], sums_ref, new_tops_ref, query_ref, spreads_ref, apart_ref
        )
        refs = refs[len(masks) :]
        for head, here, sums, tops in merged:
            slot_of = iota(sums.shape, 1) >> 6
            sums_ref[here, :] = jnp.where(slot_of == head, sums, sums_ref[here, :])
            new_tops_ref[head, here, :] = tops


def mid_kernel(groups, acc_ref, tops_ref, query_ref, spreads_ref, back_ref, *refs, n_sent):
    sent_refs = refs[-n_sent:]
    refs = refs[:-n_sent]
    sums_ref, _, early_ref, centre_ref = refs[-4:]
    near_kernel(groups, acc_ref, tops_ref, query_ref, spreads_ref, *refs[:-2])
    rows, wide = query_ref.shape
    heads = wide // SLOT
    every = sums_ref[...]
    inner = iota((rows, wide), 1) & (SLOT - 1)
    attn = jnp.where(inner < HEAD_DIM, every / slot_lane(every, HEAD_DIM), 0.0)
    average = jnp.full((wide, wide), 1.0, BF16)
    centre = (dot(attn.astype(BF16), average) * (1.0 / (heads * HEAD_DIM))).astype(BF16).astype(F32)
    centre_ref[...] = centre
    early = jnp.where(inner < HEAD_DIM, attn - centre, centre).astype(BF16)
    early_ref[...] = early
    for index, ref in enumerate(sent_refs):
        ref[...] = dot(back_ref[back_ref.shape[0] - n_sent + index], early).astype(BF16)


def far_kernel(n_tp, level, masks, acc_ref, tops_ref, query_ref, spreads_ref, early_ref, centre_ref, back_ref, *refs):
    apart_ref, refs = refs[0], refs[1:]
    sets, refs = refs[: len(masks)], refs[len(masks) :]
    out_refs, message = refs[:n_tp], refs[-1]
    message[...] = early_ref[...]

    merged = merge_sets(level, masks, sets, acc_ref, tops_ref, query_ref, spreads_ref, apart_ref)
    changed = None
    for head, here, sums, _ in merged:
        lane = iota(sums.shape, 1)
        mine = (lane >= head * SLOT) & (lane < head * SLOT + HEAD_DIM)
        new = (sums / slot_lane(sums, HEAD_DIM) - centre_ref[here, :]).astype(BF16)
        message[here, :] = jnp.where(mine, new, message[here, :])
        changed = new if changed is None else jnp.where(lane >= head * SLOT, new, changed)
    final = message[...]
    rows = message.shape[0]
    count = rows >> level
    for turn in range(n_tp):
        ref = out_refs[turn]
        if ref.shape[0] == back_ref.shape[1]:
            ref[...] = dot(back_ref[turn], final).astype(BF16)
        else:
            each = rows // CLASSES
            classes = count // each
            line = iota((ref.shape[0], count), 0)
            spot = (lax.axis_index("tp") ^ turn) * (each // n_tp) + line // classes
            wanted = (line % classes) * each + spot
            pick = (iota((ref.shape[0], count), 1) == wanted) & (line < count // n_tp)
            ref[...] = dot(one_hot(pick), changed).astype(BF16)


def base_kernel(n_tp, codes_ref, *refs):
    shards, part_refs = refs[:n_tp], refs[n_tp : 2 * n_tp]
    base_ref, weights_ref = refs[-2:]
    share = base_ref.shape[0]
    wanted = stored_at(lax.axis_index("tp") * share + iota((share, 1), 0), share * n_tp)
    base = None
    for turn in range(n_tp):
        spots = codes_ref[turn]
        moved = dot(one_hot(wanted == spots)[:, : shards[turn].shape[0]], shards[turn][...])
        base = moved if base is None else base + moved
    base_ref[...] = base.astype(BF16)
    heads = weights_ref.shape[1] // SLOT
    gap = jnp.zeros((SLOT - HEAD_DIM, weights_ref.shape[2]), BF16)
    for turn, ref in enumerate(part_refs):
        for head in range(heads):
            at, to = head * HEAD_DIM, head * SLOT
            weights_ref[turn, to : to + HEAD_DIM, :] = ref[at : at + HEAD_DIM, :]
            weights_ref[turn, to + HEAD_DIM : to + SLOT, :] = gap


def mix_kernel(n_tp, level, base_ref, weights_ref, *refs):
    message_refs, change_refs, out_ref = refs[:n_tp], refs[n_tp:-1], refs[-1]
    share, wide = base_ref.shape[0], weights_ref.shape[1]
    features = n_tp * (wide // SLOT) * HEAD_DIM
    lane = iota((share, wide), 1)
    inside = (lane & (SLOT - 1)) < HEAD_DIM
    parts, centres = [], []
    for turn, ref in enumerate(message_refs):
        message = ref[...].astype(F32)
        centres.append(message[:, HEAD_DIM : HEAD_DIM + 1])
        if turn >= n_tp - len(change_refs):
            change = change_refs[turn - n_tp + len(change_refs)][...]
            count = change.shape[0]
            moved = dot(one_hot(iota((share, count), 1) == iota((share, count), 0) >> level), change)
            head = (lax.axis_index("tp") ^ turn) * (wide // SLOT) + (lane >> 6)
            late = ((iota((share, wide), 0) ^ head) & (2**level - 1)) == 0
            message = jnp.where(late, moved, message)
        parts.append(jnp.where(inside, message, 0.0))
    each = features // n_tp
    sums = [jnp.sum(part, axis=1, keepdims=True) + centre * each for part, centre in zip(parts, centres)]
    mean = sum(sums) * (1.0 / features)
    parts = [jnp.where(inside, part + (centre - mean), 0.0) for part, centre in zip(parts, centres)]
    spread = jnp.sum(sum(part * part for part in parts), axis=1, keepdims=True) * (1.0 / features)
    factor = lax.rsqrt(spread + EPS)
    total = base_ref[...].astype(F32)
    for turn, part in enumerate(parts):
        total = total + dot((part * factor).astype(BF16), weights_ref[turn])
    out_ref[...] = total.astype(BF16)


def swap(block, axis, mask):
    count = lax.axis_size(axis)
    return lax.ppermute(block, axis, [(index, index ^ mask) for index in range(count)])


def gather_tp(block):
    across = swap(block, "tp", 2)
    return [block, swap(block, "tp", 1), across, swap(across, "tp", 1)]


def body(
    tiles,
    tile_target,
    slide_id,
    proj_weight,
    norm_gain,
    query_weight,
    key_weight,
    value_weight,
    sub_gain,
    out_weight,
):
    n_seq = lax.axis_size("seq")
    n_tp = lax.axis_size("tp")
    rows, tile_width = tiles.shape
    features = proj_weight.shape[1]
    width = query_weight.shape[1]
    heads = width // HEAD_DIM
    wide = heads * SLOT
    share = rows // n_tp
    peer = rows // n_seq
    sub_pad = up_to(peer // n_tp, 8)
    arriving = n_seq * sub_pad
    chunks = tile_width // LANES
    block_rows = up_to(chunks * sub_pad + 8, 16)

    first_group = max(1, n_seq // 16)
    sizes = [min(first_group * 2**branch, n_seq) for branch in range(BRANCHES)]
    groups = []
    for level in range(BRANCHES):
        masks = tuple(range(1 if level == 0 else sizes[level - 1], sizes[level]))
        if masks:
            groups.append((level, masks))

    vmem_bytes = VMEM_BYTES if n_seq <= 8 else LARGE_VMEM_BYTES
    (blocks,) = call(
        functools.partial(route_kernel, n_seq, n_tp, peer),
        "route",
        [((n_seq * n_tp, block_rows, LANES), BF16)],
        [tile_target.reshape(-1, LANES), slide_id.reshape(-1, LANES), tiles],
        scratch=[
            pltpu.VMEM((rows // LANES, LANES), jnp.int32),
            pltpu.VMEM((rows // LANES, LANES), jnp.int32),
            pltpu.VMEM(tiles.shape, BF16),
            pltpu.VMEM((n_seq * n_tp, block_rows, LANES), BF16),
            pltpu.SemaphoreType.DMA((3,)),
            pltpu.SemaphoreType.DMA((n_seq,)),
        ],
        cost=3,
        vmem_bytes=ALL_VMEM_BYTES,
        apart=(0, 1, 2),
        out_apart=(0,),
    )
    received = lax.all_to_all(blocks, ("seq", "tp"), split_axis=0, concat_axis=0, tiled=True)
    proj_parts = gather_tp(proj_weight)
    (early,) = call(hint_kernel, "hint", [((16, LANES), BF16)], [proj_parts[-1]], cost=HINT_COST)
    (scaled,) = call(
        scale_kernel,
        "scale",
        [((width, features), BF16)],
        [sub_gain.reshape(1, width), out_weight],
        scratch=[pltpu.VMEM((width, features), BF16), pltpu.SemaphoreType.DMA],
        cost=1,
        out_apart=(0,),
    )

    beside = swap(scaled, "tp", 1)
    stream, codes, ids = call(
        functools.partial(project_kernel, n_seq, n_tp, peer),
        "project",
        [((arriving, features), BF16)]
        + [((n_tp, 1, up_to(arriving, LANES)), jnp.int32), ((n_seq, rows), F32)],
        [received, early, beside] + proj_parts,
        cost=0.5,
        scratch=[
            pltpu.VMEM(received.shape, BF16),
            pltpu.SemaphoreType.DMA((n_seq,)),
        ],
        vmem_bytes=vmem_bytes,
        apart=(0,),
    )
    shards = gather_tp(stream)

    gain = norm_gain.reshape(-1, LANES)
    weights = [gain, key_weight.T, value_weight.T, query_weight.T]
    partial, same, apart, back, spreads, *far_apart = call(
        functools.partial(first_heads_kernel, groups),
        "heads_1",
        [
            ((rows, 3 * width), BF16),
            ((rows, wide), BF16),
            ((rows, wide), BF16),
            ((n_tp, share, rows), BF16),
            ((2, 2 * width, wide), BF16),
        ]
        + [(((rows >> level) * len(masks), wide), BF16) for level, masks in groups],
        [codes] + weights + [shards[0], ids],
        scratch=[pltpu.VMEM((rows, wide), BF16)],
        vmem_bytes=vmem_bytes,
    )
    across = swap(scaled, "tp", 2)
    out_parts = [scaled, beside]
    for turn in range(1, n_tp - 1):
        given = [across] if turn == 1 else out_parts[3:]
        partial, *on = call(
            functools.partial(more_heads_kernel, turn),
            "heads_2",
            [((rows, 3 * width), BF16)] + [((width, features), BF16)] * (turn == 1),
            [codes] + weights + [shards[turn], partial] + given,
            cost=10 if turn == n_tp - 2 else 1,
            vmem_bytes=vmem_bytes,
        )
        if on:
            out_parts += on + [swap(on[0], "tp", 1)]
    packed, *sets = call(
        functools.partial(last_heads_kernel, n_tp - 1, [level for level, _ in groups]),
        "heads_3",
        [((rows, 3 * width), BF16)] + [((rows >> level, 2 * width), BF16) for level, _ in groups],
        [codes] + weights + [shards[n_tp - 1], partial],
        vmem_bytes=vmem_bytes,
    )
    sent = [[swap(one, "seq", mask) for mask in masks] for one, (_, masks) in zip(sets[:-1], groups)]
    direct = {mask: swap(sets[-1], "seq", mask) for mask in groups[-1][1] if mask % 2 == 0}
    sent.append([swap(direct[mask - 1], "seq", 1) if mask % 2 else direct[mask] for mask in groups[-1][1]])

    acc, tops, masked = call(
        own_kernel,
        "own",
        [((rows, wide), F32), ((heads, rows, LANES), F32), ((rows, wide), BF16)],
        [packed, same, apart, spreads],
        scratch=[pltpu.VMEM((rows, wide), BF16)] * 2,
        cost=0.1,
        vmem_bytes=vmem_bytes,
    )
    n_sent = n_tp - 1
    for index in range(len(groups) - 1):
        kernel, outs, given = near_kernel, [], []
        if index == len(groups) - 2:
            kernel, given = functools.partial(mid_kernel, n_sent=n_sent), [back]
            outs = [((rows, wide), BF16), ((rows, wide), F32)] + [((share, wide), BF16)] * n_sent
        acc, tops, *more = call(
            functools.partial(kernel, [groups[index]]),
            "mid" if outs else "near",
            [((rows, wide), F32), ((heads, rows, LANES), F32)] + outs,
            [acc, tops, masked, spreads] + given + [far_apart[index]] + sent[index],
            aliases={0: 0, 1: 1},
            cost=6,
            vmem_bytes=vmem_bytes,
        )
    early, centre, *ahead = more
    messages = call(
        functools.partial(far_kernel, n_tp, *groups[-1]),
        "far",
        [((share, wide), BF16)] * (n_tp - n_sent)
        + [((up_to((rows >> groups[-1][0]) // n_tp, 16), wide), BF16)] * n_sent,
        [acc, tops, masked, spreads, early, centre, back, far_apart[-1]] + sent[-1],
        scratch=[pltpu.VMEM((rows, wide), BF16)],
        vmem_bytes=vmem_bytes,
    )
    ahead = [swap(one, "tp", n_tp - n_sent + index) for index, one in enumerate(ahead)]
    arrived = [messages[0]] + [swap(messages[turn], "tp", turn) for turn in range(1, n_tp)]
    arrived = arrived[: n_tp - n_sent] + ahead + arrived[n_tp - n_sent :]
    base, padded = call(
        functools.partial(base_kernel, n_tp),
        "base",
        [((share, features), BF16), ((n_tp, wide, features), BF16)],
        [codes] + shards + out_parts,
        cost=0.3,
        vmem_bytes=vmem_bytes,
    )
    (result,) = call(
        functools.partial(mix_kernel, n_tp, groups[-1][0]),
        "mix",
        [((share, features), BF16)],
        [base, padded] + arrived,
    )
    return result


def solution(mesh):
    return jax.shard_map(
        body,
        mesh=mesh,
        in_specs=(
            P("seq", "tp"),
            P("seq"),
            P("seq"),
            P("tp", None),
            P(),
            P(None, "tp"),
            P(None, "tp"),
            P(None, "tp"),
            P("tp"),
            P("tp", None),
        ),
        out_specs=P(("seq", "tp"), None),
        check_vma=False,
    )
```

```python
import functools

import jax
import jax.numpy as jnp
from jax import lax
from jax.experimental import pallas as pl
from jax.experimental.pallas import tpu as pltpu
from jax.sharding import PartitionSpec as P

BRANCHES = 5
HEAD_DIM = 48
SLOT = 64
LANES = 128
IDS = 16
CLASSES = 2 ** (BRANCHES - 1)
NEG = -1e30
EPS = 1e-05
BF16 = jnp.bfloat16
F32 = jnp.float32
HINT_COST = 1
VMEM_BYTES = 16 * 1024 * 1024
LARGE_VMEM_BYTES = 48 * 1024 * 1024
ALL_VMEM_BYTES = 56 * 1024 * 1024


def up_to(count, step):
    return (count + step - 1) // step * step


def iota(shape, dim):
    return lax.broadcasted_iota(jnp.int32, shape, dim)


def dot(left, right):
    return jnp.dot(left, right, preferred_element_type=F32)


def dot_nt(left, right):
    return lax.dot_general(left, right, (((1,), (1,)), ((), ())), preferred_element_type=F32)


def dot_tn(left, right):
    return lax.dot_general(left, right, (((0,), (0,)), ((), ())), preferred_element_type=F32)


def one_hot(mask):
    return jnp.where(mask, 1.0, 0.0).astype(BF16)


def stored_at(position, rows):
    residue = position & (CLASSES - 1)
    flipped = jnp.zeros_like(residue)
    for bit in range(BRANCHES - 1):
        flipped = flipped + (((residue >> bit) & 1) << (BRANCHES - 2 - bit))
    return flipped * (rows // CLASSES) + (position >> (BRANCHES - 1))


def head_start(level, head, column, rows):
    start = 0
    for bit in range(level):
        value = (head >> bit) & 1 if bit < 2 else (column >> (bit - 2)) & 1
        start = start + value * (rows >> (bit + 1))
    return start


def call(kernel, name, outs, args, scratch=(), cost=1, vmem_bytes=VMEM_BYTES, apart=(), out_apart=(), aliases=None):
    vmem = pl.BlockSpec(memory_space=pltpu.VMEM)
    anywhere = pl.BlockSpec(memory_space=pltpu.HBM)
    return pl.pallas_call(
        kernel,
        name=name,
        out_shape=[jax.ShapeDtypeStruct(shape, dtype) for shape, dtype in outs],
        in_specs=[anywhere if index in apart else vmem for index in range(len(args))],
        out_specs=[anywhere if index in out_apart else vmem for index in range(len(outs))],
        scratch_shapes=list(scratch),
        input_output_aliases=aliases or {},
        compiler_params=pltpu.CompilerParams(vmem_limit_bytes=vmem_bytes),
        cost_estimate=pl.CostEstimate(flops=int(cost * 1e9), bytes_accessed=0, transcendentals=0),
    )(*args)


def one_row(ref):
    return jnp.concatenate([ref[index : index + 1, :] for index in range(ref.shape[0])], axis=1)


def route_kernel(
    n_seq,
    n_tp,
    peer,
    target_hbm,
    slide_hbm,
    tiles_hbm,
    out_hbm,
    target_ref,
    slide_ref,
    tiles_ref,
    out_ref,
    sems,
    out_sems,
):
    fetches = [
        pltpu.make_async_copy(target_hbm, target_ref, sems.at[0]),
        pltpu.make_async_copy(slide_hbm, slide_ref, sems.at[1]),
        pltpu.make_async_copy(tiles_hbm, tiles_ref, sems.at[2]),
    ]
    for fetch in fetches:
        fetch.start()
    rows = tiles_ref.shape[0]
    share = rows // n_tp
    code_rows = up_to(n_seq * up_to(peer // n_tp, 8), LANES) // LANES
    kept = stored_at(iota((1, rows), 1), rows) - lax.axis_index("tp") * share
    held = (kept >= 0) & (kept < share) & ((kept >> 7) + code_rows == (iota((n_seq * 8, rows), 0) & 7))
    kept_lane = one_hot(iota((LANES, rows), 0) == (kept & 127))
    before = one_hot(iota((LANES, LANES), 0) <= iota((LANES, LANES), 1))
    fetches[0].wait()
    chunks = tiles_ref.shape[1] // LANES
    sub = peer // n_tp
    sub_pad = up_to(sub, 8)
    blocks = n_seq * n_tp
    place, column = lax.axis_index("seq"), lax.axis_index("tp")
    target = one_row(target_ref)
    owner = jnp.floor((target.astype(F32) + 0.5) * (1.0 / rows)).astype(jnp.int32)
    flags = jnp.where(iota((n_seq, rows), 0) == owner, 1.0, 0.0)
    parts = [flags[:, at : at + LANES] for at in range(0, rows, LANES)]
    counts = dot(jnp.concatenate(parts, axis=0).astype(BF16), before)
    ahead = jnp.zeros((n_seq, 1), F32)
    slots = []
    for index, part in enumerate(parts):
        count = counts[index * n_seq : (index + 1) * n_seq]
        slots.append(jnp.sum(part * (count + ahead), axis=0, keepdims=True))
        ahead = ahead + count[:, LANES - 1 :]
    slot = jnp.concatenate(slots, axis=1).astype(jnp.int32) - 1
    lane_of = jnp.zeros_like(slot)
    for turn in range(1, n_tp):
        lane_of = lane_of + jnp.where(slot >= turn * sub, 1, 0)
    low = slot - lane_of * sub
    target_row = (owner * n_tp + lane_of) * sub_pad + low
    chooser = one_hot(iota((blocks * sub_pad, rows), 0) == target_row)

    stores = []
    fetches[1].wait()
    fetches[2].wait()
    picked = dot(chooser, tiles_ref[...])
    spot = stored_at(target - owner * rows, rows)
    high = spot >> 7
    code = ((spot & 127) + 128).astype(F32)
    for bit in range(3):
        code = code * jnp.where((high >> bit) & 1 == 1, 256.0 ** (2**bit), 1.0)
    arrival = place * sub_pad + low
    extra = n_seq * 8
    line = iota((extra, rows), 0)
    mine = (owner == (line >> 3)) & (lane_of == column) & ((arrival >> 7) == (line & 7))
    coded = dot_nt(
        jnp.where(mine, code, 0.0).astype(BF16),
        one_hot(iota((LANES, rows), 0) == (arrival & 127)),
    )
    ids = dot_nt(jnp.where(held, one_row(slide_ref).astype(F32), 0.0).astype(BF16), kept_lane)
    notes = coded + ids
    pad = out_hbm.shape[1] - chunks * sub_pad - 8
    for block in range(blocks):
        base = block * sub_pad
        pieces = [
            picked[base : base + sub_pad, part * LANES : (part + 1) * LANES] for part in range(chunks)
        ]
        start = block // n_tp * 8
        pieces.append(notes[start : start + 8])
        if pad:
            pieces.append(jnp.zeros((pad, LANES), F32))
        out_ref[block] = jnp.concatenate(pieces, axis=0).astype(BF16)
        if block % n_tp == n_tp - 1:
            some = pl.ds(block - n_tp + 1, n_tp)
            stores.append(pltpu.make_async_copy(out_ref.at[some], out_hbm.at[some], out_sems.at[block // n_tp]))
            stores[-1].start()
    for store in stores:
        store.wait()


def spread_mask(width, wide, shift):
    row = iota((width, wide), 0) - shift
    lane = iota((width, wide), 1)
    inner = lane & (SLOT - 1)
    return (inner < HEAD_DIM) & (row == (lane >> 6) * HEAD_DIM + inner)


def hint_kernel(weight_ref, out_ref):
    out_ref[...] = weight_ref[: out_ref.shape[0], : out_ref.shape[1]]


def scale_kernel(gain_ref, weight_ref, scaled_hbm, scaled_ref, sem):
    width = weight_ref.shape[0]
    same = iota((width, width), 0) == iota((width, width), 1)
    gain = jnp.sum(jnp.where(same, gain_ref[...], 0.0), axis=1, keepdims=True)
    scaled_ref[...] = (weight_ref[...].astype(F32) * gain).astype(BF16)
    store = pltpu.make_async_copy(scaled_ref, scaled_hbm, sem)
    store.start()
    store.wait()


def project_kernel(n_seq, n_tp, peer, recv_hbm, early_ref, beside_ref, *refs):
    del early_ref, beside_ref
    weight_refs = refs[:n_tp]
    stream_ref, codes_ref, ids_ref, recv_ref, sems = refs[n_tp:]
    fetches = []
    for source in range(n_seq):
        some = pl.ds(source * n_tp, n_tp)
        fetches.append(pltpu.make_async_copy(recv_hbm.at[some], recv_ref.at[some], sems.at[source]))
        fetches[-1].start()
    sub_pad = up_to(peer // n_tp, 8)
    chunks = weight_refs[0].shape[0] // LANES
    column = lax.axis_index("tp")
    code_rows = codes_ref.shape[2] // LANES
    share = ids_ref.shape[1] // n_tp
    at = chunks * sub_pad
    even = at // 16 * 16
    for fetch in fetches:
        fetch.wait()
    notes, laid = [], []
    for turn in range(n_tp):
        blocks = [recv_ref[source * n_tp + (column ^ turn)].astype(F32) for source in range(n_seq)]
        notes.append(sum(block[at : at + 8] for block in blocks))
        columns = [
            jnp.concatenate([block[part * sub_pad : (part + 1) * sub_pad] for block in blocks], axis=0).astype(BF16)
            for part in range(chunks)
        ]
        laid.append(jnp.concatenate(columns, axis=1))
    total = None
    for turn in reversed(range(n_tp)):
        part_sum = dot(laid[turn], weight_refs[turn][...])
        total = part_sum if total is None else total + part_sum
    stream_ref[...] = total.astype(BF16)
    for source in range(n_seq):
        pieces = []
        for other in range(n_tp):
            note = recv_ref[source * n_tp + other, even : even + 16, :].astype(F32)[at - even :]
            for piece in range(up_to(share, LANES) // LANES):
                length = min(LANES, share - piece * LANES)
                pieces.append(note[code_rows + piece : code_rows + piece + 1, :length])
        ids_ref[source : source + 1, :] = jnp.concatenate(pieces, axis=1)
    for turn in range(n_tp):
        codes = notes[turn]
        power = jnp.zeros((8, LANES), F32)
        scale = jnp.ones((8, LANES), F32)
        for step in range(1, 8):
            above = codes >= 128.0 * 256.0**step
            power = power + jnp.where(above, 128.0, 0.0)
            scale = scale * jnp.where(above, 1.0 / 256.0, 1.0)
        spots = jnp.where(codes > 0.0, codes * scale - 128.0 + power, -1.0)
        for piece in range(code_rows):
            codes_ref[turn, :, piece * LANES : (piece + 1) * LANES] = spots[piece : piece + 1].astype(jnp.int32)


def key_value_query(stream, gain, weights):
    rows = stream.astype(F32)
    mean = jnp.mean(rows, axis=-1, keepdims=True)
    second = jnp.mean(rows * rows, axis=-1, keepdims=True)
    normed = ((rows - mean) * lax.rsqrt(second - mean * mean + EPS) * gain).astype(BF16)
    result = dot_nt(normed, weights)
    third = weights.shape[0] // 3
    scale = jnp.where(iota((1, 3 * third), 1) >= 2 * third, HEAD_DIM ** (-0.5), 1.0)
    return (result * scale).astype(BF16)


def place_heads(turn, codes_ref, gain_ref, key_ref, value_ref, query_ref, stream_ref, rows):
    weights = jnp.concatenate([key_ref[...], value_ref[...], query_ref[...]], axis=0)
    result = key_value_query(stream_ref[...], one_row(gain_ref), weights)
    spots = codes_ref[turn]
    place = one_hot(iota((rows, spots.shape[1]), 0) == spots)[:, : result.shape[0]]
    return dot(place, result)


def first_heads_kernel(
    groups,
    codes_ref,
    gain_ref,
    key_ref,
    value_ref,
    query_ref,
    stream_ref,
    ids_ref,
    *refs,
):
    out_ref, same_ref, apart_ref, back_ref, spreads_ref = refs[:5]
    refs = refs[5:]
    rows, wide = same_ref.shape
    heads = wide // SLOT
    width = heads * HEAD_DIM
    place, column = lax.axis_index("seq"), lax.axis_index("tp")
    first = place_heads(0, codes_ref, gain_ref, key_ref, value_ref, query_ref, stream_ref, rows)
    out_ref[...] = first.astype(BF16)
    for shift in range(2):
        spreads_ref[shift] = one_hot(spread_mask(2 * width, wide, shift * width))

    ids = ids_ref[pl.ds(place, 1), :].astype(jnp.int32)
    same_ref[...] = id_lanes(ids, wide, None).astype(BF16)
    apart_ref[...] = id_lanes(ids, wide, NEG).astype(BF16)
    share = back_ref.shape[1]
    for turn in range(back_ref.shape[0]):
        wanted = stored_at((column ^ turn) * share + iota((share, 1), 0), rows)
        back_ref[turn] = one_hot(wanted == iota((share, rows), 1))
    apart_refs, apart_all = refs[:-1], refs[-1]
    for ref, (level, masks) in zip(apart_refs, groups):
        count = rows >> level
        slots = iota((count, wide), 1) >> 6
        for index, mask in enumerate(masks):
            far = ids_ref[pl.ds(place ^ mask, 1), :].astype(jnp.int32)
            apart_all[...] = id_lanes(far, wide, NEG).astype(BF16)
            chosen = None
            for head in range(heads):
                part = apart_all[pl.ds(head_start(level, head, column, rows), count), :]
                chosen = part if chosen is None else jnp.where(slots >= head, part, chosen)
            ref[index * count : (index + 1) * count, :] = chosen


def more_heads_kernel(turn, codes_ref, gain_ref, key_ref, value_ref, query_ref, stream_ref, before_ref, *refs):
    given_ref, out_ref, on_ref = refs if len(refs) == 3 else (None, refs[-1], None)
    more = place_heads(turn, codes_ref, gain_ref, key_ref, value_ref, query_ref, stream_ref, out_ref.shape[0])
    out_ref[...] = (before_ref[...].astype(F32) + more).astype(BF16)
    if on_ref is not None:
        on_ref[...] = given_ref[...]


def last_heads_kernel(
    turn, levels, codes_ref, gain_ref, key_ref, value_ref, query_ref, stream_ref, before_ref, packed, *sets
):
    rows = packed.shape[0]
    width = key_ref.shape[0]
    heads = width // HEAD_DIM
    column = lax.axis_index("tp")
    more_heads_kernel(
        turn, codes_ref, gain_ref, key_ref, value_ref, query_ref, stream_ref, before_ref, packed
    )
    for ref, level in zip(sets, levels):
        count = rows >> level
        lane = iota((count, 2 * width), 1)
        lane = jnp.where(lane >= width, lane - width, lane)
        chosen = None
        for head in range(heads):
            part = packed[pl.ds(head_start(level, head, column, rows), count), : 2 * width]
            chosen = part if chosen is None else jnp.where(lane >= head * HEAD_DIM, part, chosen)
        ref[...] = chosen


def id_lanes(ids, wide, apart):
    count = ids.shape[1]
    lane = iota((IDS, wide), 1) & (SLOT - 1)
    group = iota((IDS, wide), 0)
    same = lane - HEAD_DIM == group
    if apart is None:
        table = jnp.where(same, 1.0, 0.0)
    else:
        table = jnp.where((lane >= HEAD_DIM) & ~same, apart, 0.0)
    return dot_tn(one_hot(iota((IDS, count), 0) == ids), table.astype(BF16))


def agreement(level, group, column, rows, total, count):
    q_on, k_on = [], []
    for index, (head, first) in enumerate(group):
        for size, on in ((count, q_on), (total, k_on)):
            line, at = iota((8, size), 0), iota((8, size), 1)
            for step in range(1, size // count):
                at = at - jnp.where(iota((8, size), 1) >= step * count, count, 0)
            start = jnp.zeros((8, size), jnp.int32)
            length = jnp.zeros((8, size), jnp.int32)
            for branch in range(level, BRANCHES):
                start = jnp.where(line == branch, head_start(branch, head, column, rows) - first, start)
                length = jnp.where(line == branch, rows >> branch, length)
            on.append(jnp.where((at >= start) & (at < start + length), 1.0, 0.0))
        blank = jnp.zeros((8, count), F32)
        q_on[index] = jnp.concatenate([q_on[index] if place == index else blank for place in range(len(group))], axis=1)
    return jnp.concatenate(q_on, axis=0).astype(BF16), jnp.concatenate(k_on, axis=0).astype(BF16)


def repeat(block, times):
    return jnp.concatenate([block] * times, axis=1)


def own_kernel(packed_ref, same_ref, apart_ref, spreads_ref, acc_ref, tops_ref, masked_ref, keys_ref, values_ref):
    rows, wide = masked_ref.shape
    heads = wide // SLOT
    width = heads * HEAD_DIM
    column = lax.axis_index("tp")
    pairs = packed_ref[:, : 2 * width]
    query = dot(packed_ref[:, 2 * width :], spreads_ref[0, :width])
    masked_ref[...] = (query + same_ref[...].astype(F32)).astype(BF16)
    key = dot(pairs, spreads_ref[0])
    keys_ref[...] = (key + apart_ref[...].astype(F32)).astype(BF16)
    ones = jnp.where((iota((rows, wide), 1) & (SLOT - 1)) >= HEAD_DIM, 1.0, 0.0)
    value = dot(pairs, spreads_ref[1])
    values_ref[...] = (value + ones).astype(BF16)
    half = rows // 2
    slot_of = iota((rows, wide), 1) >> 6
    query = masked_ref[...]
    acc = None
    for head in range(heads):
        one = jnp.where(slot_of == head, query, jnp.zeros((), BF16))
        scores = dot_nt(one, keys_ref[...])
        top = jnp.max(scores, axis=1, keepdims=True)
        tops_ref[head] = jnp.broadcast_to(top, (rows, LANES))
        weights = jnp.exp(scores - top)
        start = (head & 1) * half
        times = dot_tn(*agreement(0, [(head, start)], column, rows, half, half))
        scaled = weights[start : start + half, start : start + half] * times
        others = weights[start : start + half, half - start : rows - start]
        part = jnp.concatenate([others, scaled] if start else [scaled, others], axis=1)
        rest = weights[half - start : rows - start]
        weights = jnp.concatenate([rest, part] if start else [part, rest], axis=0)
        got = dot(weights.astype(BF16), values_ref[...])
        acc = got if acc is None else jnp.where(slot_of == head, got, acc)
    acc_ref[...] = acc


def weigh_inner(weights, group, column, rows):
    count = rows >> 1
    length = rows >> 2
    head = group[0][0]
    start = head_start(2, head, column, rows) - head_start(1, head, column, rows)
    low, high = start // LANES * LANES, up_to(start + length, LANES)
    q_on, k_on = agreement(1, group, column, rows, count, count)
    part = weights[start : start + length]
    part = [part[:, :low], part[:, low:high] * dot_tn(q_on[:, start : start + length], k_on[:, low:high]), part[:, high:]]
    part = jnp.concatenate([one for one in part if one.shape[1]], axis=1)
    return jnp.concatenate([part, weights[length:]] if start == 0 else [weights[:start], part], axis=0)


def merge_sets(level, masks, sets, acc_ref, tops_ref, query_ref, spreads_ref, apart_ref):
    rows, wide = query_ref.shape
    column = lax.axis_index("tp")
    count = rows >> level
    some = min(max(1, rows // count), len(masks))
    total = some * count
    slot_of = iota((count, wide), 1) >> 6
    ones = jnp.where((iota((total, wide), 1) & (SLOT - 1)) >= HEAD_DIM, 1.0, 0.0)
    chunks = []
    for begin in range(0, len(masks), some):
        pairs = jnp.concatenate([ref[...] for ref in sets[begin : begin + some]], axis=0)
        keys = dot(pairs, spreads_ref[0]) + apart_ref[begin * count : begin * count + total, :].astype(F32)
        values = dot(pairs, spreads_ref[1]) + ones
        chunks.append((keys.astype(BF16), values.astype(BF16)))
    heads = wide // SLOT
    together = heads if heads * count * total <= 2**19 else 1
    states = []
    for low in range(0, heads, together):
        group = [(head, head_start(level, head, column, rows)) for head in range(low, low + together)]
        heres = [(head, pl.ds(first, count)) for head, first in group]
        query = [jnp.where(slot_of == head, query_ref[here, :], jnp.zeros((), BF16)) for head, here in heres]
        sums = [acc_ref[here, :] for _, here in heres]
        tops = [tops_ref[head, here, :] for head, here in heres]
        states.append((group, heres) + tuple(jnp.concatenate(parts, axis=0) for parts in (query, sums, tops)))
    merged = []
    for group, heres, query, sums, tops in states:
        inner = level == 1 and total == count and together == 1
        if not inner:
            times = dot_tn(*agreement(level, group, column, rows, total, count))
        for keys, values in chunks:
            scores = dot_nt(query, keys)
            top = jnp.maximum(tops, jnp.max(scores, axis=1, keepdims=True))
            weights = jnp.exp(scores - repeat(top, total // LANES))
            weights = weigh_inner(weights, group, column, rows) if inner else weights * times
            got = dot(weights.astype(BF16), values)
            sums = sums * repeat(jnp.exp(tops - top), wide // LANES) + got
            tops = top
        for index, (head, here) in enumerate(heres):
            part = slice(index * count, (index + 1) * count)
            merged.append((head, here, sums[part], tops[part]))
    return merged


def slot_lane(values, inner):
    wide = values.shape[1]
    row, lane = iota((wide, wide), 0), iota((wide, wide), 1)
    pick = one_hot(row == (lane >> 6) * SLOT + inner)
    high = values.astype(BF16)
    low = (values - high.astype(F32)).astype(BF16)
    return dot(high, pick) + dot(low, pick)


def near_kernel(groups, acc_ref, tops_ref, query_ref, spreads_ref, *refs):
    apart_refs, refs = refs[: len(groups)], refs[len(groups) :]
    sums_ref, new_tops_ref = refs[-2:]
    wide = query_ref.shape[1]
    del acc_ref, tops_ref

    for apart_ref, (level, masks) in zip(apart_refs, groups):
        merged = merge_sets(
            level, masks, refs[: len(masks)], sums_ref, new_tops_ref, query_ref, spreads_ref, apart_ref
        )
        refs = refs[len(masks) :]
        for head, here, sums, tops in merged:
            slot_of = iota(sums.shape, 1) >> 6
            sums_ref[here, :] = jnp.where(slot_of == head, sums, sums_ref[here, :])
            new_tops_ref[head, here, :] = tops


def mid_kernel(groups, acc_ref, tops_ref, query_ref, spreads_ref, back_ref, *refs, n_sent):
    sent_refs = refs[-n_sent:]
    refs = refs[:-n_sent]
    sums_ref, _, early_ref, centre_ref = refs[-4:]
    near_kernel(groups, acc_ref, tops_ref, query_ref, spreads_ref, *refs[:-2])
    rows, wide = query_ref.shape
    heads = wide // SLOT
    every = sums_ref[...]
    inner = iota((rows, wide), 1) & (SLOT - 1)
    attn = jnp.where(inner < HEAD_DIM, every / slot_lane(every, HEAD_DIM), 0.0)
    average = jnp.full((wide, wide), 1.0, BF16)
    centre = (dot(attn.astype(BF16), average) * (1.0 / (heads * HEAD_DIM))).astype(BF16).astype(F32)
    centre_ref[...] = centre
    early = jnp.where(inner < HEAD_DIM, attn - centre, centre).astype(BF16)
    early_ref[...] = early
    for index, ref in enumerate(sent_refs):
        share = back_ref.shape[1]
        ref[:share] = dot(back_ref[back_ref.shape[0] - n_sent + index], early).astype(BF16)
        ref[share:] = jnp.zeros((ref.shape[0] - share, ref.shape[1]), BF16)


def far_kernel(n_tp, level, masks, acc_ref, tops_ref, query_ref, spreads_ref, early_ref, centre_ref, back_ref, *refs):
    apart_ref, refs = refs[0], refs[1:]
    sets, refs = refs[: len(masks)], refs[len(masks) :]
    out_refs, message = refs[:n_tp], refs[-1]
    message[...] = early_ref[...]

    merged = merge_sets(level, masks, sets, acc_ref, tops_ref, query_ref, spreads_ref, apart_ref)
    changed = None
    for head, here, sums, _ in merged:
        lane = iota(sums.shape, 1)
        mine = (lane >= head * SLOT) & (lane < head * SLOT + HEAD_DIM)
        new = (sums / slot_lane(sums, HEAD_DIM) - centre_ref[here, :]).astype(BF16)
        message[here, :] = jnp.where(mine, new, message[here, :])
        changed = new if changed is None else jnp.where(lane >= head * SLOT, new, changed)
    final = message[...]
    rows = message.shape[0]
    count = rows >> level
    for turn in range(n_tp):
        ref = out_refs[turn]
        if ref.shape[0] == back_ref.shape[1]:
            ref[...] = dot(back_ref[turn], final).astype(BF16)
        else:
            each = rows // CLASSES
            classes = count // each
            line = iota((ref.shape[0], count), 0)
            spot = (lax.axis_index("tp") ^ turn) * (each // n_tp) + line // classes
            wanted = (line % classes) * each + spot
            pick = (iota((ref.shape[0], count), 1) == wanted) & (line < count // n_tp)
            ref[...] = dot(one_hot(pick), changed).astype(BF16)


def base_kernel(n_tp, codes_ref, *refs):
    shards, part_refs = refs[:n_tp], refs[n_tp : 2 * n_tp]
    base_ref, weights_ref = refs[-2:]
    share = base_ref.shape[0]
    wanted = stored_at(lax.axis_index("tp") * share + iota((share, 1), 0), share * n_tp)
    base = None
    for turn in range(n_tp):
        spots = codes_ref[turn]
        moved = dot(one_hot(wanted == spots)[:, : shards[turn].shape[0]], shards[turn][...])
        base = moved if base is None else base + moved
    base_ref[...] = base.astype(BF16)
    heads = weights_ref.shape[1] // SLOT
    gap = jnp.zeros((SLOT - HEAD_DIM, weights_ref.shape[2]), BF16)
    for turn, ref in enumerate(part_refs):
        for head in range(heads):
            at, to = head * HEAD_DIM, head * SLOT
            weights_ref[turn, to : to + HEAD_DIM, :] = ref[at : at + HEAD_DIM, :]
            weights_ref[turn, to + HEAD_DIM : to + SLOT, :] = gap


def mix_kernel(n_tp, level, base_ref, weights_ref, *refs):
    message_refs, change_refs, out_ref = refs[:n_tp], refs[n_tp:-1], refs[-1]
    share, wide = base_ref.shape[0], weights_ref.shape[1]
    features = n_tp * (wide // SLOT) * HEAD_DIM
    lane = iota((share, wide), 1)
    inside = (lane & (SLOT - 1)) < HEAD_DIM
    parts, centres = [], []
    for turn, ref in enumerate(message_refs):
        message = ref[:share].astype(F32)
        centres.append(message[:, HEAD_DIM : HEAD_DIM + 1])
        if turn >= n_tp - len(change_refs):
            change = change_refs[turn - n_tp + len(change_refs)][...]
            count = change.shape[0]
            moved = dot(one_hot(iota((share, count), 1) == iota((share, count), 0) >> level), change)
            head = (lax.axis_index("tp") ^ turn) * (wide // SLOT) + (lane >> 6)
            late = ((iota((share, wide), 0) ^ head) & (2**level - 1)) == 0
            message = jnp.where(late, moved, message)
        parts.append(jnp.where(inside, message, 0.0))
    each = features // n_tp
    sums = [jnp.sum(part, axis=1, keepdims=True) + centre * each for part, centre in zip(parts, centres)]
    mean = sum(sums) * (1.0 / features)
    parts = [jnp.where(inside, part + (centre - mean), 0.0) for part, centre in zip(parts, centres)]
    spread = jnp.sum(sum(part * part for part in parts), axis=1, keepdims=True) * (1.0 / features)
    factor = lax.rsqrt(spread + EPS)
    total = base_ref[...].astype(F32)
    for turn, part in enumerate(parts):
        total = total + dot((part * factor).astype(BF16), weights_ref[turn])
    out_ref[...] = total.astype(BF16)


def swap(block, axis, mask):
    count = lax.axis_size(axis)
    return lax.ppermute(block, axis, [(index, index ^ mask) for index in range(count)])


def gather_tp(block):
    across = swap(block, "tp", 2)
    return [block, swap(block, "tp", 1), across, swap(across, "tp", 1)]


def body(
    tiles,
    tile_target,
    slide_id,
    proj_weight,
    norm_gain,
    query_weight,
    key_weight,
    value_weight,
    sub_gain,
    out_weight,
):
    n_seq = lax.axis_size("seq")
    n_tp = lax.axis_size("tp")
    rows, tile_width = tiles.shape
    features = proj_weight.shape[1]
    width = query_weight.shape[1]
    heads = width // HEAD_DIM
    wide = heads * SLOT
    share = rows // n_tp
    peer = rows // n_seq
    sub_pad = up_to(peer // n_tp, 8)
    arriving = n_seq * sub_pad
    chunks = tile_width // LANES
    block_rows = up_to(chunks * sub_pad + 8, 16)

    first_group = max(1, n_seq // 16)
    sizes = [min(first_group * 2**branch, n_seq) for branch in range(BRANCHES)]
    groups = []
    for level in range(BRANCHES):
        masks = tuple(range(1 if level == 0 else sizes[level - 1], sizes[level]))
        if masks:
            groups.append((level, masks))

    vmem_bytes = VMEM_BYTES if n_seq <= 8 else LARGE_VMEM_BYTES
    (blocks,) = call(
        functools.partial(route_kernel, n_seq, n_tp, peer),
        "route",
        [((n_seq * n_tp, block_rows, LANES), BF16)],
        [tile_target.reshape(-1, LANES), slide_id.reshape(-1, LANES), tiles],
        scratch=[
            pltpu.VMEM((rows // LANES, LANES), jnp.int32),
            pltpu.VMEM((rows // LANES, LANES), jnp.int32),
            pltpu.VMEM(tiles.shape, BF16),
            pltpu.VMEM((n_seq * n_tp, block_rows, LANES), BF16),
            pltpu.SemaphoreType.DMA((3,)),
            pltpu.SemaphoreType.DMA((n_seq,)),
        ],
        cost=3,
        vmem_bytes=ALL_VMEM_BYTES,
        apart=(0, 1, 2),
        out_apart=(0,),
    )
    received = lax.all_to_all(blocks, ("seq", "tp"), split_axis=0, concat_axis=0, tiled=True)
    proj_parts = gather_tp(proj_weight)
    (early,) = call(hint_kernel, "hint", [((16, LANES), BF16)], [proj_parts[-1]], cost=HINT_COST)
    (scaled,) = call(
        scale_kernel,
        "scale",
        [((width, features), BF16)],
        [sub_gain.reshape(1, width), out_weight],
        scratch=[pltpu.VMEM((width, features), BF16), pltpu.SemaphoreType.DMA],
        cost=1,
        out_apart=(0,),
    )

    beside = swap(scaled, "tp", 1)
    stream, codes, ids = call(
        functools.partial(project_kernel, n_seq, n_tp, peer),
        "project",
        [((arriving, features), BF16)]
        + [((n_tp, 1, up_to(arriving, LANES)), jnp.int32), ((n_seq, rows), F32)],
        [received, early, beside] + proj_parts,
        cost=0.5,
        scratch=[
            pltpu.VMEM(received.shape, BF16),
            pltpu.SemaphoreType.DMA((n_seq,)),
        ],
        vmem_bytes=vmem_bytes,
        apart=(0,),
    )
    shards = gather_tp(stream)

    gain = norm_gain.reshape(-1, LANES)
    weights = [gain, key_weight.T, value_weight.T, query_weight.T]
    partial, same, apart, back, spreads, *far_apart = call(
        functools.partial(first_heads_kernel, groups),
        "heads_1",
        [
            ((rows, 3 * width), BF16),
            ((rows, wide), BF16),
            ((rows, wide), BF16),
            ((n_tp, share, rows), BF16),
            ((2, 2 * width, wide), BF16),
        ]
        + [(((rows >> level) * len(masks), wide), BF16) for level, masks in groups],
        [codes] + weights + [shards[0], ids],
        scratch=[pltpu.VMEM((rows, wide), BF16)],
        vmem_bytes=vmem_bytes,
    )
    across = swap(scaled, "tp", 2)
    out_parts = [scaled, beside]
    for turn in range(1, n_tp - 1):
        given = [across] if turn == 1 else out_parts[3:]
        partial, *on = call(
            functools.partial(more_heads_kernel, turn),
            "heads_2",
            [((rows, 3 * width), BF16)] + [((width, features), BF16)] * (turn == 1),
            [codes] + weights + [shards[turn], partial] + given,
            cost=10 if turn == n_tp - 2 else 1,
            vmem_bytes=vmem_bytes,
        )
        if on:
            out_parts += on + [swap(on[0], "tp", 1)]
    packed, *sets = call(
        functools.partial(last_heads_kernel, n_tp - 1, [level for level, _ in groups]),
        "heads_3",
        [((rows, 3 * width), BF16)] + [((rows >> level, 2 * width), BF16) for level, _ in groups],
        [codes] + weights + [shards[n_tp - 1], partial],
        vmem_bytes=vmem_bytes,
    )
    sent = [[swap(one, "seq", mask) for mask in masks] for one, (_, masks) in zip(sets[:-1], groups)]
    direct = {mask: swap(sets[-1], "seq", mask) for mask in groups[-1][1] if mask % 2 == 0}
    sent.append([swap(direct[mask - 1], "seq", 1) if mask % 2 else direct[mask] for mask in groups[-1][1]])

    acc, tops, masked = call(
        own_kernel,
        "own",
        [((rows, wide), F32), ((heads, rows, LANES), F32), ((rows, wide), BF16)],
        [packed, same, apart, spreads],
        scratch=[pltpu.VMEM((rows, wide), BF16)] * 2,
        cost=0.1,
        vmem_bytes=vmem_bytes,
    )
    n_sent = n_tp // 2
    for index in range(len(groups) - 1):
        kernel, outs, given = near_kernel, [], []
        if index == len(groups) - 2:
            kernel, given = functools.partial(mid_kernel, n_sent=n_sent), [back]
            outs = [((rows, wide), BF16), ((rows, wide), F32)] + [((share + 16, wide), BF16)] * n_sent
        acc, tops, *more = call(
            functools.partial(kernel, [groups[index]]),
            "mid" if outs else "near",
            [((rows, wide), F32), ((heads, rows, LANES), F32)] + outs,
            [acc, tops, masked, spreads] + given + [far_apart[index]] + sent[index],
            aliases={0: 0, 1: 1},
            cost=6,
            vmem_bytes=vmem_bytes,
        )
    early, centre, *ahead = more
    messages = call(
        functools.partial(far_kernel, n_tp, *groups[-1]),
        "far",
        [((share, wide), BF16)] * (n_tp - n_sent)
        + [((up_to((rows >> groups[-1][0]) // n_tp, 16), wide), BF16)] * n_sent,
        [acc, tops, masked, spreads, early, centre, back, far_apart[-1]] + sent[-1],
        scratch=[pltpu.VMEM((rows, wide), BF16)],
        vmem_bytes=vmem_bytes,
    )
    ahead = [swap(one, "tp", n_tp - n_sent + index) for index, one in enumerate(ahead)]
    arrived = [messages[0]] + [swap(messages[turn], "tp", turn) for turn in range(1, n_tp)]
    arrived = arrived[: n_tp - n_sent] + ahead + arrived[n_tp - n_sent :]
    base, padded = call(
        functools.partial(base_kernel, n_tp),
        "base",
        [((share, features), BF16), ((n_tp, wide, features), BF16)],
        [codes] + shards + out_parts,
        cost=0.3,
        vmem_bytes=vmem_bytes,
    )
    (result,) = call(
        functools.partial(mix_kernel, n_tp, groups[-1][0]),
        "mix",
        [((share, features), BF16)],
        [base, padded] + arrived,
    )
    return result


def solution(mesh):
    return jax.shard_map(
        body,
        mesh=mesh,
        in_specs=(
            P("seq", "tp"),
            P("seq"),
            P("seq"),
            P("tp", None),
            P(),
            P(None, "tp"),
            P(None, "tp"),
            P(None, "tp"),
            P("tp"),
            P("tp", None),
        ),
        out_specs=P(("seq", "tp"), None),
        check_vma=False,
    )
```

```python
import functools

import jax
import jax.numpy as jnp
from jax import lax
from jax.experimental import pallas as pl
from jax.experimental.pallas import tpu as pltpu
from jax.sharding import PartitionSpec as P

BRANCHES = 5
HEAD_DIM = 48
SLOT = 64
LANES = 128
IDS = 16
CLASSES = 2 ** (BRANCHES - 1)
NEG = -1e30
EPS = 1e-05
BF16 = jnp.bfloat16
F32 = jnp.float32
HINT_COST = 1
VMEM_BYTES = 16 * 1024 * 1024
LARGE_VMEM_BYTES = 48 * 1024 * 1024
ALL_VMEM_BYTES = 56 * 1024 * 1024


def up_to(count, step):
    return (count + step - 1) // step * step


def iota(shape, dim):
    return lax.broadcasted_iota(jnp.int32, shape, dim)


def dot(left, right):
    return jnp.dot(left, right, preferred_element_type=F32)


def dot_nt(left, right):
    return lax.dot_general(left, right, (((1,), (1,)), ((), ())), preferred_element_type=F32)


def dot_tn(left, right):
    return lax.dot_general(left, right, (((0,), (0,)), ((), ())), preferred_element_type=F32)


def one_hot(mask):
    return jnp.where(mask, 1.0, 0.0).astype(BF16)


def stored_at(position, rows):
    residue = position & (CLASSES - 1)
    flipped = jnp.zeros_like(residue)
    for bit in range(BRANCHES - 1):
        flipped = flipped + (((residue >> bit) & 1) << (BRANCHES - 2 - bit))
    return flipped * (rows // CLASSES) + (position >> (BRANCHES - 1))


def head_start(level, head, column, rows):
    start = 0
    for bit in range(level):
        value = (head >> bit) & 1 if bit < 2 else (column >> (bit - 2)) & 1
        start = start + value * (rows >> (bit + 1))
    return start


def call(kernel, name, outs, args, scratch=(), cost=1, vmem_bytes=VMEM_BYTES, apart=(), out_apart=(), aliases=None):
    vmem = pl.BlockSpec(memory_space=pltpu.VMEM)
    anywhere = pl.BlockSpec(memory_space=pltpu.HBM)
    return pl.pallas_call(
        kernel,
        name=name,
        out_shape=[jax.ShapeDtypeStruct(shape, dtype) for shape, dtype in outs],
        in_specs=[anywhere if index in apart else vmem for index in range(len(args))],
        out_specs=[anywhere if index in out_apart else vmem for index in range(len(outs))],
        scratch_shapes=list(scratch),
        input_output_aliases=aliases or {},
        compiler_params=pltpu.CompilerParams(vmem_limit_bytes=vmem_bytes),
        cost_estimate=pl.CostEstimate(flops=int(cost * 1e9), bytes_accessed=0, transcendentals=0),
    )(*args)


def one_row(ref):
    return jnp.concatenate([ref[index : index + 1, :] for index in range(ref.shape[0])], axis=1)


def route_kernel(
    n_seq,
    n_tp,
    peer,
    target_hbm,
    slide_hbm,
    tiles_hbm,
    out_hbm,
    target_ref,
    slide_ref,
    tiles_ref,
    out_ref,
    sems,
    out_sems,
):
    fetches = [
        pltpu.make_async_copy(target_hbm, target_ref, sems.at[0]),
        pltpu.make_async_copy(slide_hbm, slide_ref, sems.at[1]),
        pltpu.make_async_copy(tiles_hbm, tiles_ref, sems.at[2]),
    ]
    for fetch in fetches:
        fetch.start()
    rows = tiles_ref.shape[0]
    share = rows // n_tp
    code_rows = up_to(n_seq * up_to(peer // n_tp, 8), LANES) // LANES
    kept = stored_at(iota((1, rows), 1), rows) - lax.axis_index("tp") * share
    held = (kept >= 0) & (kept < share) & ((kept >> 7) + code_rows == (iota((n_seq * 8, rows), 0) & 7))
    kept_lane = one_hot(iota((LANES, rows), 0) == (kept & 127))
    before = one_hot(iota((LANES, LANES), 0) <= iota((LANES, LANES), 1))
    fetches[0].wait()
    chunks = tiles_ref.shape[1] // LANES
    sub = peer // n_tp
    sub_pad = up_to(sub, 8)
    blocks = n_seq * n_tp
    place, column = lax.axis_index("seq"), lax.axis_index("tp")
    target = one_row(target_ref)
    owner = jnp.floor((target.astype(F32) + 0.5) * (1.0 / rows)).astype(jnp.int32)
    flags = jnp.where(iota((n_seq, rows), 0) == owner, 1.0, 0.0)
    parts = [flags[:, at : at + LANES] for at in range(0, rows, LANES)]
    counts = dot(jnp.concatenate(parts, axis=0).astype(BF16), before)
    ahead = jnp.zeros((n_seq, 1), F32)
    slots = []
    for index, part in enumerate(parts):
        count = counts[index * n_seq : (index + 1) * n_seq]
        slots.append(jnp.sum(part * (count + ahead), axis=0, keepdims=True))
        ahead = ahead + count[:, LANES - 1 :]
    slot = jnp.concatenate(slots, axis=1).astype(jnp.int32) - 1
    lane_of = jnp.zeros_like(slot)
    for turn in range(1, n_tp):
        lane_of = lane_of + jnp.where(slot >= turn * sub, 1, 0)
    low = slot - lane_of * sub
    target_row = (owner * n_tp + lane_of) * sub_pad + low
    chooser = one_hot(iota((blocks * sub_pad, rows), 0) == target_row)

    stores = []
    fetches[1].wait()
    fetches[2].wait()
    picked = dot(chooser, tiles_ref[...])
    spot = stored_at(target - owner * rows, rows)
    high = spot >> 7
    code = ((spot & 127) + 128).astype(F32)
    for bit in range(3):
        code = code * jnp.where((high >> bit) & 1 == 1, 256.0 ** (2**bit), 1.0)
    arrival = place * sub_pad + low
    extra = n_seq * 8
    line = iota((extra, rows), 0)
    mine = (owner == (line >> 3)) & (lane_of == column) & ((arrival >> 7) == (line & 7))
    coded = dot_nt(
        jnp.where(mine, code, 0.0).astype(BF16),
        one_hot(iota((LANES, rows), 0) == (arrival & 127)),
    )
    ids = dot_nt(jnp.where(held, one_row(slide_ref).astype(F32), 0.0).astype(BF16), kept_lane)
    notes = coded + ids
    pad = out_hbm.shape[1] - chunks * sub_pad - 8
    for block in range(blocks):
        base = block * sub_pad
        pieces = [
            picked[base : base + sub_pad, part * LANES : (part + 1) * LANES] for part in range(chunks)
        ]
        start = block // n_tp * 8
        pieces.append(notes[start : start + 8])
        if pad:
            pieces.append(jnp.zeros((pad, LANES), F32))
        out_ref[block] = jnp.concatenate(pieces, axis=0).astype(BF16)
        if block % n_tp == n_tp - 1:
            some = pl.ds(block - n_tp + 1, n_tp)
            stores.append(pltpu.make_async_copy(out_ref.at[some], out_hbm.at[some], out_sems.at[block // n_tp]))
            stores[-1].start()
    for store in stores:
        store.wait()


def spread_mask(width, wide, shift):
    row = iota((width, wide), 0) - shift
    lane = iota((width, wide), 1)
    inner = lane & (SLOT - 1)
    return (inner < HEAD_DIM) & (row == (lane >> 6) * HEAD_DIM + inner)


def hint_kernel(weight_ref, out_ref):
    out_ref[...] = weight_ref[: out_ref.shape[0], : out_ref.shape[1]]


def scale_kernel(gain_ref, weight_ref, scaled_hbm, scaled_ref, sem):
    width = weight_ref.shape[0]
    same = iota((width, width), 0) == iota((width, width), 1)
    gain = jnp.sum(jnp.where(same, gain_ref[...], 0.0), axis=1, keepdims=True)
    scaled_ref[...] = (weight_ref[...].astype(F32) * gain).astype(BF16)
    store = pltpu.make_async_copy(scaled_ref, scaled_hbm, sem)
    store.start()
    store.wait()


def project_kernel(n_seq, n_tp, peer, recv_hbm, early_ref, beside_ref, *refs):
    del early_ref, beside_ref
    weight_refs = refs[:n_tp]
    stream_ref, codes_ref, ids_ref, recv_ref, sems = refs[n_tp:]
    fetches = []
    for source in range(n_seq):
        some = pl.ds(source * n_tp, n_tp)
        fetches.append(pltpu.make_async_copy(recv_hbm.at[some], recv_ref.at[some], sems.at[source]))
        fetches[-1].start()
    sub_pad = up_to(peer // n_tp, 8)
    chunks = weight_refs[0].shape[0] // LANES
    column = lax.axis_index("tp")
    code_rows = codes_ref.shape[2] // LANES
    share = ids_ref.shape[1] // n_tp
    at = chunks * sub_pad
    even = at // 16 * 16
    for fetch in fetches:
        fetch.wait()
    notes, laid = [], []
    for turn in range(n_tp):
        blocks = [recv_ref[source * n_tp + (column ^ turn)].astype(F32) for source in range(n_seq)]
        notes.append(sum(block[at : at + 8] for block in blocks))
        columns = [
            jnp.concatenate([block[part * sub_pad : (part + 1) * sub_pad] for block in blocks], axis=0).astype(BF16)
            for part in range(chunks)
        ]
        laid.append(jnp.concatenate(columns, axis=1))
    total = None
    for turn in reversed(range(n_tp)):
        part_sum = dot(laid[turn], weight_refs[turn][...])
        total = part_sum if total is None else total + part_sum
    stream_ref[...] = total.astype(BF16)
    for source in range(n_seq):
        pieces = []
        for other in range(n_tp):
            note = recv_ref[source * n_tp + other, even : even + 16, :].astype(F32)[at - even :]
            for piece in range(up_to(share, LANES) // LANES):
                length = min(LANES, share - piece * LANES)
                pieces.append(note[code_rows + piece : code_rows + piece + 1, :length])
        ids_ref[source : source + 1, :] = jnp.concatenate(pieces, axis=1)
    for turn in range(n_tp):
        codes = notes[turn]
        power = jnp.zeros((8, LANES), F32)
        scale = jnp.ones((8, LANES), F32)
        for step in range(1, 8):
            above = codes >= 128.0 * 256.0**step
            power = power + jnp.where(above, 128.0, 0.0)
            scale = scale * jnp.where(above, 1.0 / 256.0, 1.0)
        spots = jnp.where(codes > 0.0, codes * scale - 128.0 + power, -1.0)
        for piece in range(code_rows):
            codes_ref[turn, :, piece * LANES : (piece + 1) * LANES] = spots[piece : piece + 1].astype(jnp.int32)


def key_value_query(stream, gain, weights):
    rows = stream.astype(F32)
    mean = jnp.mean(rows, axis=-1, keepdims=True)
    second = jnp.mean(rows * rows, axis=-1, keepdims=True)
    normed = ((rows - mean) * lax.rsqrt(second - mean * mean + EPS) * gain).astype(BF16)
    result = dot_nt(normed, weights)
    third = weights.shape[0] // 3
    scale = jnp.where(iota((1, 3 * third), 1) >= 2 * third, HEAD_DIM ** (-0.5), 1.0)
    return (result * scale).astype(BF16)


def place_heads(turn, codes_ref, gain_ref, key_ref, value_ref, query_ref, stream_ref, rows):
    weights = jnp.concatenate([key_ref[...], value_ref[...], query_ref[...]], axis=0)
    result = key_value_query(stream_ref[...], one_row(gain_ref), weights)
    spots = codes_ref[turn]
    place = one_hot(iota((rows, spots.shape[1]), 0) == spots)[:, : result.shape[0]]
    return dot(place, result)


def first_heads_kernel(
    groups,
    codes_ref,
    gain_ref,
    key_ref,
    value_ref,
    query_ref,
    stream_ref,
    ids_ref,
    *refs,
):
    out_ref, same_ref, apart_ref, back_ref, spreads_ref = refs[:5]
    refs = refs[5:]
    rows, wide = same_ref.shape
    heads = wide // SLOT
    width = heads * HEAD_DIM
    place, column = lax.axis_index("seq"), lax.axis_index("tp")
    first = place_heads(0, codes_ref, gain_ref, key_ref, value_ref, query_ref, stream_ref, rows)
    out_ref[...] = first.astype(BF16)
    for shift in range(2):
        spreads_ref[shift] = one_hot(spread_mask(2 * width, wide, shift * width))

    ids = ids_ref[pl.ds(place, 1), :].astype(jnp.int32)
    same_ref[...] = id_lanes(ids, wide, None).astype(BF16)
    apart_ref[...] = id_lanes(ids, wide, NEG).astype(BF16)
    share = back_ref.shape[1]
    for turn in range(back_ref.shape[0]):
        wanted = stored_at((column ^ turn) * share + iota((share, 1), 0), rows)
        back_ref[turn] = one_hot(wanted == iota((share, rows), 1))
    apart_refs, apart_all = refs[:-1], refs[-1]
    for ref, (level, masks) in zip(apart_refs, groups):
        count = rows >> level
        slots = iota((count, wide), 1) >> 6
        for index, mask in enumerate(masks):
            far = ids_ref[pl.ds(place ^ mask, 1), :].astype(jnp.int32)
            apart_all[...] = id_lanes(far, wide, NEG).astype(BF16)
            chosen = None
            for head in range(heads):
                part = apart_all[pl.ds(head_start(level, head, column, rows), count), :]
                chosen = part if chosen is None else jnp.where(slots >= head, part, chosen)
            ref[index * count : (index + 1) * count, :] = chosen


def more_heads_kernel(turn, codes_ref, gain_ref, key_ref, value_ref, query_ref, stream_ref, before_ref, *refs):
    given_ref, out_ref, on_ref = refs if len(refs) == 3 else (None, refs[-1], None)
    more = place_heads(turn, codes_ref, gain_ref, key_ref, value_ref, query_ref, stream_ref, out_ref.shape[0])
    out_ref[...] = (before_ref[...].astype(F32) + more).astype(BF16)
    if on_ref is not None:
        on_ref[...] = given_ref[...]


def last_heads_kernel(
    turn, levels, codes_ref, gain_ref, key_ref, value_ref, query_ref, stream_ref, before_ref, packed, *sets
):
    rows = packed.shape[0]
    width = key_ref.shape[0]
    heads = width // HEAD_DIM
    column = lax.axis_index("tp")
    more_heads_kernel(
        turn, codes_ref, gain_ref, key_ref, value_ref, query_ref, stream_ref, before_ref, packed
    )
    for ref, level in zip(sets, levels):
        count = rows >> level
        lane = iota((count, 2 * width), 1)
        lane = jnp.where(lane >= width, lane - width, lane)
        chosen = None
        for head in range(heads):
            part = packed[pl.ds(head_start(level, head, column, rows), count), : 2 * width]
            chosen = part if chosen is None else jnp.where(lane >= head * HEAD_DIM, part, chosen)
        ref[...] = chosen


def id_lanes(ids, wide, apart):
    count = ids.shape[1]
    lane = iota((IDS, wide), 1) & (SLOT - 1)
    group = iota((IDS, wide), 0)
    same = lane - HEAD_DIM == group
    if apart is None:
        table = jnp.where(same, 1.0, 0.0)
    else:
        table = jnp.where((lane >= HEAD_DIM) & ~same, apart, 0.0)
    return dot_tn(one_hot(iota((IDS, count), 0) == ids), table.astype(BF16))


def agreement(level, group, column, rows, total, count):
    q_on, k_on = [], []
    for index, (head, first) in enumerate(group):
        for size, on in ((count, q_on), (total, k_on)):
            line, at = iota((8, size), 0), iota((8, size), 1)
            for step in range(1, size // count):
                at = at - jnp.where(iota((8, size), 1) >= step * count, count, 0)
            start = jnp.zeros((8, size), jnp.int32)
            length = jnp.zeros((8, size), jnp.int32)
            for branch in range(level, BRANCHES):
                start = jnp.where(line == branch, head_start(branch, head, column, rows) - first, start)
                length = jnp.where(line == branch, rows >> branch, length)
            on.append(jnp.where((at >= start) & (at < start + length), 1.0, 0.0))
        blank = jnp.zeros((8, count), F32)
        q_on[index] = jnp.concatenate([q_on[index] if place == index else blank for place in range(len(group))], axis=1)
    return jnp.concatenate(q_on, axis=0).astype(BF16), jnp.concatenate(k_on, axis=0).astype(BF16)


def repeat(block, times):
    return jnp.concatenate([block] * times, axis=1)


def own_kernel(packed_ref, same_ref, apart_ref, spreads_ref, acc_ref, tops_ref, masked_ref, keys_ref, values_ref):
    rows, wide = masked_ref.shape
    heads = wide // SLOT
    width = heads * HEAD_DIM
    column = lax.axis_index("tp")
    pairs = packed_ref[:, : 2 * width]
    query = dot(packed_ref[:, 2 * width :], spreads_ref[0, :width])
    masked_ref[...] = (query + same_ref[...].astype(F32)).astype(BF16)
    key = dot(pairs, spreads_ref[0])
    keys_ref[...] = (key + apart_ref[...].astype(F32)).astype(BF16)
    ones = jnp.where((iota((rows, wide), 1) & (SLOT - 1)) >= HEAD_DIM, 1.0, 0.0)
    value = dot(pairs, spreads_ref[1])
    values_ref[...] = (value + ones).astype(BF16)
    half = rows // 2
    slot_of = iota((rows, wide), 1) >> 6
    query = masked_ref[...]
    acc = None
    for head in range(heads):
        one = jnp.where(slot_of == head, query, jnp.zeros((), BF16))
        scores = dot_nt(one, keys_ref[...])
        top = jnp.max(scores, axis=1, keepdims=True)
        tops_ref[head] = jnp.broadcast_to(top, (rows, LANES))
        weights = jnp.exp(scores - top)
        start = (head & 1) * half
        times = dot_tn(*agreement(0, [(head, start)], column, rows, half, half))
        scaled = weights[start : start + half, start : start + half] * times
        others = weights[start : start + half, half - start : rows - start]
        part = jnp.concatenate([others, scaled] if start else [scaled, others], axis=1)
        rest = weights[half - start : rows - start]
        weights = jnp.concatenate([rest, part] if start else [part, rest], axis=0)
        got = dot(weights.astype(BF16), values_ref[...])
        acc = got if acc is None else jnp.where(slot_of == head, got, acc)
    acc_ref[...] = acc


def weigh_inner(weights, group, column, rows):
    count = rows >> 1
    length = rows >> 2
    head = group[0][0]
    start = head_start(2, head, column, rows) - head_start(1, head, column, rows)
    low, high = start // LANES * LANES, up_to(start + length, LANES)
    q_on, k_on = agreement(1, group, column, rows, count, count)
    part = weights[start : start + length]
    part = [part[:, :low], part[:, low:high] * dot_tn(q_on[:, start : start + length], k_on[:, low:high]), part[:, high:]]
    part = jnp.concatenate([one for one in part if one.shape[1]], axis=1)
    return jnp.concatenate([part, weights[length:]] if start == 0 else [weights[:start], part], axis=0)


def merge_sets(level, masks, sets, acc_ref, tops_ref, query_ref, spreads_ref, apart_ref):
    rows, wide = query_ref.shape
    column = lax.axis_index("tp")
    count = rows >> level
    some = min(max(1, rows // count), len(masks))
    total = some * count
    slot_of = iota((count, wide), 1) >> 6
    ones = jnp.where((iota((total, wide), 1) & (SLOT - 1)) >= HEAD_DIM, 1.0, 0.0)
    chunks = []
    for begin in range(0, len(masks), some):
        pairs = jnp.concatenate([ref[...] for ref in sets[begin : begin + some]], axis=0)
        keys = dot(pairs, spreads_ref[0]) + apart_ref[begin * count : begin * count + total, :].astype(F32)
        values = dot(pairs, spreads_ref[1]) + ones
        chunks.append((keys.astype(BF16), values.astype(BF16)))
    heads = wide // SLOT
    together = heads if heads * count * total <= 2**19 else 1
    states = []
    for low in range(0, heads, together):
        group = [(head, head_start(level, head, column, rows)) for head in range(low, low + together)]
        heres = [(head, pl.ds(first, count)) for head, first in group]
        query = [jnp.where(slot_of == head, query_ref[here, :], jnp.zeros((), BF16)) for head, here in heres]
        sums = [acc_ref[here, :] for _, here in heres]
        tops = [tops_ref[head, here, :] for head, here in heres]
        states.append((group, heres) + tuple(jnp.concatenate(parts, axis=0) for parts in (query, sums, tops)))
    merged = []
    for group, heres, query, sums, tops in states:
        inner = level == 1 and total == count and together == 1
        if not inner:
            times = dot_tn(*agreement(level, group, column, rows, total, count))
        for keys, values in chunks:
            scores = dot_nt(query, keys)
            top = jnp.maximum(tops, jnp.max(scores, axis=1, keepdims=True))
            weights = jnp.exp(scores - repeat(top, total // LANES))
            weights = weigh_inner(weights, group, column, rows) if inner else weights * times
            got = dot(weights.astype(BF16), values)
            sums = sums * repeat(jnp.exp(tops - top), wide // LANES) + got
            tops = top
        for index, (head, here) in enumerate(heres):
            part = slice(index * count, (index + 1) * count)
            merged.append((head, here, sums[part], tops[part]))
    return merged


def slot_lane(values, inner):
    wide = values.shape[1]
    row, lane = iota((wide, wide), 0), iota((wide, wide), 1)
    pick = one_hot(row == (lane >> 6) * SLOT + inner)
    high = values.astype(BF16)
    low = (values - high.astype(F32)).astype(BF16)
    return dot(high, pick) + dot(low, pick)


def near_kernel(groups, acc_ref, tops_ref, query_ref, spreads_ref, *refs):
    apart_refs, refs = refs[: len(groups)], refs[len(groups) :]
    sums_ref, new_tops_ref = refs[-2:]
    wide = query_ref.shape[1]
    del acc_ref, tops_ref

    for apart_ref, (level, masks) in zip(apart_refs, groups):
        merged = merge_sets(
            level, masks, refs[: len(masks)], sums_ref, new_tops_ref, query_ref, spreads_ref, apart_ref
        )
        refs = refs[len(masks) :]
        for head, here, sums, tops in merged:
            slot_of = iota(sums.shape, 1) >> 6
            sums_ref[here, :] = jnp.where(slot_of == head, sums, sums_ref[here, :])
            new_tops_ref[head, here, :] = tops


def mid_kernel(groups, acc_ref, tops_ref, query_ref, spreads_ref, back_ref, *refs, n_sent):
    sent_refs = refs[-n_sent:]
    refs = refs[:-n_sent]
    sums_ref, _, early_ref, centre_ref = refs[-4:]
    near_kernel(groups, acc_ref, tops_ref, query_ref, spreads_ref, *refs[:-2])
    rows, wide = query_ref.shape
    heads = wide // SLOT
    every = sums_ref[...]
    inner = iota((rows, wide), 1) & (SLOT - 1)
    attn = jnp.where(inner < HEAD_DIM, every / slot_lane(every, HEAD_DIM), 0.0)
    average = jnp.full((wide, wide), 1.0, BF16)
    centre = (dot(attn.astype(BF16), average) * (1.0 / (heads * HEAD_DIM))).astype(BF16).astype(F32)
    centre_ref[...] = centre
    early = jnp.where(inner < HEAD_DIM, attn - centre, centre).astype(BF16)
    early_ref[...] = early
    for index, ref in enumerate(sent_refs):
        share = back_ref.shape[1]
        ref[:share] = dot(back_ref[back_ref.shape[0] - n_sent + index], early).astype(BF16)
        ref[share:] = jnp.zeros((ref.shape[0] - share, ref.shape[1]), BF16)


def far_kernel(n_tp, level, masks, acc_ref, tops_ref, query_ref, spreads_ref, early_ref, centre_ref, back_ref, *refs):
    apart_ref, refs = refs[0], refs[1:]
    sets, refs = refs[: len(masks)], refs[len(masks) :]
    out_refs, message = refs[:n_tp], refs[-1]
    message[...] = early_ref[...]

    merged = merge_sets(level, masks, sets, acc_ref, tops_ref, query_ref, spreads_ref, apart_ref)
    changed = None
    stacked = jnp.concatenate([sums for _, _, sums, _ in merged], axis=0)
    stacked = stacked / slot_lane(stacked, HEAD_DIM)
    for index, (head, here, sums, _) in enumerate(merged):
        lane = iota(sums.shape, 1)
        length = sums.shape[0]
        mine = (lane >= head * SLOT) & (lane < head * SLOT + HEAD_DIM)
        new = (stacked[index * length : (index + 1) * length] - centre_ref[here, :]).astype(BF16)
        message[here, :] = jnp.where(mine, new, message[here, :])
        changed = new if changed is None else jnp.where(lane >= head * SLOT, new, changed)
    final = message[...]
    rows = message.shape[0]
    count = rows >> level
    for turn in range(n_tp):
        ref = out_refs[turn]
        if ref.shape[0] == back_ref.shape[1]:
            ref[...] = dot(back_ref[turn], final).astype(BF16)
        else:
            each = rows // CLASSES
            classes = count // each
            line = iota((ref.shape[0], count), 0)
            spot = (lax.axis_index("tp") ^ turn) * (each // n_tp) + line // classes
            wanted = (line % classes) * each + spot
            pick = (iota((ref.shape[0], count), 1) == wanted) & (line < count // n_tp)
            ref[...] = dot(one_hot(pick), changed).astype(BF16)


def base_kernel(n_tp, codes_ref, *refs):
    shards, part_refs = refs[:n_tp], refs[n_tp : 2 * n_tp]
    base_ref, weights_ref = refs[-2:]
    share = base_ref.shape[0]
    wanted = stored_at(lax.axis_index("tp") * share + iota((share, 1), 0), share * n_tp)
    base = None
    for turn in range(n_tp):
        spots = codes_ref[turn]
        moved = dot(one_hot(wanted == spots)[:, : shards[turn].shape[0]], shards[turn][...])
        base = moved if base is None else base + moved
    base_ref[...] = base.astype(BF16)
    heads = weights_ref.shape[1] // SLOT
    gap = jnp.zeros((SLOT - HEAD_DIM, weights_ref.shape[2]), BF16)
    for turn, ref in enumerate(part_refs):
        for head in range(heads):
            at, to = head * HEAD_DIM, head * SLOT
            weights_ref[turn, to : to + HEAD_DIM, :] = ref[at : at + HEAD_DIM, :]
            weights_ref[turn, to + HEAD_DIM : to + SLOT, :] = gap


def mix_kernel(n_tp, level, base_ref, weights_ref, *refs):
    message_refs, change_refs, out_ref = refs[:n_tp], refs[n_tp:-1], refs[-1]
    share, wide = base_ref.shape[0], weights_ref.shape[1]
    features = n_tp * (wide // SLOT) * HEAD_DIM
    lane = iota((share, wide), 1)
    inside = (lane & (SLOT - 1)) < HEAD_DIM
    parts, centres = [], []
    for turn, ref in enumerate(message_refs):
        message = ref[:share].astype(F32)
        centres.append(message[:, HEAD_DIM : HEAD_DIM + 1])
        if turn >= n_tp - len(change_refs):
            change = change_refs[turn - n_tp + len(change_refs)][...]
            count = change.shape[0]
            moved = dot(one_hot(iota((share, count), 1) == iota((share, count), 0) >> level), change)
            head = (lax.axis_index("tp") ^ turn) * (wide // SLOT) + (lane >> 6)
            late = ((iota((share, wide), 0) ^ head) & (2**level - 1)) == 0
            message = jnp.where(late, moved, message)
        parts.append(jnp.where(inside, message, 0.0))
    each = features // n_tp
    mean = (jnp.sum(sum(parts), axis=1, keepdims=True) + sum(centres) * each) * (1.0 / features)
    parts = [jnp.where(inside, part + (centre - mean), 0.0) for part, centre in zip(parts, centres)]
    spread = jnp.sum(sum(part * part for part in parts), axis=1, keepdims=True) * (1.0 / features)
    factor = lax.rsqrt(spread + EPS)
    total = base_ref[...].astype(F32)
    for turn, part in enumerate(parts):
        total = total + dot((part * factor).astype(BF16), weights_ref[turn])
    out_ref[...] = total.astype(BF16)


def swap(block, axis, mask):
    count = lax.axis_size(axis)
    return lax.ppermute(block, axis, [(index, index ^ mask) for index in range(count)])


def gather_tp(block):
    across = swap(block, "tp", 2)
    return [block, swap(block, "tp", 1), across, swap(across, "tp", 1)]


def body(
    tiles,
    tile_target,
    slide_id,
    proj_weight,
    norm_gain,
    query_weight,
    key_weight,
    value_weight,
    sub_gain,
    out_weight,
):
    n_seq = lax.axis_size("seq")
    n_tp = lax.axis_size("tp")
    rows, tile_width = tiles.shape
    features = proj_weight.shape[1]
    width = query_weight.shape[1]
    heads = width // HEAD_DIM
    wide = heads * SLOT
    share = rows // n_tp
    peer = rows // n_seq
    sub_pad = up_to(peer // n_tp, 8)
    arriving = n_seq * sub_pad
    chunks = tile_width // LANES
    block_rows = up_to(chunks * sub_pad + 8, 16)

    first_group = max(1, n_seq // 16)
    sizes = [min(first_group * 2**branch, n_seq) for branch in range(BRANCHES)]
    groups = []
    for level in range(BRANCHES):
        masks = tuple(range(1 if level == 0 else sizes[level - 1], sizes[level]))
        if masks:
            groups.append((level, masks))

    vmem_bytes = VMEM_BYTES if n_seq <= 8 else LARGE_VMEM_BYTES
    (blocks,) = call(
        functools.partial(route_kernel, n_seq, n_tp, peer),
        "route",
        [((n_seq * n_tp, block_rows, LANES), BF16)],
        [tile_target.reshape(-1, LANES), slide_id.reshape(-1, LANES), tiles],
        scratch=[
            pltpu.VMEM((rows // LANES, LANES), jnp.int32),
            pltpu.VMEM((rows // LANES, LANES), jnp.int32),
            pltpu.VMEM(tiles.shape, BF16),
            pltpu.VMEM((n_seq * n_tp, block_rows, LANES), BF16),
            pltpu.SemaphoreType.DMA((3,)),
            pltpu.SemaphoreType.DMA((n_seq,)),
        ],
        cost=3,
        vmem_bytes=ALL_VMEM_BYTES,
        apart=(0, 1, 2),
        out_apart=(0,),
    )
    received = lax.all_to_all(blocks, ("seq", "tp"), split_axis=0, concat_axis=0, tiled=True)
    proj_parts = gather_tp(proj_weight)
    (early,) = call(hint_kernel, "hint", [((16, LANES), BF16)], [proj_parts[-1]], cost=HINT_COST)
    (scaled,) = call(
        scale_kernel,
        "scale",
        [((width, features), BF16)],
        [sub_gain.reshape(1, width), out_weight],
        scratch=[pltpu.VMEM((width, features), BF16), pltpu.SemaphoreType.DMA],
        cost=1,
        out_apart=(0,),
    )

    beside = swap(scaled, "tp", 1)
    stream, codes, ids = call(
        functools.partial(project_kernel, n_seq, n_tp, peer),
        "project",
        [((arriving, features), BF16)]
        + [((n_tp, 1, up_to(arriving, LANES)), jnp.int32), ((n_seq, rows), F32)],
        [received, early, beside] + proj_parts,
        cost=0.5,
        scratch=[
            pltpu.VMEM(received.shape, BF16),
            pltpu.SemaphoreType.DMA((n_seq,)),
        ],
        vmem_bytes=vmem_bytes,
        apart=(0,),
    )
    shards = gather_tp(stream)

    gain = norm_gain.reshape(-1, LANES)
    weights = [gain, key_weight.T, value_weight.T, query_weight.T]
    partial, same, apart, back, spreads, *far_apart = call(
        functools.partial(first_heads_kernel, groups),
        "heads_1",
        [
            ((rows, 3 * width), BF16),
            ((rows, wide), BF16),
            ((rows, wide), BF16),
            ((n_tp, share, rows), BF16),
            ((2, 2 * width, wide), BF16),
        ]
        + [(((rows >> level) * len(masks), wide), BF16) for level, masks in groups],
        [codes] + weights + [shards[0], ids],
        scratch=[pltpu.VMEM((rows, wide), BF16)],
        vmem_bytes=vmem_bytes,
    )
    across = swap(scaled, "tp", 2)
    out_parts = [scaled, beside]
    for turn in range(1, n_tp - 1):
        given = [across] if turn == 1 else out_parts[3:]
        partial, *on = call(
            functools.partial(more_heads_kernel, turn),
            "heads_2",
            [((rows, 3 * width), BF16)] + [((width, features), BF16)] * (turn == 1),
            [codes] + weights + [shards[turn], partial] + given,
            cost=10 if turn == n_tp - 2 else 1,
            vmem_bytes=vmem_bytes,
        )
        if on:
            out_parts += on + [swap(on[0], "tp", 1)]
    packed, *sets = call(
        functools.partial(last_heads_kernel, n_tp - 1, [level for level, _ in groups]),
        "heads_3",
        [((rows, 3 * width), BF16)] + [((rows >> level, 2 * width), BF16) for level, _ in groups],
        [codes] + weights + [shards[n_tp - 1], partial],
        vmem_bytes=vmem_bytes,
    )
    sent = [[swap(one, "seq", mask) for mask in masks] for one, (_, masks) in zip(sets[:-1], groups)]
    direct = {mask: swap(sets[-1], "seq", mask) for mask in groups[-1][1] if mask % 2 == 0}
    sent.append([swap(direct[mask - 1], "seq", 1) if mask % 2 else direct[mask] for mask in groups[-1][1]])

    acc, tops, masked = call(
        own_kernel,
        "own",
        [((rows, wide), F32), ((heads, rows, LANES), F32), ((rows, wide), BF16)],
        [packed, same, apart, spreads],
        scratch=[pltpu.VMEM((rows, wide), BF16)] * 2,
        cost=0.1,
        vmem_bytes=vmem_bytes,
    )
    n_sent = n_tp // 2
    for index in range(len(groups) - 1):
        kernel, outs, given = near_kernel, [], []
        if index == len(groups) - 2:
            kernel, given = functools.partial(mid_kernel, n_sent=n_sent), [back]
            outs = [((rows, wide), BF16), ((rows, wide), F32)] + [((share + 16, wide), BF16)] * n_sent
        acc, tops, *more = call(
            functools.partial(kernel, [groups[index]]),
            "mid" if outs else "near",
            [((rows, wide), F32), ((heads, rows, LANES), F32)] + outs,
            [acc, tops, masked, spreads] + given + [far_apart[index]] + sent[index],
            aliases={0: 0, 1: 1},
            cost=6,
            vmem_bytes=vmem_bytes,
        )
    early, centre, *ahead = more
    messages = call(
        functools.partial(far_kernel, n_tp, *groups[-1]),
        "far",
        [((share, wide), BF16)] * (n_tp - n_sent)
        + [((up_to((rows >> groups[-1][0]) // n_tp, 16), wide), BF16)] * n_sent,
        [acc, tops, masked, spreads, early, centre, back, far_apart[-1]] + sent[-1],
        scratch=[pltpu.VMEM((rows, wide), BF16)],
        vmem_bytes=vmem_bytes,
    )
    ahead = [swap(one, "tp", n_tp - n_sent + index) for index, one in enumerate(ahead)]
    arrived = [messages[0]] + [swap(messages[turn], "tp", turn) for turn in range(1, n_tp)]
    arrived = arrived[: n_tp - n_sent] + ahead + arrived[n_tp - n_sent :]
    base, padded = call(
        functools.partial(base_kernel, n_tp),
        "base",
        [((share, features), BF16), ((n_tp, wide, features), BF16)],
        [codes] + shards + out_parts,
        cost=0.3,
        vmem_bytes=vmem_bytes,
    )
    (result,) = call(
        functools.partial(mix_kernel, n_tp, groups[-1][0]),
        "mix",
        [((share, features), BF16)],
        [base, padded] + arrived,
    )
    return result


def solution(mesh):
    return jax.shard_map(
        body,
        mesh=mesh,
        in_specs=(
            P("seq", "tp"),
            P("seq"),
            P("seq"),
            P("tp", None),
            P(),
            P(None, "tp"),
            P(None, "tp"),
            P(None, "tp"),
            P("tp"),
            P("tp", None),
        ),
        out_specs=P(("seq", "tp"), None),
        check_vma=False,
    )
```

```python
import functools

import jax
import jax.numpy as jnp
from jax import lax
from jax.experimental import pallas as pl
from jax.experimental.pallas import tpu as pltpu
from jax.sharding import PartitionSpec as P

BRANCHES = 5
HEAD_DIM = 48
SLOT = 64
LANES = 128
IDS = 16
CLASSES = 2 ** (BRANCHES - 1)
NEG = -1e30
EPS = 1e-05
BF16 = jnp.bfloat16
F32 = jnp.float32
HINT_COST = 1
VMEM_BYTES = 16 * 1024 * 1024
LARGE_VMEM_BYTES = 48 * 1024 * 1024
ALL_VMEM_BYTES = 56 * 1024 * 1024


def up_to(count, step):
    return (count + step - 1) // step * step


def iota(shape, dim):
    return lax.broadcasted_iota(jnp.int32, shape, dim)


def dot(left, right):
    return jnp.dot(left, right, preferred_element_type=F32)


def dot_nt(left, right):
    return lax.dot_general(left, right, (((1,), (1,)), ((), ())), preferred_element_type=F32)


def dot_tn(left, right):
    return lax.dot_general(left, right, (((0,), (0,)), ((), ())), preferred_element_type=F32)


def one_hot(mask):
    return jnp.where(mask, 1.0, 0.0).astype(BF16)


def stored_at(position, rows):
    residue = position & (CLASSES - 1)
    flipped = jnp.zeros_like(residue)
    for bit in range(BRANCHES - 1):
        flipped = flipped + (((residue >> bit) & 1) << (BRANCHES - 2 - bit))
    return flipped * (rows // CLASSES) + (position >> (BRANCHES - 1))


def head_start(level, head, column, rows):
    start = 0
    for bit in range(level):
        value = (head >> bit) & 1 if bit < 2 else (column >> (bit - 2)) & 1
        start = start + value * (rows >> (bit + 1))
    return start


def call(kernel, name, outs, args, scratch=(), cost=1, vmem_bytes=VMEM_BYTES, apart=(), out_apart=(), aliases=None):
    vmem = pl.BlockSpec(memory_space=pltpu.VMEM)
    anywhere = pl.BlockSpec(memory_space=pltpu.HBM)
    return pl.pallas_call(
        kernel,
        name=name,
        out_shape=[jax.ShapeDtypeStruct(shape, dtype) for shape, dtype in outs],
        in_specs=[anywhere if index in apart else vmem for index in range(len(args))],
        out_specs=[anywhere if index in out_apart else vmem for index in range(len(outs))],
        scratch_shapes=list(scratch),
        input_output_aliases=aliases or {},
        compiler_params=pltpu.CompilerParams(vmem_limit_bytes=vmem_bytes),
        cost_estimate=pl.CostEstimate(flops=int(cost * 1e9), bytes_accessed=0, transcendentals=0),
    )(*args)


def one_row(ref):
    return jnp.concatenate([ref[index : index + 1, :] for index in range(ref.shape[0])], axis=1)


def route_kernel(
    n_seq,
    n_tp,
    peer,
    target_hbm,
    slide_hbm,
    tiles_hbm,
    out_hbm,
    target_ref,
    slide_ref,
    tiles_ref,
    out_ref,
    sems,
    out_sems,
):
    fetches = [
        pltpu.make_async_copy(target_hbm, target_ref, sems.at[0]),
        pltpu.make_async_copy(slide_hbm, slide_ref, sems.at[1]),
        pltpu.make_async_copy(tiles_hbm, tiles_ref, sems.at[2]),
    ]
    for fetch in fetches:
        fetch.start()
    rows = tiles_ref.shape[0]
    share = rows // n_tp
    code_rows = up_to(n_seq * up_to(peer // n_tp, 8), LANES) // LANES
    kept = stored_at(iota((1, rows), 1), rows) - lax.axis_index("tp") * share
    held = (kept >= 0) & (kept < share) & ((kept >> 7) + code_rows == (iota((n_seq * 8, rows), 0) & 7))
    kept_lane = one_hot(iota((LANES, rows), 0) == (kept & 127))
    before = one_hot(iota((LANES, LANES), 0) <= iota((LANES, LANES), 1))
    fetches[0].wait()
    chunks = tiles_ref.shape[1] // LANES
    sub = peer // n_tp
    sub_pad = up_to(sub, 8)
    blocks = n_seq * n_tp
    place, column = lax.axis_index("seq"), lax.axis_index("tp")
    target = one_row(target_ref)
    owner = jnp.floor((target.astype(F32) + 0.5) * (1.0 / rows)).astype(jnp.int32)
    flags = jnp.where(iota((n_seq, rows), 0) == owner, 1.0, 0.0)
    parts = [flags[:, at : at + LANES] for at in range(0, rows, LANES)]
    counts = dot(jnp.concatenate(parts, axis=0).astype(BF16), before)
    ahead = jnp.zeros((n_seq, 1), F32)
    slots = []
    for index, part in enumerate(parts):
        count = counts[index * n_seq : (index + 1) * n_seq]
        slots.append(jnp.sum(part * (count + ahead), axis=0, keepdims=True))
        ahead = ahead + count[:, LANES - 1 :]
    slot = jnp.concatenate(slots, axis=1).astype(jnp.int32) - 1
    lane_of = jnp.zeros_like(slot)
    for turn in range(1, n_tp):
        lane_of = lane_of + jnp.where(slot >= turn * sub, 1, 0)
    low = slot - lane_of * sub
    target_row = (owner * n_tp + lane_of) * sub_pad + low
    chooser = one_hot(iota((blocks * sub_pad, rows), 0) == target_row)

    stores = []
    fetches[1].wait()
    fetches[2].wait()
    picked = dot(chooser, tiles_ref[...])
    spot = stored_at(target - owner * rows, rows)
    high = spot >> 7
    code = ((spot & 127) + 128).astype(F32)
    for bit in range(3):
        code = code * jnp.where((high >> bit) & 1 == 1, 256.0 ** (2**bit), 1.0)
    arrival = place * sub_pad + low
    extra = n_seq * 8
    line = iota((extra, rows), 0)
    mine = (owner == (line >> 3)) & (lane_of == column) & ((arrival >> 7) == (line & 7))
    coded = dot_nt(
        jnp.where(mine, code, 0.0).astype(BF16),
        one_hot(iota((LANES, rows), 0) == (arrival & 127)),
    )
    ids = dot_nt(jnp.where(held, one_row(slide_ref).astype(F32), 0.0).astype(BF16), kept_lane)
    notes = coded + ids
    pad = out_hbm.shape[1] - chunks * sub_pad - 8
    for block in range(blocks):
        base = block * sub_pad
        pieces = [
            picked[base : base + sub_pad, part * LANES : (part + 1) * LANES] for part in range(chunks)
        ]
        start = block // n_tp * 8
        pieces.append(notes[start : start + 8])
        if pad:
            pieces.append(jnp.zeros((pad, LANES), F32))
        out_ref[block] = jnp.concatenate(pieces, axis=0).astype(BF16)
        if block % n_tp == n_tp - 1:
            some = pl.ds(block - n_tp + 1, n_tp)
            stores.append(pltpu.make_async_copy(out_ref.at[some], out_hbm.at[some], out_sems.at[block // n_tp]))
            stores[-1].start()
    for store in stores:
        store.wait()


def spread_mask(width, wide, shift):
    row = iota((width, wide), 0) - shift
    lane = iota((width, wide), 1)
    inner = lane & (SLOT - 1)
    return (inner < HEAD_DIM) & (row == (lane >> 6) * HEAD_DIM + inner)


def hint_kernel(weight_ref, out_ref):
    out_ref[...] = weight_ref[: out_ref.shape[0], : out_ref.shape[1]]


def scale_kernel(gain_ref, weight_ref, scaled_hbm, scaled_ref, sem):
    width = weight_ref.shape[0]
    same = iota((width, width), 0) == iota((width, width), 1)
    gain = jnp.sum(jnp.where(same, gain_ref[...], 0.0), axis=1, keepdims=True)
    scaled_ref[...] = (weight_ref[...].astype(F32) * gain).astype(BF16)
    store = pltpu.make_async_copy(scaled_ref, scaled_hbm, sem)
    store.start()
    store.wait()


def project_kernel(n_seq, n_tp, peer, recv_hbm, early_ref, beside_ref, *refs):
    del early_ref, beside_ref
    weight_refs = refs[:n_tp]
    stream_ref, codes_ref, ids_ref, recv_ref, sems = refs[n_tp:]
    fetches = []
    for source in range(n_seq):
        some = pl.ds(source * n_tp, n_tp)
        fetches.append(pltpu.make_async_copy(recv_hbm.at[some], recv_ref.at[some], sems.at[source]))
        fetches[-1].start()
    sub_pad = up_to(peer // n_tp, 8)
    chunks = weight_refs[0].shape[0] // LANES
    column = lax.axis_index("tp")
    code_rows = codes_ref.shape[2] // LANES
    share = ids_ref.shape[1] // n_tp
    at = chunks * sub_pad
    even = at // 16 * 16
    for fetch in fetches:
        fetch.wait()
    notes, laid = [], []
    for turn in range(n_tp):
        blocks = [recv_ref[source * n_tp + (column ^ turn)].astype(F32) for source in range(n_seq)]
        notes.append(sum(block[at : at + 8] for block in blocks))
        columns = [
            jnp.concatenate([block[part * sub_pad : (part + 1) * sub_pad] for block in blocks], axis=0).astype(BF16)
            for part in range(chunks)
        ]
        laid.append(jnp.concatenate(columns, axis=1))
    total = None
    for turn in reversed(range(n_tp)):
        part_sum = dot(laid[turn], weight_refs[turn][...])
        total = part_sum if total is None else total + part_sum
    stream_ref[...] = total.astype(BF16)
    for source in range(n_seq):
        pieces = []
        for other in range(n_tp):
            note = recv_ref[source * n_tp + other, even : even + 16, :].astype(F32)[at - even :]
            for piece in range(up_to(share, LANES) // LANES):
                length = min(LANES, share - piece * LANES)
                pieces.append(note[code_rows + piece : code_rows + piece + 1, :length])
        ids_ref[source : source + 1, :] = jnp.concatenate(pieces, axis=1)
    for turn in range(n_tp):
        codes = notes[turn]
        power = jnp.zeros((8, LANES), F32)
        scale = jnp.ones((8, LANES), F32)
        for step in range(1, 8):
            above = codes >= 128.0 * 256.0**step
            power = power + jnp.where(above, 128.0, 0.0)
            scale = scale * jnp.where(above, 1.0 / 256.0, 1.0)
        spots = jnp.where(codes > 0.0, codes * scale - 128.0 + power, -1.0)
        for piece in range(code_rows):
            codes_ref[turn, :, piece * LANES : (piece + 1) * LANES] = spots[piece : piece + 1].astype(jnp.int32)


def key_value_query(stream, gain, weights):
    rows = stream.astype(F32)
    mean = jnp.mean(rows, axis=-1, keepdims=True)
    second = jnp.mean(rows * rows, axis=-1, keepdims=True)
    normed = ((rows - mean) * lax.rsqrt(second - mean * mean + EPS) * gain).astype(BF16)
    result = dot_nt(normed, weights)
    third = weights.shape[0] // 3
    scale = jnp.where(iota((1, 3 * third), 1) >= 2 * third, HEAD_DIM ** (-0.5), 1.0)
    return (result * scale).astype(BF16)


def place_heads(turn, codes_ref, gain_ref, key_ref, value_ref, query_ref, stream_ref, rows):
    weights = jnp.concatenate([key_ref[...], value_ref[...], query_ref[...]], axis=0)
    result = key_value_query(stream_ref[...], one_row(gain_ref), weights)
    spots = codes_ref[turn]
    place = one_hot(iota((rows, spots.shape[1]), 0) == spots)[:, : result.shape[0]]
    return dot(place, result)


def first_heads_kernel(
    groups,
    codes_ref,
    gain_ref,
    key_ref,
    value_ref,
    query_ref,
    stream_ref,
    ids_ref,
    *refs,
):
    out_ref, same_ref, apart_ref, back_ref, spreads_ref = refs[:5]
    refs = refs[5:]
    rows, wide = same_ref.shape
    heads = wide // SLOT
    width = heads * HEAD_DIM
    place, column = lax.axis_index("seq"), lax.axis_index("tp")
    first = place_heads(0, codes_ref, gain_ref, key_ref, value_ref, query_ref, stream_ref, rows)
    out_ref[...] = first.astype(BF16)
    for shift in range(2):
        spreads_ref[shift] = one_hot(spread_mask(2 * width, wide, shift * width))

    ids = ids_ref[pl.ds(place, 1), :].astype(jnp.int32)
    same_ref[...] = id_lanes(ids, wide, None).astype(BF16)
    apart_ref[...] = id_lanes(ids, wide, NEG).astype(BF16)
    share = back_ref.shape[1]
    for turn in range(back_ref.shape[0]):
        wanted = stored_at((column ^ turn) * share + iota((share, 1), 0), rows)
        back_ref[turn] = one_hot(wanted == iota((share, rows), 1))
    apart_refs, apart_all = refs[:-1], refs[-1]
    for ref, (level, masks) in zip(apart_refs, groups):
        count = rows >> level
        slots = iota((count, wide), 1) >> 6
        for index, mask in enumerate(masks):
            far = ids_ref[pl.ds(place ^ mask, 1), :].astype(jnp.int32)
            apart_all[...] = id_lanes(far, wide, NEG).astype(BF16)
            chosen = None
            for head in range(heads):
                part = apart_all[pl.ds(head_start(level, head, column, rows), count), :]
                chosen = part if chosen is None else jnp.where(slots >= head, part, chosen)
            ref[index * count : (index + 1) * count, :] = chosen


def more_heads_kernel(turn, codes_ref, gain_ref, key_ref, value_ref, query_ref, stream_ref, before_ref, *refs):
    given_ref, out_ref, on_ref = refs if len(refs) == 3 else (None, refs[-1], None)
    more = place_heads(turn, codes_ref, gain_ref, key_ref, value_ref, query_ref, stream_ref, out_ref.shape[0])
    out_ref[...] = (before_ref[...].astype(F32) + more).astype(BF16)
    if on_ref is not None:
        on_ref[...] = given_ref[...]


def last_heads_kernel(
    turn, levels, codes_ref, gain_ref, key_ref, value_ref, query_ref, stream_ref, before_ref, packed, *sets
):
    rows = packed.shape[0]
    width = key_ref.shape[0]
    heads = width // HEAD_DIM
    column = lax.axis_index("tp")
    more_heads_kernel(
        turn, codes_ref, gain_ref, key_ref, value_ref, query_ref, stream_ref, before_ref, packed
    )
    for ref, level in zip(sets, levels):
        count = rows >> level
        lane = iota((count, 2 * width), 1)
        lane = jnp.where(lane >= width, lane - width, lane)
        chosen = None
        for head in range(heads):
            part = packed[pl.ds(head_start(level, head, column, rows), count), : 2 * width]
            chosen = part if chosen is None else jnp.where(lane >= head * HEAD_DIM, part, chosen)
        ref[...] = chosen


def id_lanes(ids, wide, apart):
    count = ids.shape[1]
    lane = iota((IDS, wide), 1) & (SLOT - 1)
    group = iota((IDS, wide), 0)
    same = lane - HEAD_DIM == group
    if apart is None:
        table = jnp.where(same, 1.0, 0.0)
    else:
        table = jnp.where((lane >= HEAD_DIM) & ~same, apart, 0.0)
    return dot_tn(one_hot(iota((IDS, count), 0) == ids), table.astype(BF16))


def agreement(level, group, column, rows, total, count):
    q_on, k_on = [], []
    for index, (head, first) in enumerate(group):
        for size, on in ((count, q_on), (total, k_on)):
            line, at = iota((8, size), 0), iota((8, size), 1)
            for step in range(1, size // count):
                at = at - jnp.where(iota((8, size), 1) >= step * count, count, 0)
            start = jnp.zeros((8, size), jnp.int32)
            length = jnp.zeros((8, size), jnp.int32)
            for branch in range(level, BRANCHES):
                start = jnp.where(line == branch, head_start(branch, head, column, rows) - first, start)
                length = jnp.where(line == branch, rows >> branch, length)
            on.append(jnp.where((at >= start) & (at < start + length), 1.0, 0.0))
        blank = jnp.zeros((8, count), F32)
        q_on[index] = jnp.concatenate([q_on[index] if place == index else blank for place in range(len(group))], axis=1)
    return jnp.concatenate(q_on, axis=0).astype(BF16), jnp.concatenate(k_on, axis=0).astype(BF16)


def repeat(block, times):
    return jnp.concatenate([block] * times, axis=1)


def own_kernel(packed_ref, same_ref, apart_ref, spreads_ref, acc_ref, tops_ref, masked_ref, keys_ref, values_ref):
    rows, wide = masked_ref.shape
    heads = wide // SLOT
    width = heads * HEAD_DIM
    column = lax.axis_index("tp")
    pairs = packed_ref[:, : 2 * width]
    query = dot(packed_ref[:, 2 * width :], spreads_ref[0, :width])
    masked_ref[...] = (query + same_ref[...].astype(F32)).astype(BF16)
    key = dot(pairs, spreads_ref[0])
    keys_ref[...] = (key + apart_ref[...].astype(F32)).astype(BF16)
    ones = jnp.where((iota((rows, wide), 1) & (SLOT - 1)) >= HEAD_DIM, 1.0, 0.0)
    value = dot(pairs, spreads_ref[1])
    values_ref[...] = (value + ones).astype(BF16)
    half = rows // 2
    slot_of = iota((rows, wide), 1) >> 6
    query = masked_ref[...]
    acc = None
    for head in range(heads):
        one = jnp.where(slot_of == head, query, jnp.zeros((), BF16))
        scores = dot_nt(one, keys_ref[...])
        top = jnp.max(scores, axis=1, keepdims=True)
        tops_ref[head] = jnp.broadcast_to(top, (rows, LANES))
        weights = jnp.exp(scores - top)
        start = (head & 1) * half
        times = dot_tn(*agreement(0, [(head, start)], column, rows, half, half))
        scaled = weights[start : start + half, start : start + half] * times
        others = weights[start : start + half, half - start : rows - start]
        part = jnp.concatenate([others, scaled] if start else [scaled, others], axis=1)
        rest = weights[half - start : rows - start]
        weights = jnp.concatenate([rest, part] if start else [part, rest], axis=0)
        got = dot(weights.astype(BF16), values_ref[...])
        acc = got if acc is None else jnp.where(slot_of == head, got, acc)
    acc_ref[...] = acc


def weigh_inner(weights, group, column, rows):
    count = rows >> 1
    length = rows >> 2
    head = group[0][0]
    start = head_start(2, head, column, rows) - head_start(1, head, column, rows)
    low, high = start // LANES * LANES, up_to(start + length, LANES)
    q_on, k_on = agreement(1, group, column, rows, count, count)
    part = weights[start : start + length]
    part = [part[:, :low], part[:, low:high] * dot_tn(q_on[:, start : start + length], k_on[:, low:high]), part[:, high:]]
    part = jnp.concatenate([one for one in part if one.shape[1]], axis=1)
    return jnp.concatenate([part, weights[length:]] if start == 0 else [weights[:start], part], axis=0)


def merge_sets(level, masks, sets, acc_ref, tops_ref, query_ref, spreads_ref, apart_ref):
    rows, wide = query_ref.shape
    column = lax.axis_index("tp")
    count = rows >> level
    some = min(max(1, rows // count), len(masks))
    total = some * count
    slot_of = iota((count, wide), 1) >> 6
    ones = jnp.where((iota((total, wide), 1) & (SLOT - 1)) >= HEAD_DIM, 1.0, 0.0)
    chunks = []
    for begin in range(0, len(masks), some):
        pairs = jnp.concatenate([ref[...] for ref in sets[begin : begin + some]], axis=0)
        keys = dot(pairs, spreads_ref[0]) + apart_ref[begin * count : begin * count + total, :].astype(F32)
        values = dot(pairs, spreads_ref[1]) + ones
        chunks.append((keys.astype(BF16), values.astype(BF16)))
    heads = wide // SLOT
    together = heads if heads * count * total <= 2**19 else 1
    states = []
    for low in range(0, heads, together):
        group = [(head, head_start(level, head, column, rows)) for head in range(low, low + together)]
        heres = [(head, pl.ds(first, count)) for head, first in group]
        query = [jnp.where(slot_of == head, query_ref[here, :], jnp.zeros((), BF16)) for head, here in heres]
        sums = [acc_ref[here, :] for _, here in heres]
        tops = [tops_ref[head, here, :] for head, here in heres]
        states.append((group, heres) + tuple(jnp.concatenate(parts, axis=0) for parts in (query, sums, tops)))
    merged = []
    for group, heres, query, sums, tops in states:
        inner = level == 1 and total == count and together == 1
        if not inner:
            times = dot_tn(*agreement(level, group, column, rows, total, count))
        for keys, values in chunks:
            scores = dot_nt(query, keys)
            top = jnp.maximum(tops, jnp.max(scores, axis=1, keepdims=True))
            weights = jnp.exp(scores - repeat(top, total // LANES))
            weights = weigh_inner(weights, group, column, rows) if inner else weights * times
            got = dot(weights.astype(BF16), values)
            sums = sums * repeat(jnp.exp(tops - top), wide // LANES) + got
            tops = top
        for index, (head, here) in enumerate(heres):
            part = slice(index * count, (index + 1) * count)
            merged.append((head, here, sums[part], tops[part]))
    return merged


def slot_lane(values, inner):
    wide = values.shape[1]
    row, lane = iota((wide, wide), 0), iota((wide, wide), 1)
    pick = one_hot(row == (lane >> 6) * SLOT + inner)
    high = values.astype(BF16)
    low = (values - high.astype(F32)).astype(BF16)
    return dot(high, pick) + dot(low, pick)


def near_kernel(groups, acc_ref, tops_ref, query_ref, spreads_ref, *refs):
    apart_refs, refs = refs[: len(groups)], refs[len(groups) :]
    sums_ref, new_tops_ref = refs[-2:]
    wide = query_ref.shape[1]
    del acc_ref, tops_ref

    for apart_ref, (level, masks) in zip(apart_refs, groups):
        merged = merge_sets(
            level, masks, refs[: len(masks)], sums_ref, new_tops_ref, query_ref, spreads_ref, apart_ref
        )
        refs = refs[len(masks) :]
        for head, here, sums, tops in merged:
            slot_of = iota(sums.shape, 1) >> 6
            sums_ref[here, :] = jnp.where(slot_of == head, sums, sums_ref[here, :])
            new_tops_ref[head, here, :] = tops


def mid_kernel(groups, acc_ref, tops_ref, query_ref, spreads_ref, back_ref, *refs, n_sent):
    sent_refs = refs[-n_sent:]
    refs = refs[:-n_sent]
    sums_ref, _, early_ref, centre_ref = refs[-4:]
    near_kernel(groups, acc_ref, tops_ref, query_ref, spreads_ref, *refs[:-2])
    rows, wide = query_ref.shape
    heads = wide // SLOT
    every = sums_ref[...]
    inner = iota((rows, wide), 1) & (SLOT - 1)
    attn = jnp.where(inner < HEAD_DIM, every / slot_lane(every, HEAD_DIM), 0.0)
    average = jnp.full((wide, wide), 1.0, BF16)
    centre = (dot(attn.astype(BF16), average) * (1.0 / (heads * HEAD_DIM))).astype(BF16).astype(F32)
    centre_ref[...] = centre
    early = jnp.where(inner < HEAD_DIM, attn - centre, centre).astype(BF16)
    early_ref[...] = early
    for index, ref in enumerate(sent_refs):
        share = back_ref.shape[1]
        ref[:share] = dot(back_ref[back_ref.shape[0] - n_sent + index], early).astype(BF16)
        ref[share:] = jnp.zeros((ref.shape[0] - share, ref.shape[1]), BF16)


def far_kernel(n_tp, level, masks, acc_ref, tops_ref, query_ref, spreads_ref, early_ref, centre_ref, back_ref, *refs):
    apart_ref, refs = refs[0], refs[1:]
    sets, refs = refs[: len(masks)], refs[len(masks) :]
    out_refs, message = refs[:n_tp], refs[-1]
    message[...] = early_ref[...]

    merged = merge_sets(level, masks, sets, acc_ref, tops_ref, query_ref, spreads_ref, apart_ref)
    changed = None
    stacked = jnp.concatenate([sums for _, _, sums, _ in merged], axis=0)
    stacked = stacked / slot_lane(stacked, HEAD_DIM)
    for index, (head, here, sums, _) in enumerate(merged):
        lane = iota(sums.shape, 1)
        length = sums.shape[0]
        mine = (lane >= head * SLOT) & (lane < head * SLOT + HEAD_DIM)
        new = (stacked[index * length : (index + 1) * length] - centre_ref[here, :]).astype(BF16)
        message[here, :] = jnp.where(mine, new, message[here, :])
        changed = new if changed is None else jnp.where(lane >= head * SLOT, new, changed)
    final = message[...]
    rows = message.shape[0]
    count = rows >> level
    late = [turn for turn in range(n_tp) if out_refs[turn].shape[0] != back_ref.shape[1]]
    each = rows // CLASSES
    classes = count // each
    picks = []
    for turn in late:
        line = iota((out_refs[turn].shape[0], count), 0)
        spot = (lax.axis_index("tp") ^ turn) * (each // n_tp) + line // classes
        wanted = (line % classes) * each + spot
        picks.append((iota(line.shape, 1) == wanted) & (line < count // n_tp))
    picked = dot(jnp.concatenate([one_hot(pick) for pick in picks], axis=0), changed).astype(BF16)
    for index, turn in enumerate(late):
        length = out_refs[turn].shape[0]
        out_refs[turn][...] = picked[index * length : (index + 1) * length]
    for turn in range(n_tp):
        if turn not in late:
            out_refs[turn][...] = dot(back_ref[turn], final).astype(BF16)


def base_kernel(n_tp, codes_ref, *refs):
    shards, part_refs = refs[:n_tp], refs[n_tp : 2 * n_tp]
    base_ref, weights_ref = refs[-2:]
    share = base_ref.shape[0]
    wanted = stored_at(lax.axis_index("tp") * share + iota((share, 1), 0), share * n_tp)
    base = None
    for turn in range(n_tp):
        spots = codes_ref[turn]
        moved = dot(one_hot(wanted == spots)[:, : shards[turn].shape[0]], shards[turn][...])
        base = moved if base is None else base + moved
    base_ref[...] = base.astype(BF16)
    heads = weights_ref.shape[1] // SLOT
    gap = jnp.zeros((SLOT - HEAD_DIM, weights_ref.shape[2]), BF16)
    for turn, ref in enumerate(part_refs):
        for head in range(heads):
            at, to = head * HEAD_DIM, head * SLOT
            weights_ref[turn, to : to + HEAD_DIM, :] = ref[at : at + HEAD_DIM, :]
            weights_ref[turn, to + HEAD_DIM : to + SLOT, :] = gap


def mix_kernel(n_tp, level, base_ref, weights_ref, *refs):
    message_refs, change_refs, out_ref = refs[:n_tp], refs[n_tp:-1], refs[-1]
    share, wide = base_ref.shape[0], weights_ref.shape[1]
    features = n_tp * (wide // SLOT) * HEAD_DIM
    lane = iota((share, wide), 1)
    inside = (lane & (SLOT - 1)) < HEAD_DIM
    parts, centres = [], []
    for turn, ref in enumerate(message_refs):
        message = ref[:share].astype(F32)
        centres.append(message[:, HEAD_DIM : HEAD_DIM + 1])
        if turn >= n_tp - len(change_refs):
            change = change_refs[turn - n_tp + len(change_refs)][...]
            count = change.shape[0]
            moved = dot(one_hot(iota((share, count), 1) == iota((share, count), 0) >> level), change)
            head = (lax.axis_index("tp") ^ turn) * (wide // SLOT) + (lane >> 6)
            late = ((iota((share, wide), 0) ^ head) & (2**level - 1)) == 0
            message = jnp.where(late, moved, message)
        parts.append(jnp.where(inside, message, 0.0))
    each = features // n_tp
    mean = (jnp.sum(sum(parts), axis=1, keepdims=True) + sum(centres) * each) * (1.0 / features)
    parts = [jnp.where(inside, part + (centre - mean), 0.0) for part, centre in zip(parts, centres)]
    spread = jnp.sum(sum(part * part for part in parts), axis=1, keepdims=True) * (1.0 / features)
    factor = lax.rsqrt(spread + EPS)
    total = base_ref[...].astype(F32)
    for turn, part in enumerate(parts):
        total = total + dot((part * factor).astype(BF16), weights_ref[turn])
    out_ref[...] = total.astype(BF16)


def swap(block, axis, mask):
    count = lax.axis_size(axis)
    return lax.ppermute(block, axis, [(index, index ^ mask) for index in range(count)])


def gather_tp(block):
    across = swap(block, "tp", 2)
    return [block, swap(block, "tp", 1), across, swap(across, "tp", 1)]


def body(
    tiles,
    tile_target,
    slide_id,
    proj_weight,
    norm_gain,
    query_weight,
    key_weight,
    value_weight,
    sub_gain,
    out_weight,
):
    n_seq = lax.axis_size("seq")
    n_tp = lax.axis_size("tp")
    rows, tile_width = tiles.shape
    features = proj_weight.shape[1]
    width = query_weight.shape[1]
    heads = width // HEAD_DIM
    wide = heads * SLOT
    share = rows // n_tp
    peer = rows // n_seq
    sub_pad = up_to(peer // n_tp, 8)
    arriving = n_seq * sub_pad
    chunks = tile_width // LANES
    block_rows = up_to(chunks * sub_pad + 8, 16)

    first_group = max(1, n_seq // 16)
    sizes = [min(first_group * 2**branch, n_seq) for branch in range(BRANCHES)]
    groups = []
    for level in range(BRANCHES):
        masks = tuple(range(1 if level == 0 else sizes[level - 1], sizes[level]))
        if masks:
            groups.append((level, masks))

    vmem_bytes = VMEM_BYTES if n_seq <= 8 else LARGE_VMEM_BYTES
    (blocks,) = call(
        functools.partial(route_kernel, n_seq, n_tp, peer),
        "route",
        [((n_seq * n_tp, block_rows, LANES), BF16)],
        [tile_target.reshape(-1, LANES), slide_id.reshape(-1, LANES), tiles],
        scratch=[
            pltpu.VMEM((rows // LANES, LANES), jnp.int32),
            pltpu.VMEM((rows // LANES, LANES), jnp.int32),
            pltpu.VMEM(tiles.shape, BF16),
            pltpu.VMEM((n_seq * n_tp, block_rows, LANES), BF16),
            pltpu.SemaphoreType.DMA((3,)),
            pltpu.SemaphoreType.DMA((n_seq,)),
        ],
        cost=3,
        vmem_bytes=ALL_VMEM_BYTES,
        apart=(0, 1, 2),
        out_apart=(0,),
    )
    received = lax.all_to_all(blocks, ("seq", "tp"), split_axis=0, concat_axis=0, tiled=True)
    proj_parts = gather_tp(proj_weight)
    (early,) = call(hint_kernel, "hint", [((16, LANES), BF16)], [proj_parts[-1]], cost=HINT_COST)
    (scaled,) = call(
        scale_kernel,
        "scale",
        [((width, features), BF16)],
        [sub_gain.reshape(1, width), out_weight],
        scratch=[pltpu.VMEM((width, features), BF16), pltpu.SemaphoreType.DMA],
        cost=1,
        out_apart=(0,),
    )

    beside = swap(scaled, "tp", 1)
    stream, codes, ids = call(
        functools.partial(project_kernel, n_seq, n_tp, peer),
        "project",
        [((arriving, features), BF16)]
        + [((n_tp, 1, up_to(arriving, LANES)), jnp.int32), ((n_seq, rows), F32)],
        [received, early, beside] + proj_parts,
        cost=0.5,
        scratch=[
            pltpu.VMEM(received.shape, BF16),
            pltpu.SemaphoreType.DMA((n_seq,)),
        ],
        vmem_bytes=vmem_bytes,
        apart=(0,),
    )
    shards = gather_tp(stream)

    gain = norm_gain.reshape(-1, LANES)
    weights = [gain, key_weight.T, value_weight.T, query_weight.T]
    partial, same, apart, back, spreads, *far_apart = call(
        functools.partial(first_heads_kernel, groups),
        "heads_1",
        [
            ((rows, 3 * width), BF16),
            ((rows, wide), BF16),
            ((rows, wide), BF16),
            ((n_tp, share, rows), BF16),
            ((2, 2 * width, wide), BF16),
        ]
        + [(((rows >> level) * len(masks), wide), BF16) for level, masks in groups],
        [codes] + weights + [shards[0], ids],
        scratch=[pltpu.VMEM((rows, wide), BF16)],
        vmem_bytes=vmem_bytes,
    )
    across = swap(scaled, "tp", 2)
    out_parts = [scaled, beside]
    for turn in range(1, n_tp - 1):
        given = [across] if turn == 1 else out_parts[3:]
        partial, *on = call(
            functools.partial(more_heads_kernel, turn),
            "heads_2",
            [((rows, 3 * width), BF16)] + [((width, features), BF16)] * (turn == 1),
            [codes] + weights + [shards[turn], partial] + given,
            cost=10 if turn == n_tp - 2 else 1,
            vmem_bytes=vmem_bytes,
        )
        if on:
            out_parts += on + [swap(on[0], "tp", 1)]
    packed, *sets = call(
        functools.partial(last_heads_kernel, n_tp - 1, [level for level, _ in groups]),
        "heads_3",
        [((rows, 3 * width), BF16)] + [((rows >> level, 2 * width), BF16) for level, _ in groups],
        [codes] + weights + [shards[n_tp - 1], partial],
        vmem_bytes=vmem_bytes,
    )
    sent = [[swap(one, "seq", mask) for mask in masks] for one, (_, masks) in zip(sets[:-1], groups)]
    direct = {mask: swap(sets[-1], "seq", mask) for mask in groups[-1][1] if mask % 2 == 0}
    sent.append([swap(direct[mask - 1], "seq", 1) if mask % 2 else direct[mask] for mask in groups[-1][1]])

    acc, tops, masked = call(
        own_kernel,
        "own",
        [((rows, wide), F32), ((heads, rows, LANES), F32), ((rows, wide), BF16)],
        [packed, same, apart, spreads],
        scratch=[pltpu.VMEM((rows, wide), BF16)] * 2,
        cost=0.1,
        vmem_bytes=vmem_bytes,
    )
    n_sent = n_tp // 2
    for index in range(len(groups) - 1):
        kernel, outs, given = near_kernel, [], []
        if index == len(groups) - 2:
            kernel, given = functools.partial(mid_kernel, n_sent=n_sent), [back]
            outs = [((rows, wide), BF16), ((rows, wide), F32)] + [((share + 16, wide), BF16)] * n_sent
        acc, tops, *more = call(
            functools.partial(kernel, [groups[index]]),
            "mid" if outs else "near",
            [((rows, wide), F32), ((heads, rows, LANES), F32)] + outs,
            [acc, tops, masked, spreads] + given + [far_apart[index]] + sent[index],
            aliases={0: 0, 1: 1},
            cost=6,
            vmem_bytes=vmem_bytes,
        )
    early, centre, *ahead = more
    messages = call(
        functools.partial(far_kernel, n_tp, *groups[-1]),
        "far",
        [((share, wide), BF16)] * (n_tp - n_sent)
        + [((up_to((rows >> groups[-1][0]) // n_tp, 16), wide), BF16)] * n_sent,
        [acc, tops, masked, spreads, early, centre, back, far_apart[-1]] + sent[-1],
        scratch=[pltpu.VMEM((rows, wide), BF16)],
        vmem_bytes=vmem_bytes,
    )
    ahead = [swap(one, "tp", n_tp - n_sent + index) for index, one in enumerate(ahead)]
    arrived = [messages[0]] + [swap(messages[turn], "tp", turn) for turn in range(1, n_tp)]
    arrived = arrived[: n_tp - n_sent] + ahead + arrived[n_tp - n_sent :]
    base, padded = call(
        functools.partial(base_kernel, n_tp),
        "base",
        [((share, features), BF16), ((n_tp, wide, features), BF16)],
        [codes] + shards + out_parts,
        cost=0.3,
        vmem_bytes=vmem_bytes,
    )
    (result,) = call(
        functools.partial(mix_kernel, n_tp, groups[-1][0]),
        "mix",
        [((share, features), BF16)],
        [base, padded] + arrived,
    )
    return result


def solution(mesh):
    return jax.shard_map(
        body,
        mesh=mesh,
        in_specs=(
            P("seq", "tp"),
            P("seq"),
            P("seq"),
            P("tp", None),
            P(),
            P(None, "tp"),
            P(None, "tp"),
            P(None, "tp"),
            P("tp"),
            P("tp", None),
        ),
        out_specs=P(("seq", "tp"), None),
        check_vma=False,
    )
```
